32 devices in a mesh: dp: 16 (over z, y, x), mp: 2 (over core).
Axes of the slice: x: 2, y: 2, z: 4, core: 2. Of those that a mesh axis runs over, the one named last changes fastest.
Arguments:
- tokens: bfloat16 [16384, 768], P(('dp', 'mp')), may hold values from -6 to 6
- cotangent: bfloat16 [16384, 768], P(('dp', 'mp')), may hold values from -6 to 6
- gain_attn: float32 [768], replicated, may hold values from 0.1 to 1.9
- w_query: bfloat16 [768, 768], P('dp', 'mp'), may hold values from -0.0546875 to 0.0546875
- w_key: bfloat16 [768, 768], P('dp', 'mp'), may hold values from -0.21875 to 0.21875
- w_value: bfloat16 [768, 768], P('dp', 'mp'), may hold values from -0.21875 to 0.21875
- w_out: bfloat16 [768, 768], P('mp', 'dp'), may hold values from -1.75 to 1.75
- rel_table: float32 [32, 12], replicated, may hold values from -5 to 5
- buckets: int32 [2047], replicated, may hold values from 0 to 31
- gain_ffn: float32 [768], replicated, may hold values from 0.1 to 1.9
- w_gate: bfloat16 [768, 2048], P('dp', 'mp'), may hold values from -0.21875 to 0.21875
- w_up: bfloat16 [768, 2048], P('dp', 'mp'), may hold values from -0.21875 to 0.21875
- w_down: bfloat16 [2048, 768], P('mp', 'dp'), may hold values from -0.125 to 0.125
Outputs:
- output: bfloat16 [16384, 768], P(('dp', 'mp'))
- d_tokens: bfloat16 [16384, 768], P(('dp', 'mp'))
- d_gain_attn: float32 [768], replicated
- d_w_query: float32 [768, 768], P('dp', 'mp')
- d_w_key: float32 [768, 768], P('dp', 'mp')
- d_w_value: float32 [768, 768], P('dp', 'mp')
- d_w_out: float32 [768, 768], P('mp', 'dp')
- d_rel_table: float32 [32, 12], replicated
- d_gain_ffn: float32 [768], replicated
- d_w_gate: float32 [768, 2048], P('dp', 'mp')
- d_w_up: float32 [768, 2048], P('dp', 'mp')
- d_w_down: float32 [2048, 768], P('mp', 'dp')
The draws below stay inside these ranges and needn't reach their ends.
Inputs may be any that keep to these rules, and one draw needn't show every extreme that they name: `buckets`: entry o is the bucket of the offset key position minus query position = o - 1023.
All inputs are finite; a program needn't handle non-finite values.
Results may differ from the reference program's by a relative error of at most 0.02.
Values may be sent and summed in bfloat16 or wider, within the bound.
No kernel may reach another device: no remote copies, remote signals or barrier semaphores. Data moves between devices by JAX's collectives and lax.ppermute only.
A program may use at most 256 MiB of HBM per device.

```python
import jax
import jax.numpy as jnp
from jax import lax

D = 768
HEADS = 12
HEAD_DIM = 64
FF = 2048
BUCKETS = 32
SEQ = 1024
TOKENS = 16384
N_DP = 16


def plant(values, stream_key, smallest, largest):
    dims = values.shape
    spot = [jax.random.randint(jax.random.fold_in(stream_key, axis), (), 0, dims[axis]) for axis in range(len(dims))]
    values = values.at[tuple(spot)].set(smallest)
    longest = dims.index(max(dims))
    spot[longest] = (spot[longest] + 1) % dims[longest]
    return values.at[tuple(spot)].set(largest)


def block_scale(own_key, extent, cuts, smallest, largest):
    def one(dim, blocks):
        heights = jax.random.uniform(jax.random.fold_in(jax.random.fold_in(own_key, 6), dim), (blocks,), jnp.float32, smallest / len(cuts), largest / len(cuts))
        return jnp.repeat(jnp.exp(heights), extent[dim] // blocks).reshape((-1,) + (1,) * (len(extent) - dim - 1))

    loudness = one(*cuts[0])
    for cut in cuts[1:]:
        loudness = loudness * one(*cut)
    return loudness


def gaussian(rng, shape, spread, most, cuts=(), held_as=jnp.bfloat16):
    loudness = block_scale(rng, shape, cuts, -0.22, 0.18) if cuts else 1.0
    array = jax.random.normal(rng, shape, jnp.float32) * spread * loudness
    return jnp.minimum(jnp.maximum(array, -most), most).astype(held_as)


def setup_inputs(seed: int = 0) -> dict:
    key_list = jax.random.split(jax.random.key(seed), 14)
    tokens = gaussian(key_list[0], (TOKENS, D), 1.0, 6.0, ((0, 32),))
    cotangent = gaussian(key_list[1], (TOKENS, D), 1.0, 6.0, ((0, 32),))
    gain_attn = jnp.clip(1.0 + 0.18 * jax.random.normal(key_list[2], (D,), jnp.float32), 0.1, 1.9)
    w_query = gaussian(key_list[3], (D, D), (16 * D) ** -0.5, 0.0546875, ((0, 16), (1, 2)))
    w_key = gaussian(key_list[4], (D, D), D ** -0.5, 0.21875, ((0, 16), (1, 2)))
    w_value = gaussian(key_list[5], (D, D), D ** -0.5, 0.21875, ((0, 16), (1, 2)))
    w_out = gaussian(key_list[6], (D, D), (D // 64) ** -0.5, 1.75, ((0, 2), (1, 16)))
    rel_table = gaussian(key_list[7], (BUCKETS, HEADS), 1.0, 5.0, (), jnp.float32)
    buckets = plant(jax.random.randint(key_list[8], (2 * SEQ - 1,), 0, BUCKETS), jax.random.fold_in(key_list[8], 1), 0, BUCKETS - 1).astype(jnp.int32)
    gain_ffn = jnp.clip(1.0 + 0.18 * jax.random.normal(key_list[9], (D,), jnp.float32), 0.1, 1.9)
    w_gate = gaussian(key_list[10], (D, FF), D ** -0.5, 0.21875, ((0, 16), (1, 2)))
    w_up = gaussian(key_list[11], (D, FF), D ** -0.5, 0.21875, ((0, 16), (1, 2)))
    w_down = gaussian(key_list[12], (FF, D), FF ** -0.5, 0.125, ((0, 2), (1, 16)))
    return dict(tokens=tokens, cotangent=cotangent, gain_attn=gain_attn, w_query=w_query, w_key=w_key, w_value=w_value, w_out=w_out, rel_table=rel_table, buckets=buckets, gain_ffn=gain_ffn, w_gate=w_gate, w_up=w_up, w_down=w_down)


@jax.custom_vjp
def low(v):
    return lax.optimization_barrier(v.astype(jnp.bfloat16)).astype(jnp.float32)

@jax.custom_vjp
def low_back(v):
    return v

def low_keep(v):
    return (low(v), None)

def low_pass(kept, grad):
    return (grad,)

def back_keep(v):
    return (v, None)

def back_low(kept, grad):
    return (low(grad),)
low.defvjp(low_keep, low_pass)
low_back.defvjp(back_keep, back_low)
precise = lax.Precision.HIGHEST
epsilon = 1e-06
block_limit = 512

def matmul_hi(left, right):
    return jnp.dot(left, right, precision=precise)

def rms_scale(inputs, gain):
    return inputs * lax.rsqrt(lax.optimization_barrier(jnp.mean(inputs * inputs, axis=-1, keepdims=True)) + epsilon) * gain

def attention(queries, keys_all, values, offset_bias):
    block_rows = min(block_limit, SEQ)
    blocks = SEQ // block_rows
    heads_q = queries.reshape(blocks, block_rows, HEADS, HEAD_DIM)
    heads_k = keys_all.reshape(SEQ, HEADS, HEAD_DIM)
    heads_v = values.reshape(SEQ, HEADS, HEAD_DIM)
    starts = jnp.arange(blocks, dtype=jnp.int32) * block_rows
    positions = jnp.arange(SEQ, dtype=jnp.int32)
    local_rows = jnp.arange(block_rows, dtype=jnp.int32)

    def one_block(pieces):
        block_q, first_row = pieces
        offsets = positions[None, :] - (first_row + local_rows)[:, None] + (SEQ - 1)
        bias_block = jnp.transpose(offset_bias[offsets], (2, 0, 1))
        scores = jnp.einsum('qhd,khd->hqk', block_q, heads_k, precision=precise) + bias_block
        scores = low_back(scores)
        probs_low = low(jax.nn.softmax(scores, axis=-1))
        return jnp.einsum('hqk,khd->qhd', probs_low, heads_v, precision=precise)
    mixed = lax.map(jax.checkpoint(one_block), (heads_q, starts))
    return mixed.reshape(SEQ, D)

def layer(inputs, gain_attn, w_query, w_key, w_value, w_out, rel_table, gain_ffn, w_gate, w_up, w_down, buckets):
    normed_a = low(rms_scale(inputs, gain_attn))
    queries = low(low_back(matmul_hi(normed_a, w_query)))
    keys_all = low(low_back(matmul_hi(normed_a, w_key)))
    values = low(low_back(matmul_hi(normed_a, w_value)))
    offset_bias = jnp.take(rel_table, buckets, axis=0)
    mixed_out = low(low_back(attention(queries, keys_all, values, offset_bias)))
    attended = inputs + low_back(matmul_hi(mixed_out, w_out))
    normed_f = low(rms_scale(attended, gain_ffn))
    gate_pre = low_back(matmul_hi(normed_f, w_gate))
    up_pre = low_back(matmul_hi(normed_f, w_up))
    hidden = low(jax.nn.gelu(gate_pre, approximate=True) * up_pre)
    return attended + matmul_hi(hidden, w_down)

def reference(tokens, cotangent, gain_attn, w_query, w_key, w_value, w_out, rel_table, buckets, gain_ffn, w_gate, w_up, w_down):
    params = (gain_attn.astype(jnp.float32), w_query.astype(jnp.float32), w_key.astype(jnp.float32), w_value.astype(jnp.float32), w_out.astype(jnp.float32), rel_table.astype(jnp.float32), gain_ffn.astype(jnp.float32), w_gate.astype(jnp.float32), w_up.astype(jnp.float32), w_down.astype(jnp.float32))
    sequences = tokens.astype(jnp.float32).reshape(N_DP, SEQ, D)
    grad_seqs = cotangent.astype(jnp.float32).reshape(N_DP, SEQ, D)

    def forward(inputs, *weights):
        return layer(inputs, *weights, buckets)

    def one_sequence(totals, pieces):
        inputs, grad_out = pieces
        result, pullback = jax.vjp(forward, inputs, *params)
        grads = pullback(grad_out)
        totals = tuple((total + grad for total, grad in zip(totals, grads[1:])))
        return (totals, (result.astype(jnp.bfloat16), grads[0].astype(jnp.bfloat16)))
    zeros = tuple((jnp.zeros(param.shape, jnp.float32) for param in params))
    totals, (outputs, d_inputs) = lax.scan(one_sequence, zeros, (sequences, grad_seqs))
    return (outputs.reshape(TOKENS, D), d_inputs.reshape(TOKENS, D), totals[0], totals[1], totals[2], totals[3], totals[4], totals[5], totals[6], totals[7], totals[8], totals[9])
```

```python
import jax
import jax.numpy as jnp
from jax import lax
from jax.experimental import pallas as pl
from jax.experimental.pallas import tpu as pltpu
from jax.sharding import PartitionSpec as P

epsilon = 1e-06
block_limit = 512
precise = lax.Precision.HIGHEST


def as_sent(array):

    def short(part):
        return part.astype(jnp.bfloat16) if part.dtype == jnp.float32 else part

    return jax.tree.map(short, array)


def matmul_nn(left, right):
    return jnp.dot(left, right, preferred_element_type=jnp.float32)


def matmul_nt(left, right):
    return lax.dot_general(
        left, right, (((1,), (1,)), ((), ())), preferred_element_type=jnp.float32
    )


def matmul_tn(left, right):
    return lax.dot_general(
        left, right, (((0,), (0,)), ((), ())), preferred_element_type=jnp.float32
    )


def rms_parts(inputs):
    scale = lax.rsqrt(jnp.mean(inputs * inputs, axis=-1, keepdims=True) + epsilon)
    return (inputs * scale, scale)


def rms_back(d_normed, unit, scale, gain):
    d_unit = d_normed * gain
    return scale * (d_unit - unit * jnp.mean(d_unit * unit, axis=-1, keepdims=True))


def gated(gate_pre, up_pre):
    return jax.nn.gelu(gate_pre, approximate=True) * up_pre


def window_base(first_query, first_key, row_count, seq_len):
    return first_key - first_query - row_count + seq_len


def make_bias(bias_full, base, row_count, width):
    span = width + row_count - 1
    head_count = bias_full.shape[0]
    strip = lax.dynamic_slice_in_dim(bias_full, base, span, 1)
    tiled = jnp.tile(strip, (1, row_count + 1))
    window = tiled[:, row_count - 1 : row_count - 1 + row_count * (span - 1)]
    return window.reshape(head_count, row_count, span - 1)[:, :, :width]


def skew_sum(d_block, row_count, width):
    head_count = d_block.shape[0]
    span = width + row_count - 1
    padded = jnp.pad(d_block, ((0, 0), (0, 0), (row_count - 1, 0)))
    flat = padded.reshape(head_count, row_count * span)
    flat = jnp.pad(flat, ((0, 0), (0, row_count)))
    skewed = flat.reshape(head_count, row_count, span + 1)[:, :, :span]
    return jnp.sum(skewed, axis=1)


def add_window(d_bias, piece, base):
    current = lax.dynamic_slice_in_dim(d_bias, base, piece.shape[1], 1)
    return lax.dynamic_update_slice_in_dim(d_bias, current + piece, base, 1)


def sum_rows(partial_value):
    return lax.psum_scatter(
        partial_value.astype(jnp.bfloat16), "mp", scatter_dimension=0, tiled=True
    ).astype(jnp.float32)


def split_heads(queries, keys_all, values, head_count):
    row_count = queries.shape[0]
    seq_len = keys_all.shape[0]
    head_dim = queries.shape[1] // head_count
    width = min(block_limit, seq_len)
    blocks = seq_len // width
    heads_q = queries.reshape(row_count, head_count, head_dim)
    heads_k = keys_all.reshape(blocks, width, head_count, head_dim)
    heads_v = values.reshape(blocks, width, head_count, head_dim)
    starts = jnp.arange(blocks, dtype=jnp.int32) * width
    return (heads_q, heads_k, heads_v, starts, width)


def attend_forward(queries, keys_all, values, bias_full, head_count, first_row):
    row_count = queries.shape[0]
    seq_len = keys_all.shape[0]
    heads_q, heads_k, heads_v, starts, width = split_heads(queries, keys_all, values, head_count)

    def block_scores(key_block, first_key):
        raw_scores = jnp.einsum(
            "qhd,khd->hqk", heads_q, key_block, preferred_element_type=jnp.float32
        )
        base = window_base(first_row, first_key, row_count, seq_len)
        return raw_scores + make_bias(bias_full, base, row_count, width)

    def stats_step(running, pieces):
        top_now, total = running
        scores = block_scores(pieces[0], pieces[1])
        top_new = jnp.maximum(top_now, jnp.max(scores, axis=-1))
        total = total * jnp.exp(top_now - top_new) + jnp.sum(
            jnp.exp(scores - top_new[..., None]), axis=-1
        )
        return ((top_new, total), None)

    start_top = jnp.full((head_count, row_count), -jnp.inf, jnp.float32)
    start_total = jnp.zeros((head_count, row_count), jnp.float32)
    (top_all, total), _ = lax.scan(stats_step, (start_top, start_total), (heads_k, starts))
    log_total = top_all + jnp.log(total)

    def mix_step(running, pieces):
        scores = block_scores(pieces[0], pieces[2])
        probs_low = jnp.exp(scores - log_total[..., None]).astype(jnp.bfloat16)
        update = jnp.einsum(
            "hqk,khd->qhd", probs_low, pieces[1], preferred_element_type=jnp.float32
        )
        return (running + update, None)

    start_mix = jnp.zeros(heads_q.shape, jnp.float32)
    mixed_f, _ = lax.scan(mix_step, start_mix, (heads_k, heads_v, starts))
    return (mixed_f.reshape(row_count, queries.shape[1]), log_total)


def attend_backward(
    queries, keys_all, values, bias_full, head_count, first_row, log_total, deltas, d_mixed
):
    row_count = queries.shape[0]
    seq_len = keys_all.shape[0]
    heads_q, heads_k, heads_v, starts, width = split_heads(queries, keys_all, values, head_count)
    heads_d = d_mixed.reshape(heads_q.shape)

    def back_step(running, pieces):
        d_query, d_bias = running
        key_block, value_block, first_key = pieces
        base = window_base(first_row, first_key, row_count, seq_len)
        scores = jnp.einsum("qhd,khd->hqk", heads_q, key_block, preferred_element_type=jnp.float32)
        scores = scores + make_bias(bias_full, base, row_count, width)
        probs = jnp.exp(scores - log_total[..., None])
        d_probs = jnp.einsum(
            "qhd,khd->hqk", heads_d, value_block, preferred_element_type=jnp.float32
        )
        d_scores = (probs * (d_probs - deltas[..., None])).astype(jnp.bfloat16)
        d_query = d_query + jnp.einsum(
            "hqk,khd->qhd", d_scores, key_block, preferred_element_type=jnp.float32
        )
        d_bias = add_window(d_bias, skew_sum(d_scores.astype(jnp.float32), row_count, width), base)
        probs_low = probs.astype(jnp.bfloat16)
        d_value = jnp.einsum("hqk,qhd->khd", probs_low, heads_d, preferred_element_type=jnp.float32)
        d_key = jnp.einsum("hqk,qhd->khd", d_scores, heads_q, preferred_element_type=jnp.float32)
        return ((d_query, d_bias), (d_key, d_value))

    start_query = jnp.zeros(heads_q.shape, jnp.float32)
    (d_query, d_bias), kv_parts = lax.scan(
        back_step, (start_query, jnp.zeros_like(bias_full)), (heads_k, heads_v, starts)
    )
    feature_count = queries.shape[1]
    d_query = d_query.reshape(row_count, feature_count)
    return (
        d_query,
        d_bias,
        kv_parts[0].reshape(seq_len, feature_count),
        kv_parts[1].reshape(seq_len, feature_count),
    )


def on_device(
    tokens,
    cotangent,
    gain_attn,
    w_query,
    w_key,
    w_value,
    w_out,
    rel_table,
    buckets,
    gain_ffn,
    w_gate,
    w_up,
    w_down,
):
    head_count = rel_table.shape[1]
    bucket_count = rel_table.shape[0]
    inputs = tokens.astype(jnp.float32)
    row_count = inputs.shape[0]
    feature_count = inputs.shape[1]
    first_row = lax.axis_index("mp") * row_count
    attn_parts = (w_query, w_key, w_value, w_out.T)
    ffn_parts = (w_gate, w_up, w_down.T)
    ffn_cols = ()
    col_parts = lax.all_gather(as_sent(attn_parts + ffn_cols), "mp", axis=1, tiled=True)
    full_parts = lax.all_gather(as_sent(tuple(col_parts) + ffn_parts), "dp", axis=0, tiled=True)
    query_full, key_full, value_full, out_full, gate_full, up_full, down_full = full_parts
    unit_a, scale_a = rms_parts(inputs)
    normed_a = (unit_a * gain_attn).astype(jnp.bfloat16)
    queries = matmul_nn(normed_a, query_full).astype(jnp.bfloat16)
    own_keys = matmul_nn(normed_a, key_full).astype(jnp.bfloat16)
    own_values = matmul_nn(normed_a, value_full).astype(jnp.bfloat16)
    keys_all, values = (
        lax.all_gather(own_keys, "mp", axis=0, tiled=True),
        lax.all_gather(own_values, "mp", axis=0, tiled=True),
    )
    one_hot = (buckets[:, None] == jnp.arange(bucket_count, dtype=jnp.int32)[None, :]).astype(
        jnp.float32
    )
    bias_full = jnp.dot(one_hot, rel_table, precision=precise).T
    mixed_f, log_total = attend_forward(queries, keys_all, values, bias_full, head_count, first_row)
    mixed_out = mixed_f.astype(jnp.bfloat16)
    attended = inputs + matmul_nt(mixed_out, out_full)
    unit_f, scale_f = rms_parts(attended)
    normed_f = (unit_f * gain_ffn).astype(jnp.bfloat16)
    normed_seq, cot_seq = (
        lax.all_gather(normed_f, "mp", axis=0, tiled=True),
        lax.all_gather(cotangent, "mp", axis=0, tiled=True),
    )
    gate_pre = matmul_nn(normed_seq, gate_full)
    up_pre = matmul_nn(normed_seq, up_full)
    hidden = gated(gate_pre, up_pre).astype(jnp.bfloat16)
    output = attended + sum_rows(matmul_nt(hidden, down_full))
    d_hidden = matmul_nn(cot_seq, down_full)
    d_down = matmul_tn(cot_seq, hidden)
    _, pull_gate = jax.vjp(gated, gate_pre, up_pre)
    d_gate, d_up = pull_gate(d_hidden)
    d_gate = d_gate.astype(jnp.bfloat16)
    d_up = d_up.astype(jnp.bfloat16)
    d_normed_f = sum_rows(matmul_nt(d_gate, gate_full) + matmul_nt(d_up, up_full))
    d_gate_w = matmul_tn(normed_seq, d_gate)
    d_up_w = matmul_tn(normed_seq, d_up)
    d_gain_f = jnp.sum(d_normed_f * unit_f, axis=0)
    d_attended = cotangent.astype(jnp.float32) + rms_back(d_normed_f, unit_f, scale_f, gain_ffn)
    d_att_low = d_attended.astype(jnp.bfloat16)
    d_out_w = matmul_tn(d_att_low, mixed_out)
    d_mixed = matmul_nn(d_att_low, out_full).astype(jnp.bfloat16)
    head_dim = feature_count // head_count
    deltas = jnp.sum(
        (d_mixed.astype(jnp.float32) * mixed_f).reshape(row_count, head_count, head_dim), axis=-1
    ).T
    d_query, d_bias, d_keys_part, d_values_part = attend_backward(
        queries, keys_all, values, bias_full, head_count, first_row, log_total, deltas, d_mixed
    )
    d_keys_own, d_values_own = (
        lax.psum_scatter(
            d_keys_part.astype(jnp.bfloat16), "mp", scatter_dimension=0, tiled=True
        ).astype(jnp.float32),
        lax.psum_scatter(
            d_values_part.astype(jnp.bfloat16), "mp", scatter_dimension=0, tiled=True
        ).astype(jnp.float32),
    )
    d_keys_own = d_keys_own.astype(jnp.bfloat16)
    d_values_own = d_values_own.astype(jnp.bfloat16)
    d_query = d_query.astype(jnp.bfloat16)
    d_normed_a = (
        matmul_nt(d_query, query_full)
        + matmul_nt(d_keys_own, key_full)
        + matmul_nt(d_values_own, value_full)
    )
    d_query_w = matmul_tn(normed_a, d_query)
    d_key_w = matmul_tn(normed_a, d_keys_own)
    d_value_w = matmul_tn(normed_a, d_values_own)
    d_gain_a = jnp.sum(d_normed_a * unit_a, axis=0)
    d_tokens = (d_attended + rms_back(d_normed_a, unit_a, scale_a, gain_attn)).astype(jnp.bfloat16)
    d_table = jnp.dot(d_bias, one_hot, precision=precise).T
    row_grads = (
        lax.psum_scatter(
            d_query_w.astype(jnp.bfloat16), "dp", scatter_dimension=0, tiled=True
        ).astype(jnp.float32),
        lax.psum_scatter(
            d_key_w.astype(jnp.bfloat16), "dp", scatter_dimension=0, tiled=True
        ).astype(jnp.float32),
        lax.psum_scatter(
            d_value_w.astype(jnp.bfloat16), "dp", scatter_dimension=0, tiled=True
        ).astype(jnp.float32),
        lax.psum_scatter(
            d_out_w.astype(jnp.bfloat16), "dp", scatter_dimension=0, tiled=True
        ).astype(jnp.float32),
        lax.psum_scatter(
            d_gate_w.astype(jnp.bfloat16), "dp", scatter_dimension=0, tiled=True
        ).astype(jnp.float32),
        lax.psum_scatter(d_up_w.astype(jnp.bfloat16), "dp", scatter_dimension=0, tiled=True).astype(
            jnp.float32
        ),
        lax.psum_scatter(d_down.astype(jnp.bfloat16), "dp", scatter_dimension=0, tiled=True).astype(
            jnp.float32
        ),
    )
    row_grads = tuple(row_grads)
    ffn_late = ()
    col_grads = tuple(
        jax.tree.map(
            lambda part: part.astype(jnp.float32),
            lax.psum_scatter(
                as_sent(row_grads[:4] + ffn_late), "mp", scatter_dimension=1, tiled=True
            ),
        )
    )
    ffn_done = row_grads[4:]
    small_sums = lax.psum((d_gain_a, d_gain_f, d_table), ("dp", "mp"))
    return (
        output.astype(jnp.bfloat16),
        d_tokens,
        small_sums[0],
        col_grads[0],
        col_grads[1],
        col_grads[2],
        col_grads[3].T,
        small_sums[2],
        small_sums[1],
        ffn_done[0],
        ffn_done[1],
        ffn_done[2].T,
    )


MXU_ROWS = 256
LANES = 128
VMEM_LIMIT = 56 * 2**20


def call(body, grid, in_specs, out_specs, out_shape, scratch=(), prefetch=0, flops=0, moved=0):
    return pl.pallas_call(
        body,
        grid_spec=pltpu.PrefetchScalarGridSpec(
            num_scalar_prefetch=prefetch,
            grid=grid,
            in_specs=in_specs,
            out_specs=out_specs,
            scratch_shapes=list(scratch),
        ),
        out_shape=out_shape,
        compiler_params=pltpu.CompilerParams(vmem_limit_bytes=VMEM_LIMIT),
        cost_estimate=pl.CostEstimate(flops=flops, bytes_accessed=moved, transcendentals=0),
    )


def shaped(shape, dtype):
    return jax.ShapeDtypeStruct(shape, dtype)


def whole(shape):
    return pl.BlockSpec(shape, lambda *_: (0,) * len(shape))


def head_masks(dtype):
    lane = lax.broadcasted_iota(jnp.int32, (1, LANES), 1)
    first = (lane < LANES // 2).astype(jnp.float32)
    return (first.astype(dtype), (1.0 - first).astype(dtype))


def project_body(x_ref, gain_ref, wq_ref, wk_ref, wv_ref, normed_ref, q_ref, k_ref, v_ref):
    unit, _ = rms_parts(x_ref[...].astype(jnp.float32))
    normed = (unit * gain_ref[...]).astype(jnp.bfloat16)
    normed_ref[...] = normed
    q_ref[...] = matmul_nn(normed, wq_ref[...]).astype(jnp.bfloat16)
    k_ref[...] = matmul_nn(normed, wk_ref[...]).astype(jnp.bfloat16)
    v_ref[...] = matmul_nn(normed, wv_ref[...]).astype(jnp.bfloat16)


def attend_body(
    q_ref, k_ref, v_ref, strip_ref, wo_ref, e_ref, mixed_ref, inv_ref, part_ref, table_ref, acc_ref
):
    pair = pl.program_id(0)
    seq_len = k_ref.shape[0]
    rows = table_ref.shape[1]
    low_masks = head_masks(jnp.bfloat16)
    masks = head_masks(jnp.float32)
    for head in range(2):
        row = jnp.broadcast_to(strip_ref[0, head : head + 1, :], (rows, 2 * seq_len))
        table_ref[head] = pltpu.roll(row, 0, 1, stride=1, stride_axis=0)
    keys = k_ref[...]
    values = v_ref[...]
    values_h = tuple(values * low_masks[h] + low_masks[1 - h] for h in range(2))
    own_lanes = tuple(mask > 0.5 for mask in masks)
    for block in range(seq_len // rows):
        at = slice(block * rows, (block + 1) * rows)
        queries = q_ref[at, :]
        mixed = jnp.zeros((rows, LANES), jnp.float32)
        inverse = jnp.zeros((rows, LANES), jnp.float32)
        for head in range(2):
            scores = matmul_nt(queries * low_masks[head], keys)
            scores = scores + table_ref[head, :, seq_len - block * rows : 2 * seq_len - block * rows]
            top = jnp.max(scores, axis=-1, keepdims=True)
            weights = jnp.exp(scores - top).astype(jnp.bfloat16)
            e_ref[head, at, :] = weights
            summed = matmul_nn(weights, values_h[head])
            total = jnp.where(own_lanes[head], pltpu.roll(summed, LANES // 2, 1), 1.0)
            inv = masks[head] / total
            mixed = mixed + summed * inv
            inverse = inverse + inv
        mixed_ref[at, :] = mixed
        inv_ref[at, :] = inverse
        update = matmul_nt(mixed.astype(jnp.bfloat16), wo_ref[...])

        @pl.when(pair == 0)
        def _():
            acc_ref[at, :] = update

        @pl.when(pair != 0)
        def _():
            acc_ref[at, :] += update

    @pl.when(pair == pl.num_programs(0) - 1)
    def _():
        part_ref[...] = acc_ref[...].astype(jnp.bfloat16)


def feed_body(
    me_ref,
    x_ref,
    p_ref,
    r_ref,
    g_ref,
    gain_ref,
    wg_ref,
    wu_ref,
    wd_ref,
    normed_ref,
    hidden_ref,
    dgate_ref,
    dup_ref,
    dn_ref,
    send_ref,
    own_ref,
):
    step = pl.program_id(0)
    attended = x_ref[...].astype(jnp.float32) + (
        p_ref[...].astype(jnp.float32) + r_ref[...].astype(jnp.float32)
    )
    unit, _ = rms_parts(attended)
    normed = (unit * gain_ref[...]).astype(jnp.bfloat16)
    normed_ref[...] = normed
    gate = matmul_nn(normed, wg_ref[...])
    up = matmul_nn(normed, wu_ref[...])
    d_hidden = matmul_nn(g_ref[...], wd_ref[...])
    square = gate * gate
    root = 0.7978845608028654
    bend = jnp.tanh(gate * (root + (root * 0.044715) * square))
    half = 0.5 + 0.5 * bend
    gelu = gate * half
    slope = half + (0.5 * gate) * (1.0 - bend * bend) * (root + (3 * root * 0.044715) * square)
    hidden = (gelu * up).astype(jnp.bfloat16)
    d_gate = (d_hidden * up * slope).astype(jnp.bfloat16)
    d_up = (d_hidden * gelu).astype(jnp.bfloat16)
    hidden_ref[...] = hidden
    dgate_ref[...] = d_gate
    dup_ref[...] = d_up
    dn_ref[...] = (matmul_nt(d_gate, wg_ref[...]) + matmul_nt(d_up, wu_ref[...])).astype(
        jnp.bfloat16
    )
    out = matmul_nt(hidden, wd_ref[...])

    @pl.when(step < pl.num_programs(0) // 2)
    def _():
        send_ref[...] = out.astype(jnp.bfloat16)

    @pl.when(step >= pl.num_programs(0) // 2)
    def _():
        own_ref[...] = attended + out


def grads_body(left_ref, right_ref, out_ref, turned_ref):
    @pl.when(pl.program_id(0) == 0)
    def _():
        turned_ref[...] = left_ref[...].T

    out_ref[...] = matmul_nn(turned_ref[...], right_ref[...]).astype(jnp.bfloat16)


def turn_body(
    x_ref,
    p_ref,
    r_ref,
    g_ref,
    a_ref,
    b_ref,
    gain_ref,
    wo_ref,
    datt_ref,
    low_ref,
    dmix_ref,
    dgain_ref,
):
    attended = x_ref[...].astype(jnp.float32) + (
        p_ref[...].astype(jnp.float32) + r_ref[...].astype(jnp.float32)
    )
    unit, scale = rms_parts(attended)
    d_normed = a_ref[...].astype(jnp.float32) + b_ref[...].astype(jnp.float32)
    d_gain = jnp.sum(d_normed * unit, axis=0, keepdims=True)
    d_attended = g_ref[...].astype(jnp.float32) + rms_back(d_normed, unit, scale, gain_ref[...])
    d_low = d_attended.astype(jnp.bfloat16)
    datt_ref[...] = d_attended
    low_ref[...] = d_low
    dmix_ref[...] = matmul_nn(d_low, wo_ref[...]).astype(jnp.bfloat16)

    @pl.when(pl.program_id(0) == 0)
    def _():
        dgain_ref[...] = d_gain

    @pl.when(pl.program_id(0) != 0)
    def _():
        dgain_ref[...] += d_gain


def backward_body(
    q_ref,
    k_ref,
    v_ref,
    e_ref,
    dmix_ref,
    mixed_ref,
    inv_ref,
    dq_ref,
    dk_ref,
    dv_ref,
    strip_ref,
    table_ref,
    dkt_ref,
    dvt_ref,
):
    seq_len = k_ref.shape[0]
    rows = table_ref.shape[1]
    low_masks = head_masks(jnp.bfloat16)
    masks = head_masks(jnp.float32)
    keys = k_ref[...]
    values = v_ref[...]
    keys_h = tuple(keys * low_masks[h] for h in range(2))
    table_ref[...] = jnp.zeros_like(table_ref)
    for block in range(seq_len // rows):
        at = slice(block * rows, (block + 1) * rows)
        queries = q_ref[at, :]
        scaled = (dmix_ref[at, :].astype(jnp.float32) * inv_ref[at, :]).astype(jnp.bfloat16)
        product = scaled.astype(jnp.float32) * mixed_ref[at, :]
        d_query = jnp.zeros((rows, LANES), jnp.float32)
        d_key = jnp.zeros((LANES, seq_len), jnp.float32)
        d_value = jnp.zeros((LANES, seq_len), jnp.float32)
        for head in range(2):
            scaled_h = scaled * low_masks[head]
            delta = jnp.sum(product * masks[head], axis=-1, keepdims=True)
            weights = e_ref[head, at, :]
            d_scores = weights.astype(jnp.float32) * (matmul_nt(scaled_h, values) - delta)
            d_low = d_scores.astype(jnp.bfloat16)
            window = slice(seq_len - block * rows, 2 * seq_len - block * rows)
            table_ref[head, :, window] += d_scores
            d_query = d_query + matmul_nn(d_low, keys_h[head])
            d_key = d_key + matmul_tn(queries * low_masks[head], d_low)
            d_value = d_value + matmul_tn(scaled_h, weights)
        dq_ref[at, :] = d_query.astype(jnp.bfloat16)
        if block == 0:
            dkt_ref[...] = d_key
            dvt_ref[...] = d_value
        else:
            dkt_ref[...] += d_key
            dvt_ref[...] += d_value
    dk_ref[...] = dkt_ref[...].T.astype(jnp.bfloat16)
    dv_ref[...] = dvt_ref[...].T.astype(jnp.bfloat16)
    width = 2 * seq_len
    sub = lax.broadcasted_iota(jnp.int32, (8, 1), 0)
    for head in range(2):
        total = table_ref[head, 0:8, :]
        for group in range(1, rows // 8):
            part = table_ref[head, 8 * group : 8 * group + 8, :]
            total = total + pltpu.roll(part, width - 8 * group, 1)
        for bit in (1, 2, 4):
            total = jnp.where((sub & bit) != 0, pltpu.roll(total, width - bit, 1), total)
        strip_ref[0, head : head + 1, :] = jnp.sum(total, axis=0, keepdims=True)


def spread_body(
    me_ref,
    x_ref,
    dq_ref,
    dk_ref,
    dv_ref,
    wq_ref,
    wk_ref,
    wv_ref,
    send_ref,
    own_ref,
    dgain_ref,
):
    step = pl.program_id(0)
    unit, _ = rms_parts(x_ref[...].astype(jnp.float32))
    d_normed = (
        matmul_nt(dq_ref[...], wq_ref[...])
        + matmul_nt(dk_ref[...], wk_ref[...])
        + matmul_nt(dv_ref[...], wv_ref[...])
    )
    d_gain = jnp.sum(d_normed * unit, axis=0, keepdims=True)

    @pl.when(step == 0)
    def _():
        dgain_ref[...] = d_gain

    @pl.when(step != 0)
    def _():
        dgain_ref[...] += d_gain

    @pl.when(step < pl.num_programs(0) // 2)
    def _():
        send_ref[...] = d_normed.astype(jnp.bfloat16)

    @pl.when(step >= pl.num_programs(0) // 2)
    def _():
        own_ref[...] = d_normed


def finish_body(me_ref, x_ref, own_ref, other_ref, datt_ref, gain_ref, out_ref):
    unit, scale = rms_parts(x_ref[...].astype(jnp.float32))
    d_normed = own_ref[...] + other_ref[...].astype(jnp.float32)
    out_ref[...] = (datt_ref[...] + rms_back(d_normed, unit, scale, gain_ref[...])).astype(
        jnp.bfloat16
    )


def weight_grads(left, right, columns):
    depth, height = left.shape
    width = right.shape[1]
    return call(
        grads_body,
        (width // columns,),
        [whole((depth, height)), pl.BlockSpec((depth, columns), lambda i: (0, i))],
        pl.BlockSpec((height, columns), lambda i: (0, i)),
        shaped((height, width), jnp.bfloat16),
        [pltpu.VMEM((height, depth), jnp.bfloat16)],
        flops=2 * depth * height * width,
        moved=2 * (depth * height + depth * width + height * width),
    )(left, right)


def on_core_pair(
    tokens,
    cotangent,
    gain_attn,
    w_query,
    w_key,
    w_value,
    w_out,
    rel_table,
    buckets,
    gain_ffn,
    w_gate,
    w_up,
    w_down,
):
    low = jnp.bfloat16
    high = jnp.float32
    own_rows, features = tokens.shape
    seq_len = 2 * own_rows
    width = w_query.shape[1]
    units = w_gate.shape[1]
    pairs = width // LANES
    bucket_count = rel_table.shape[0]
    me = lax.axis_index("mp")
    me_arg = me.astype(jnp.int32).reshape(1)
    rows = MXU_ROWS
    steps = seq_len // rows
    half_steps = steps // 2
    swap = [(0, 1), (1, 0)]

    def swapped(array):
        return lax.ppermute(array, "mp", swap)

    def in_order(array):
        other = swapped(array)
        first = jnp.where(me == 0, array, other)
        second = jnp.where(me == 0, other, array)
        return jnp.concatenate([first, second], axis=0)

    parts = (w_gate, w_up, w_down.T, w_query, w_key, w_value, w_out.T)
    gathered = lax.all_gather(jnp.concatenate(parts, axis=1), "dp", axis=0, tiled=True)
    at_query = 3 * units // width

    def unit_block(index):
        return pl.BlockSpec((features, units), lambda *_: (0, index))

    def head_block(index):
        return pl.BlockSpec((features, width), lambda *_: (0, at_query + index))

    x_all = in_order(tokens)
    g_all = in_order(cotangent)
    gain_a = gain_attn.reshape(1, features)
    gain_f = gain_ffn.reshape(1, features)

    one_hot = (buckets[:, None] == jnp.arange(bucket_count, dtype=jnp.int32)[None, :]).astype(high)
    one_hot = jnp.pad(one_hot, ((1, 0), (0, 0)))
    head_count = rel_table.shape[1]
    local_heads = head_count // 2
    my_table = lax.dynamic_slice_in_dim(rel_table, me * local_heads, local_heads, 1)
    strip = lax.dot_general(my_table, one_hot, (((0,), (1,)), ((), ())), precision=precise)
    strip = strip.reshape(pairs, 2, 2 * seq_len)

    def row_block(columns):
        return pl.BlockSpec((rows, columns), lambda i, *_: (i, 0))

    normed_a, queries, keys, values = call(
        project_body,
        (steps,),
        [row_block(features), whole((1, features)), head_block(0), head_block(1), head_block(2)],
        [row_block(features)] + [row_block(width)] * 3,
        [shaped((seq_len, features), low)] + [shaped((seq_len, width), low)] * 3,
        flops=6 * seq_len * features * width,
        moved=4 * seq_len * features + 6 * (features + seq_len) * width,
    )(x_all, gain_a, gathered, gathered, gathered)

    pair_block = pl.BlockSpec((seq_len, LANES), lambda p: (0, p))
    e_block = pl.BlockSpec((2, seq_len, seq_len), lambda p: (p, 0, 0))
    strip_block = pl.BlockSpec((1, 2, 2 * seq_len), lambda p: (p, 0, 0))
    table_scratch = pltpu.VMEM((2, rows, 2 * seq_len), high)
    attend_flops = 8 * 2 * pairs * seq_len * seq_len * LANES
    e_bytes = 4 * pairs * seq_len * seq_len
    weights_e, mixed, inverse, part = call(
        attend_body,
        (pairs,),
        [
            pair_block,
            pair_block,
            pair_block,
            strip_block,
            pl.BlockSpec((features, LANES), lambda p: (0, (at_query + 3) * pairs + p)),
        ],
        [e_block, pair_block, pair_block, whole((seq_len, features))],
        [
            shaped((2 * pairs, seq_len, seq_len), low),
            shaped((seq_len, width), high),
            shaped((seq_len, width), high),
            shaped((seq_len, features), low),
        ],
        [table_scratch, pltpu.VMEM((seq_len, features), high)],
        flops=attend_flops,
        moved=e_bytes + 20 * seq_len * width,
    )(queries, keys, values, strip, gathered)
    part_other = swapped(part)

    turned_row = lambda columns: pl.BlockSpec(
        (rows, columns), lambda i, m: ((i + half_steps * (1 - m[0])) % steps, 0)
    )
    send_row = pl.BlockSpec((rows, features), lambda i, m: (jnp.minimum(i, half_steps - 1), 0))
    keep_row = pl.BlockSpec((rows, features), lambda i, m: (jnp.maximum(i - half_steps, 0), 0))
    normed_f, hidden, d_gate, d_up, dn_part, out_send, out_own = call(
        feed_body,
        (steps,),
        [turned_row(features)] * 4
        + [whole((1, features)), unit_block(0), unit_block(1), unit_block(2)],
        [turned_row(features)]
        + [turned_row(units)] * 3
        + [turned_row(features), send_row, keep_row],
        [
            shaped((seq_len, features), low),
            shaped((seq_len, units), low),
            shaped((seq_len, units), low),
            shaped((seq_len, units), low),
            shaped((seq_len, features), low),
            shaped((own_rows, features), low),
            shaped((own_rows, features), high),
        ],
        prefetch=1,
        flops=12 * seq_len * features * units,
        moved=6 * features * units + 16 * seq_len * features + 6 * seq_len * units,
    )(me_arg, x_all, part, part_other, g_all, gain_f, gathered, gathered, gathered)
    dn_other = swapped(dn_part)
    out_other = swapped(out_send)
    output = (out_own + out_other.astype(high)).astype(low)

    d_gate_w = weight_grads(normed_f, d_gate, units // 2)
    d_up_w = weight_grads(normed_f, d_up, units // 2)
    d_down_w = weight_grads(g_all, hidden, units // 2)

    d_attended, d_low, d_mixed, d_gain_f = call(
        turn_body,
        (steps,),
        [row_block(features)] * 6 + [whole((1, features)), head_block(3)],
        [row_block(features), row_block(features), row_block(width), whole((1, features))],
        [
            shaped((seq_len, features), high),
            shaped((seq_len, features), low),
            shaped((seq_len, width), low),
            shaped((1, features), high),
        ],
        flops=2 * seq_len * features * width,
        moved=20 * seq_len * features + 2 * seq_len * width,
    )(x_all, part, part_other, g_all, dn_part, dn_other, gain_f, gathered)

    d_query, d_key, d_value, d_strip = call(
        backward_body,
        (pairs,),
        [pair_block, pair_block, pair_block, e_block, pair_block, pair_block, pair_block],
        [pair_block, pair_block, pair_block, strip_block],
        [shaped((seq_len, width), low)] * 3 + [shaped((pairs, 2, 2 * seq_len), high)],
        [table_scratch, pltpu.VMEM((LANES, seq_len), high), pltpu.VMEM((LANES, seq_len), high)],
        flops=2 * attend_flops,
        moved=e_bytes + 22 * seq_len * width,
    )(queries, keys, values, weights_e, d_mixed, mixed, inverse)
    d_out_w = weight_grads(d_low, mixed.astype(low), width)

    dna_send, dna_own, d_gain_a = call(
        spread_body,
        (steps,),
        [turned_row(features)] + [turned_row(width)] * 3 + [head_block(0), head_block(1), head_block(2)],
        [send_row, keep_row, whole((1, features))],
        [
            shaped((own_rows, features), low),
            shaped((own_rows, features), high),
            shaped((1, features), high),
        ],
        prefetch=1,
        flops=6 * seq_len * features * width,
        moved=8 * seq_len * features + 6 * seq_len * width,
    )(me_arg, x_all, d_query, d_key, d_value, gathered, gathered, gathered)
    dna_other = swapped(dna_send)
    d_query_w = weight_grads(normed_a, d_query, width)
    d_key_w = weight_grads(normed_a, d_key, width)
    d_value_w = weight_grads(normed_a, d_value, width)

    grads = jnp.concatenate(
        [d_gate_w, d_up_w, d_down_w, d_query_w, d_key_w, d_value_w, d_out_w], axis=1
    )
    grads = lax.psum_scatter(grads, "dp", scatter_dimension=0, tiled=True).astype(high)

    d_tokens = call(
        finish_body,
        (half_steps,),
        [
            row_block(features),
            row_block(features),
            row_block(features),
            pl.BlockSpec((rows, features), lambda i, m: (i + m[0] * half_steps, 0)),
            whole((1, features)),
        ],
        row_block(features),
        shaped((own_rows, features), low),
        prefetch=1,
        flops=0,
        moved=14 * own_rows * features,
    )(me_arg, tokens, dna_own, dna_other, d_attended, gain_a)

    d_bias = d_strip.reshape(local_heads, 2 * seq_len)
    my_d_table = lax.dot_general(one_hot, d_bias, (((0,), (1,)), ((), ())), precision=precise)
    d_table = lax.dynamic_update_slice_in_dim(
        jnp.zeros_like(rel_table), my_d_table, me * local_heads, 1
    )
    small = lax.psum((d_gain_a, 0.5 * d_gain_f, d_table), ("dp", "mp"))
    head_grads = [
        grads[:, 3 * units + i * width : 3 * units + (i + 1) * width] for i in range(4)
    ]
    return (
        output,
        d_tokens,
        small[0].reshape(features),
        head_grads[0],
        head_grads[1],
        head_grads[2],
        head_grads[3].T,
        small[2],
        small[1].reshape(features),
        grads[:, :units],
        grads[:, units : 2 * units],
        grads[:, 2 * units : 3 * units].T,
    )


def solution(mesh):
    placed = (
        P(("dp", "mp"), None),
        P(("dp", "mp"), None),
        P(),
        P("dp", "mp"),
        P("dp", "mp"),
        P("dp", "mp"),
        P("mp", "dp"),
        P(),
        P(),
        P(),
        P("dp", "mp"),
        P("dp", "mp"),
        P("mp", "dp"),
    )
    body = on_device if mesh.shape["mp"] != 2 else on_core_pair
    return jax.shard_map(
        body,
        mesh=mesh,
        in_specs=placed,
        out_specs=(
            P(("dp", "mp"), None),
            P(("dp", "mp"), None),
            P(),
            P("dp", "mp"),
            P("dp", "mp"),
            P("dp", "mp"),
            P("mp", "dp"),
            P(),
            P(),
            P("dp", "mp"),
            P("dp", "mp"),
            P("mp", "dp"),
        ),
        check_vma=False,
    )
```

```python
import functools

import jax
import jax.numpy as jnp
from jax import lax
from jax.experimental import pallas as pl
from jax.experimental.pallas import tpu as pltpu
from jax.sharding import PartitionSpec as P

epsilon = 1e-06
block_limit = 512
precise = lax.Precision.HIGHEST


def as_sent(array):

    def short(part):
        return part.astype(jnp.bfloat16) if part.dtype == jnp.float32 else part

    return jax.tree.map(short, array)


def matmul_nn(left, right):
    return jnp.dot(left, right, preferred_element_type=jnp.float32)


def matmul_nt(left, right):
    return lax.dot_general(
        left, right, (((1,), (1,)), ((), ())), preferred_element_type=jnp.float32
    )


def matmul_tn(left, right):
    return lax.dot_general(
        left, right, (((0,), (0,)), ((), ())), preferred_element_type=jnp.float32
    )


def rms_parts(inputs):
    scale = lax.rsqrt(jnp.mean(inputs * inputs, axis=-1, keepdims=True) + epsilon)
    return (inputs * scale, scale)


def rms_back(d_normed, unit, scale, gain):
    d_unit = d_normed * gain
    return scale * (d_unit - unit * jnp.mean(d_unit * unit, axis=-1, keepdims=True))


def gated(gate_pre, up_pre):
    return jax.nn.gelu(gate_pre, approximate=True) * up_pre


def window_base(first_query, first_key, row_count, seq_len):
    return first_key - first_query - row_count + seq_len


def make_bias(bias_full, base, row_count, width):
    span = width + row_count - 1
    head_count = bias_full.shape[0]
    strip = lax.dynamic_slice_in_dim(bias_full, base, span, 1)
    tiled = jnp.tile(strip, (1, row_count + 1))
    window = tiled[:, row_count - 1 : row_count - 1 + row_count * (span - 1)]
    return window.reshape(head_count, row_count, span - 1)[:, :, :width]


def skew_sum(d_block, row_count, width):
    head_count = d_block.shape[0]
    span = width + row_count - 1
    padded = jnp.pad(d_block, ((0, 0), (0, 0), (row_count - 1, 0)))
    flat = padded.reshape(head_count, row_count * span)
    flat = jnp.pad(flat, ((0, 0), (0, row_count)))
    skewed = flat.reshape(head_count, row_count, span + 1)[:, :, :span]
    return jnp.sum(skewed, axis=1)


def add_window(d_bias, piece, base):
    current = lax.dynamic_slice_in_dim(d_bias, base, piece.shape[1], 1)
    return lax.dynamic_update_slice_in_dim(d_bias, current + piece, base, 1)


def sum_rows(partial_value):
    return lax.psum_scatter(
        partial_value.astype(jnp.bfloat16), "mp", scatter_dimension=0, tiled=True
    ).astype(jnp.float32)


def split_heads(queries, keys_all, values, head_count):
    row_count = queries.shape[0]
    seq_len = keys_all.shape[0]
    head_dim = queries.shape[1] // head_count
    width = min(block_limit, seq_len)
    blocks = seq_len // width
    heads_q = queries.reshape(row_count, head_count, head_dim)
    heads_k = keys_all.reshape(blocks, width, head_count, head_dim)
    heads_v = values.reshape(blocks, width, head_count, head_dim)
    starts = jnp.arange(blocks, dtype=jnp.int32) * width
    return (heads_q, heads_k, heads_v, starts, width)


def attend_forward(queries, keys_all, values, bias_full, head_count, first_row):
    row_count = queries.shape[0]
    seq_len = keys_all.shape[0]
    heads_q, heads_k, heads_v, starts, width = split_heads(queries, keys_all, values, head_count)

    def block_scores(key_block, first_key):
        raw_scores = jnp.einsum(
            "qhd,khd->hqk", heads_q, key_block, preferred_element_type=jnp.float32
        )
        base = window_base(first_row, first_key, row_count, seq_len)
        return raw_scores + make_bias(bias_full, base, row_count, width)

    def stats_step(running, pieces):
        top_now, total = running
        scores = block_scores(pieces[0], pieces[1])
        top_new = jnp.maximum(top_now, jnp.max(scores, axis=-1))
        total = total * jnp.exp(top_now - top_new) + jnp.sum(
            jnp.exp(scores - top_new[..., None]), axis=-1
        )
        return ((top_new, total), None)

    start_top = jnp.full((head_count, row_count), -jnp.inf, jnp.float32)
    start_total = jnp.zeros((head_count, row_count), jnp.float32)
    (top_all, total), _ = lax.scan(stats_step, (start_top, start_total), (heads_k, starts))
    log_total = top_all + jnp.log(total)

    def mix_step(running, pieces):
        scores = block_scores(pieces[0], pieces[2])
        probs_low = jnp.exp(scores - log_total[..., None]).astype(jnp.bfloat16)
        update = jnp.einsum(
            "hqk,khd->qhd", probs_low, pieces[1], preferred_element_type=jnp.float32
        )
        return (running + update, None)

    start_mix = jnp.zeros(heads_q.shape, jnp.float32)
    mixed_f, _ = lax.scan(mix_step, start_mix, (heads_k, heads_v, starts))
    return (mixed_f.reshape(row_count, queries.shape[1]), log_total)


def attend_backward(
    queries, keys_all, values, bias_full, head_count, first_row, log_total, deltas, d_mixed
):
    row_count = queries.shape[0]
    seq_len = keys_all.shape[0]
    heads_q, heads_k, heads_v, starts, width = split_heads(queries, keys_all, values, head_count)
    heads_d = d_mixed.reshape(heads_q.shape)

    def back_step(running, pieces):
        d_query, d_bias = running
        key_block, value_block, first_key = pieces
        base = window_base(first_row, first_key, row_count, seq_len)
        scores = jnp.einsum("qhd,khd->hqk", heads_q, key_block, preferred_element_type=jnp.float32)
        scores = scores + make_bias(bias_full, base, row_count, width)
        probs = jnp.exp(scores - log_total[..., None])
        d_probs = jnp.einsum(
            "qhd,khd->hqk", heads_d, value_block, preferred_element_type=jnp.float32
        )
        d_scores = (probs * (d_probs - deltas[..., None])).astype(jnp.bfloat16)
        d_query = d_query + jnp.einsum(
            "hqk,khd->qhd", d_scores, key_block, preferred_element_type=jnp.float32
        )
        d_bias = add_window(d_bias, skew_sum(d_scores.astype(jnp.float32), row_count, width), base)
        probs_low = probs.astype(jnp.bfloat16)
        d_value = jnp.einsum("hqk,qhd->khd", probs_low, heads_d, preferred_element_type=jnp.float32)
        d_key = jnp.einsum("hqk,qhd->khd", d_scores, heads_q, preferred_element_type=jnp.float32)
        return ((d_query, d_bias), (d_key, d_value))

    start_query = jnp.zeros(heads_q.shape, jnp.float32)
    (d_query, d_bias), kv_parts = lax.scan(
        back_step, (start_query, jnp.zeros_like(bias_full)), (heads_k, heads_v, starts)
    )
    feature_count = queries.shape[1]
    d_query = d_query.reshape(row_count, feature_count)
    return (
        d_query,
        d_bias,
        kv_parts[0].reshape(seq_len, feature_count),
        kv_parts[1].reshape(seq_len, feature_count),
    )


def on_device(
    tokens,
    cotangent,
    gain_attn,
    w_query,
    w_key,
    w_value,
    w_out,
    rel_table,
    buckets,
    gain_ffn,
    w_gate,
    w_up,
    w_down,
):
    head_count = rel_table.shape[1]
    bucket_count = rel_table.shape[0]
    inputs = tokens.astype(jnp.float32)
    row_count = inputs.shape[0]
    feature_count = inputs.shape[1]
    first_row = lax.axis_index("mp") * row_count
    attn_parts = (w_query, w_key, w_value, w_out.T)
    ffn_parts = (w_gate, w_up, w_down.T)
    ffn_cols = ()
    col_parts = lax.all_gather(as_sent(attn_parts + ffn_cols), "mp", axis=1, tiled=True)
    full_parts = lax.all_gather(as_sent(tuple(col_parts) + ffn_parts), "dp", axis=0, tiled=True)
    query_full, key_full, value_full, out_full, gate_full, up_full, down_full = full_parts
    unit_a, scale_a = rms_parts(inputs)
    normed_a = (unit_a * gain_attn).astype(jnp.bfloat16)
    queries = matmul_nn(normed_a, query_full).astype(jnp.bfloat16)
    own_keys = matmul_nn(normed_a, key_full).astype(jnp.bfloat16)
    own_values = matmul_nn(normed_a, value_full).astype(jnp.bfloat16)
    keys_all, values = (
        lax.all_gather(own_keys, "mp", axis=0, tiled=True),
        lax.all_gather(own_values, "mp", axis=0, tiled=True),
    )
    one_hot = (buckets[:, None] == jnp.arange(bucket_count, dtype=jnp.int32)[None, :]).astype(
        jnp.float32
    )
    bias_full = jnp.dot(one_hot, rel_table, precision=precise).T
    mixed_f, log_total = attend_forward(queries, keys_all, values, bias_full, head_count, first_row)
    mixed_out = mixed_f.astype(jnp.bfloat16)
    attended = inputs + matmul_nt(mixed_out, out_full)
    unit_f, scale_f = rms_parts(attended)
    normed_f = (unit_f * gain_ffn).astype(jnp.bfloat16)
    normed_seq, cot_seq = (
        lax.all_gather(normed_f, "mp", axis=0, tiled=True),
        lax.all_gather(cotangent, "mp", axis=0, tiled=True),
    )
    gate_pre = matmul_nn(normed_seq, gate_full)
    up_pre = matmul_nn(normed_seq, up_full)
    hidden = gated(gate_pre, up_pre).astype(jnp.bfloat16)
    output = attended + sum_rows(matmul_nt(hidden, down_full))
    d_hidden = matmul_nn(cot_seq, down_full)
    d_down = matmul_tn(cot_seq, hidden)
    _, pull_gate = jax.vjp(gated, gate_pre, up_pre)
    d_gate, d_up = pull_gate(d_hidden)
    d_gate = d_gate.astype(jnp.bfloat16)
    d_up = d_up.astype(jnp.bfloat16)
    d_normed_f = sum_rows(matmul_nt(d_gate, gate_full) + matmul_nt(d_up, up_full))
    d_gate_w = matmul_tn(normed_seq, d_gate)
    d_up_w = matmul_tn(normed_seq, d_up)
    d_gain_f = jnp.sum(d_normed_f * unit_f, axis=0)
    d_attended = cotangent.astype(jnp.float32) + rms_back(d_normed_f, unit_f, scale_f, gain_ffn)
    d_att_low = d_attended.astype(jnp.bfloat16)
    d_out_w = matmul_tn(d_att_low, mixed_out)
    d_mixed = matmul_nn(d_att_low, out_full).astype(jnp.bfloat16)
    head_dim = feature_count // head_count
    deltas = jnp.sum(
        (d_mixed.astype(jnp.float32) * mixed_f).reshape(row_count, head_count, head_dim), axis=-1
    ).T
    d_query, d_bias, d_keys_part, d_values_part = attend_backward(
        queries, keys_all, values, bias_full, head_count, first_row, log_total, deltas, d_mixed
    )
    d_keys_own, d_values_own = (
        lax.psum_scatter(
            d_keys_part.astype(jnp.bfloat16), "mp", scatter_dimension=0, tiled=True
        ).astype(jnp.float32),
        lax.psum_scatter(
            d_values_part.astype(jnp.bfloat16), "mp", scatter_dimension=0, tiled=True
        ).astype(jnp.float32),
    )
    d_keys_own = d_keys_own.astype(jnp.bfloat16)
    d_values_own = d_values_own.astype(jnp.bfloat16)
    d_query = d_query.astype(jnp.bfloat16)
    d_normed_a = (
        matmul_nt(d_query, query_full)
        + matmul_nt(d_keys_own, key_full)
        + matmul_nt(d_values_own, value_full)
    )
    d_query_w = matmul_tn(normed_a, d_query)
    d_key_w = matmul_tn(normed_a, d_keys_own)
    d_value_w = matmul_tn(normed_a, d_values_own)
    d_gain_a = jnp.sum(d_normed_a * unit_a, axis=0)
    d_tokens = (d_attended + rms_back(d_normed_a, unit_a, scale_a, gain_attn)).astype(jnp.bfloat16)
    d_table = jnp.dot(d_bias, one_hot, precision=precise).T
    row_grads = (
        lax.psum_scatter(
            d_query_w.astype(jnp.bfloat16), "dp", scatter_dimension=0, tiled=True
        ).astype(jnp.float32),
        lax.psum_scatter(
            d_key_w.astype(jnp.bfloat16), "dp", scatter_dimension=0, tiled=True
        ).astype(jnp.float32),
        lax.psum_scatter(
            d_value_w.astype(jnp.bfloat16), "dp", scatter_dimension=0, tiled=True
        ).astype(jnp.float32),
        lax.psum_scatter(
            d_out_w.astype(jnp.bfloat16), "dp", scatter_dimension=0, tiled=True
        ).astype(jnp.float32),
        lax.psum_scatter(
            d_gate_w.astype(jnp.bfloat16), "dp", scatter_dimension=0, tiled=True
        ).astype(jnp.float32),
        lax.psum_scatter(d_up_w.astype(jnp.bfloat16), "dp", scatter_dimension=0, tiled=True).astype(
            jnp.float32
        ),
        lax.psum_scatter(d_down.astype(jnp.bfloat16), "dp", scatter_dimension=0, tiled=True).astype(
            jnp.float32
        ),
    )
    row_grads = tuple(row_grads)
    ffn_late = ()
    col_grads = tuple(
        jax.tree.map(
            lambda part: part.astype(jnp.float32),
            lax.psum_scatter(
                as_sent(row_grads[:4] + ffn_late), "mp", scatter_dimension=1, tiled=True
            ),
        )
    )
    ffn_done = row_grads[4:]
    small_sums = lax.psum((d_gain_a, d_gain_f, d_table), ("dp", "mp"))
    return (
        output.astype(jnp.bfloat16),
        d_tokens,
        small_sums[0],
        col_grads[0],
        col_grads[1],
        col_grads[2],
        col_grads[3].T,
        small_sums[2],
        small_sums[1],
        ffn_done[0],
        ffn_done[1],
        ffn_done[2].T,
    )


MXU_ROWS = 256
LANES = 128
VMEM_LIMIT = 56 * 2**20
PEAK_PER_MICRO = 1_153_500_000
LOW = jnp.bfloat16
HIGH = jnp.float32


def call(
    body, grid, in_specs, out_specs, out_shape, scratch=(), prefetch=0, micros=5, aliases=None
):
    return pl.pallas_call(
        body,
        grid_spec=pltpu.PrefetchScalarGridSpec(
            num_scalar_prefetch=prefetch,
            grid=grid,
            in_specs=in_specs,
            out_specs=out_specs,
            scratch_shapes=list(scratch),
        ),
        out_shape=out_shape,
        input_output_aliases=aliases or {},
        compiler_params=pltpu.CompilerParams(vmem_limit_bytes=VMEM_LIMIT),
        cost_estimate=pl.CostEstimate(
            flops=int(micros * PEAK_PER_MICRO), bytes_accessed=0, transcendentals=0
        ),
    )


def shaped(shape, dtype):
    return jax.ShapeDtypeStruct(shape, dtype)


def whole(shape):
    return pl.BlockSpec(shape, lambda *_: (0,) * len(shape), pipeline_mode=pl.Buffered(1))


def result(shape):
    return pl.BlockSpec(shape, lambda *_: (0,) * len(shape))


def together(*arrays):
    return lax.optimization_barrier(arrays)


def ring_shift(steps, count):
    return [(i, (i + steps) % count) for i in range(count)]


def flip(bit, count):
    return [(i, i ^ bit) for i in range(count)]


def over_x(array):
    return lax.ppermute(array, "dp", flip(1, lax.axis_size("dp")))


def over_y(array):
    return lax.ppermute(array, "dp", flip(2, lax.axis_size("dp")))


def over_far(array, steps):
    return lax.ppermute(array, "dp", ring_shift(4 * steps, lax.axis_size("dp")))


def dp_place():
    index = lax.axis_index("dp")
    return (index // 4, (index // 2) % 2, index % 2)


def in_bit_order(own, other, bit, axis):
    return jnp.stack([jnp.where(bit == 0, own, other), jnp.where(bit == 0, other, own)], axis=axis)


def far_pieces(shard):
    return [over_far(shard, k) for k in range(1, lax.axis_size("dp") // 4)]


def far_stack(shard, pieces):
    far = len(pieces) + 1
    place = dp_place()[0]
    stacked = jnp.zeros((far,) + shard.shape, shard.dtype)
    for k, piece in enumerate([shard] + pieces):
        stacked = lax.dynamic_update_slice(stacked, piece[None], ((place - k) % far, 0, 0))
    return stacked


def at_bit(array, bit, axis):
    return lax.dynamic_index_in_dim(array, bit, axis, False)


def add_low(left, right):
    return (left.astype(HIGH) + right.astype(HIGH)).astype(LOW)


def sum_all(vector):
    count = lax.axis_size("dp")
    vector = vector + lax.ppermute(vector, "mp", [(0, 1), (1, 0)])
    vector = sum(far_pieces(vector), vector)
    return sum((lax.ppermute(vector, "dp", flip(k, count)) for k in range(1, 4)), vector)


def head_masks(dtype):
    lane = lax.broadcasted_iota(jnp.int32, (1, LANES), 1)
    first = (lane < LANES // 2).astype(HIGH)
    return (first.astype(dtype), (1.0 - first).astype(dtype))


def put_weights(full_ref, own_ref, other_ref, axis, bit):
    if axis == 1:
        full_ref[:, bit] = own_ref[...]
        full_ref[:, 1 - bit] = other_ref[...]
    else:
        full_ref[:, :, bit] = own_ref[...]
        full_ref[:, :, 1 - bit] = other_ref[...]


def matrix(full_ref, start, columns):
    part = full_ref[:, :, :, :, start : start + columns]
    return part.reshape(-1, columns)


def project_body(
    place_ref,
    x_ref,
    gain_ref,
    qk_own_ref,
    qk_other_ref,
    vo_own_ref,
    vo_other_ref,
    turned_ref,
    q_ref,
    k_ref,
    v_ref,
    qkv_ref,
    wo_ref,
    qk_ref,
    vo_ref,
):
    width = q_ref.shape[1]

    @pl.when(pl.program_id(0) == 0)
    def _():
        put_weights(qk_ref, qk_own_ref, qk_other_ref, 2, place_ref[1])
        put_weights(vo_ref, vo_own_ref, vo_other_ref, 1, place_ref[0])
        qkv_ref[:, : 2 * width] = matrix(qk_ref, 0, 2 * width)
        qkv_ref[:, 2 * width :] = matrix(vo_ref, 0, width)
        wo_ref[...] = matrix(vo_ref, width, width)

    unit, _ = rms_parts(x_ref[...].astype(HIGH))
    normed = (unit * gain_ref[...]).astype(LOW)
    turned_ref[...] = normed.T
    q_ref[...] = matmul_nn(normed, qkv_ref[:, :width]).astype(LOW)
    k_ref[...] = matmul_nn(normed, qkv_ref[:, width : 2 * width]).astype(LOW)
    v_ref[...] = matmul_nn(normed, qkv_ref[:, 2 * width :]).astype(LOW)


def attend_body(
    q_ref, k_ref, v_ref, strip_ref, wo_ref, e_ref, mixed_ref, low_ref, inv_ref, part_ref, table_ref, acc_ref
):
    pair = pl.program_id(0)
    seq_len = k_ref.shape[0]
    rows = table_ref.shape[1]
    low_masks = head_masks(LOW)
    masks = head_masks(HIGH)
    own_lanes = tuple(mask > 0.5 for mask in masks)
    for head in range(2):
        row = jnp.broadcast_to(strip_ref[0, head : head + 1, :], (rows, 2 * seq_len))
        table_ref[head] = pltpu.roll(row, 0, 1, stride=1, stride_axis=0)
    keys = k_ref[...]
    values = v_ref[...]
    values_h = tuple(values * low_masks[h] + low_masks[1 - h] for h in range(2))

    @pl.when(pair == 0)
    def _():
        acc_ref[...] = jnp.zeros_like(acc_ref)

    for block in range(seq_len // rows):
        at = slice(block * rows, (block + 1) * rows)
        queries = q_ref[at, :]
        mixed = jnp.zeros((rows, LANES), HIGH)
        inverse = jnp.zeros((rows, LANES), HIGH)
        for head in range(2):
            scores = matmul_nt(queries * low_masks[head], keys)
            scores = scores + table_ref[head, :, seq_len - block * rows : 2 * seq_len - block * rows]
            top = jnp.max(scores, axis=-1, keepdims=True)
            weights = jnp.exp(scores - top).astype(LOW)
            e_ref[head, at, :] = weights
            summed = matmul_nn(weights, values_h[head])
            total = jnp.where(own_lanes[head], pltpu.roll(summed, LANES // 2, 1), 1.0)
            inv = masks[head] / total
            mixed = mixed + summed * inv
            inverse = inverse + inv
        mixed_ref[at, :] = mixed
        low = mixed.astype(LOW)
        low_ref[at, :] = low
        inv_ref[at, :] = inverse
        acc_ref[at, :] += matmul_nt(low, wo_ref[...])

    @pl.when(pair == pl.num_programs(0) - 1)
    def _():
        part_ref[...] = acc_ref[...].astype(LOW)


def feed_body(
    place_ref,
    x_ref,
    p_ref,
    r_ref,
    g_ref,
    gain_ref,
    gu_own_ref,
    gu_other_ref,
    ud_own_ref,
    ud_other_ref,
    turned_ref,
    g_turned_ref,
    hidden_ref,
    dgu_ref,
    dn_ref,
    send_ref,
    own_ref,
    gu_ref,
    ud_ref,
):
    step = pl.program_id(0)

    @pl.when(step == 0)
    def _():
        put_weights(gu_ref, gu_own_ref, gu_other_ref, 2, place_ref[1])
        put_weights(ud_ref, ud_own_ref, ud_other_ref, 1, place_ref[0])

    attended = x_ref[...].astype(HIGH) + (p_ref[...].astype(HIGH) + r_ref[...].astype(HIGH))
    unit, _ = rms_parts(attended)
    normed = (unit * gain_ref[...]).astype(LOW)
    turned_ref[...] = normed.T
    cotangent = g_ref[...]
    g_turned_ref[...] = cotangent.T
    root = 0.7978845608028654
    columns = hidden_ref.shape[1] // 2
    out = 0.0
    d_normed = 0.0
    for part in range(2):
        w_gate = matrix(gu_ref, part * columns, columns)
        w_up = matrix(ud_ref, 0, columns) if part else matrix(gu_ref, 2 * columns, columns)
        w_down = matrix(ud_ref, (1 + part) * columns, columns)
        gate = matmul_nn(normed, w_gate)
        up = matmul_nn(normed, w_up)
        d_hidden = matmul_nn(cotangent, w_down)
        square = gate * gate
        bend = jnp.tanh(gate * (root + (root * 0.044715) * square))
        half = 0.5 + 0.5 * bend
        gelu = gate * half
        slope = half + (0.5 * gate) * (1.0 - bend * bend) * (root + (3 * root * 0.044715) * square)
        hidden = (gelu * up).astype(LOW)
        d_gate = (d_hidden * up * slope).astype(LOW)
        d_up = (d_hidden * gelu).astype(LOW)
        hidden_ref[:, part * columns : (part + 1) * columns] = hidden
        dgu_ref[:, part * columns : (part + 1) * columns] = d_gate
        dgu_ref[:, (2 + part) * columns : (3 + part) * columns] = d_up
        d_normed = d_normed + matmul_nt(d_gate, w_gate) + matmul_nt(d_up, w_up)
        out = out + matmul_nt(hidden, w_down)
    dn_ref[...] = d_normed.astype(LOW)

    @pl.when(step < pl.num_programs(0) // 2)
    def _():
        send_ref[...] = out.astype(LOW)

    @pl.when(step >= pl.num_programs(0) // 2)
    def _():
        own_ref[...] = attended + out


def grads_body(
    first_count, axis, place_ref, left0_ref, left1_ref, right0_ref, right1_ref, own_ref, other_ref, all_ref
):
    step = pl.program_id(0)

    def product(left_ref, right_ref):
        grads = matmul_nn(left_ref[...], right_ref[...]).astype(LOW)
        all_ref[...] = grads.reshape(all_ref.shape)

    pl.when(step < first_count)(functools.partial(product, left0_ref, right0_ref))
    pl.when(step >= first_count)(functools.partial(product, left1_ref, right1_ref))
    bit = place_ref[axis - 1]
    if axis == 1:
        own_ref[...] = all_ref[:, bit]
        other_ref[...] = all_ref[:, 1 - bit]
    else:
        own_ref[...] = all_ref[:, :, bit]
        other_ref[...] = all_ref[:, :, 1 - bit]


def turn_body(
    place_ref,
    x_ref,
    p_ref,
    r_ref,
    g_ref,
    a_ref,
    b_ref,
    gain_ref,
    wo_ref,
    datt_ref,
    turned_ref,
    dmix_ref,
    dgain_ref,
):
    step = pl.program_id(0)
    attended = x_ref[...].astype(HIGH) + (p_ref[...].astype(HIGH) + r_ref[...].astype(HIGH))
    unit, scale = rms_parts(attended)
    d_normed = a_ref[...].astype(HIGH) + b_ref[...].astype(HIGH)
    d_gain = jnp.sum(d_normed * unit, axis=0, keepdims=True)
    d_attended = g_ref[...].astype(HIGH) + rms_back(d_normed, unit, scale, gain_ref[...])
    d_low = d_attended.astype(LOW)
    turned_ref[...] = d_low.T
    dmix_ref[...] = matmul_nn(d_low, wo_ref[...]).astype(LOW)

    @pl.when(step == 0)
    def _():
        dgain_ref[...] = d_gain

    @pl.when(step != 0)
    def _():
        dgain_ref[...] += d_gain

    @pl.when(step >= pl.num_programs(0) // 2)
    def _():
        datt_ref[...] = d_attended


def backward_body(
    q_ref,
    k_ref,
    v_ref,
    e_ref,
    dmix_ref,
    mixed_ref,
    inv_ref,
    dq_ref,
    dk_ref,
    dv_ref,
    strip_ref,
    table_ref,
    dkt_ref,
    dvt_ref,
):
    seq_len = k_ref.shape[0]
    rows = table_ref.shape[1]
    low_masks = head_masks(LOW)
    masks = head_masks(HIGH)
    keys = k_ref[...]
    values = v_ref[...]
    keys_h = tuple(keys * low_masks[h] for h in range(2))
    table_ref[...] = jnp.zeros_like(table_ref)
    for block in range(seq_len // rows):
        at = slice(block * rows, (block + 1) * rows)
        queries = q_ref[at, :]
        scaled = (dmix_ref[at, :].astype(HIGH) * inv_ref[at, :]).astype(LOW)
        product = scaled.astype(HIGH) * mixed_ref[at, :]
        d_query = jnp.zeros((rows, LANES), HIGH)
        d_key = jnp.zeros((LANES, seq_len), HIGH)
        d_value = jnp.zeros((LANES, seq_len), HIGH)
        for head in range(2):
            scaled_h = scaled * low_masks[head]
            delta = jnp.sum(product * masks[head], axis=-1, keepdims=True)
            weights = e_ref[head, at, :]
            d_scores = weights.astype(HIGH) * (matmul_nt(scaled_h, values) - delta)
            d_low = d_scores.astype(LOW)
            window = slice(seq_len - block * rows, 2 * seq_len - block * rows)
            table_ref[head, :, window] += d_scores
            d_query = d_query + matmul_nn(d_low, keys_h[head])
            d_key = d_key + matmul_tn(queries * low_masks[head], d_low)
            d_value = d_value + matmul_tn(scaled_h, weights)
        dq_ref[at, :] = d_query.astype(LOW)
        if block == 0:
            dkt_ref[...] = d_key
            dvt_ref[...] = d_value
        else:
            dkt_ref[...] += d_key
            dvt_ref[...] += d_value
    dk_ref[...] = dkt_ref[...].T.astype(LOW)
    dv_ref[...] = dvt_ref[...].T.astype(LOW)
    width = 2 * seq_len
    sub = lax.broadcasted_iota(jnp.int32, (8, 1), 0)
    for head in range(2):
        total = table_ref[head, 0:8, :]
        for group in range(1, rows // 8):
            part = table_ref[head, 8 * group : 8 * group + 8, :]
            total = total + pltpu.roll(part, width - 8 * group, 1)
        for bit in (1, 2, 4):
            total = jnp.where((sub & bit) != 0, pltpu.roll(total, width - bit, 1), total)
        strip_ref[0, head : head + 1, :] = jnp.sum(total, axis=0, keepdims=True)


def spread_body(
    place_ref, x_ref, dq_ref, dk_ref, dv_ref, qkv_ref, send_ref, own_ref, dgain_ref
):
    step = pl.program_id(0)
    width = dq_ref.shape[1]
    unit, _ = rms_parts(x_ref[...].astype(HIGH))
    d_normed = (
        matmul_nt(dq_ref[...], qkv_ref[:, :width])
        + matmul_nt(dk_ref[...], qkv_ref[:, width : 2 * width])
        + matmul_nt(dv_ref[...], qkv_ref[:, 2 * width :])
    )
    d_gain = jnp.sum(d_normed * unit, axis=0, keepdims=True)

    @pl.when(step == 0)
    def _():
        dgain_ref[...] = d_gain

    @pl.when(step != 0)
    def _():
        dgain_ref[...] += d_gain

    @pl.when(step < pl.num_programs(0) // 2)
    def _():
        send_ref[...] = d_normed.astype(LOW)

    @pl.when(step >= pl.num_programs(0) // 2)
    def _():
        own_ref[...] = d_normed


def finish_body(x_ref, own_ref, other_ref, datt_ref, gain_ref, out_ref):
    unit, scale = rms_parts(x_ref[...].astype(HIGH))
    d_normed = own_ref[...] + other_ref[...].astype(HIGH)
    out_ref[...] = (datt_ref[...] + rms_back(d_normed, unit, scale, gain_ref[...])).astype(LOW)


def weight_grads(place, first, second, columns, axis, micros):
    left0, right0, at0, count0 = first
    left1, right1, at1, count1 = second
    height, depth = left0.shape
    steps = count0 + count1
    count = lax.axis_size("dp")
    block = (count // 4, 2, 2, height // count, columns)
    half = (block[0],) + block[2:]
    total = half[:-1] + (steps * columns,)
    half_spec = pl.BlockSpec(half, lambda i, *_: (0, 0, 0, i))
    return call(
        functools.partial(grads_body, count0, axis),
        (steps,),
        [
            whole((height, depth)),
            whole((height, depth)),
            pl.BlockSpec((depth, columns), lambda i, *_: (0, at0 + jnp.minimum(i, count0 - 1))),
            pl.BlockSpec((depth, columns), lambda i, *_: (0, at1 + jnp.maximum(i - count0, 0))),
        ],
        [half_spec, half_spec],
        [shaped(total, LOW), shaped(total, LOW)],
        [pltpu.VMEM(block, LOW)],
        prefetch=1,
        micros=micros,
    )(place, left0, left1, right0, right1)


def on_core_pair(
    tokens,
    cotangent,
    gain_attn,
    w_query,
    w_key,
    w_value,
    w_out,
    rel_table,
    buckets,
    gain_ffn,
    w_gate,
    w_up,
    w_down,
):
    own_rows, features = tokens.shape
    seq_len = 2 * own_rows
    width = w_query.shape[1]
    units = w_gate.shape[1]
    chunk = units // 2
    pairs = width // LANES
    bucket_count, head_count = rel_table.shape
    local_heads = head_count // 2
    count = lax.axis_size("dp")
    far_bit, y_bit, x_bit = dp_place()
    me = lax.axis_index("mp")
    place = jnp.stack([y_bit, x_bit, me, far_bit]).astype(jnp.int32)
    rows = MXU_ROWS
    steps = seq_len // rows
    half_steps = steps // 2
    block_rows = w_query.shape[0]

    def swapped(array):
        return lax.ppermute(array, "mp", [(0, 1), (1, 0)])

    def in_order(array, other):
        first = jnp.where(me == 0, array, other)
        second = jnp.where(me == 0, other, array)
        return jnp.concatenate([first, second], axis=0)

    early = jnp.concatenate([w_query, w_key, w_value, w_out.T], axis=1)
    late = jnp.concatenate([w_gate, w_up, w_down.T], axis=1)
    early_pieces = far_pieces(early)
    x_other, g_other = swapped(tokens), swapped(cotangent)
    *early_pieces, late = together(*early_pieces, late)
    near = far_stack(early, early_pieces)
    late_pieces = far_pieces(late)
    qk = near[:, :, : 2 * width]
    vo = near[:, :, 2 * width :]
    qk_next, vo_next = together(over_y(qk), over_x(vo))
    qk_own = in_bit_order(qk, qk_next, y_bit, 1)
    vo_own = in_bit_order(vo, vo_next, x_bit, 1)
    qk_other = over_x(qk_own)
    vo_other = over_y(vo_own)
    x_all = in_order(tokens, x_other)
    g_all = in_order(cotangent, g_other)
    qk_other, vo_other, x_all, g_all, *late_pieces = together(
        qk_other, vo_other, x_all, g_all, *late_pieces
    )
    near = far_stack(late, late_pieces)
    gu = near[:, :, : 3 * chunk]
    ud = near[:, :, 3 * chunk :]
    gu_next = over_y(gu)
    ud_next = over_x(ud)

    gain_a = gain_attn.reshape(1, features)
    gain_f = gain_ffn.reshape(1, features)

    one_hot = (buckets[:, None] == jnp.arange(bucket_count, dtype=jnp.int32)[None, :]).astype(HIGH)
    one_hot = jnp.pad(one_hot, ((1, 0), (0, 0)))
    my_table = lax.dynamic_slice_in_dim(rel_table, me * local_heads, local_heads, 1)
    strip = lax.dot_general(my_table, one_hot, (((0,), (1,)), ((), ())), precision=precise)
    strip = strip.reshape(pairs, 2, 2 * seq_len)

    def row_block(columns):
        return pl.BlockSpec((rows, columns), lambda i, *_: (i, 0))

    turned_block = pl.BlockSpec((features, rows), lambda i, *_: (0, i))
    full_block = (count // 4, 2, 2, block_rows, 2 * width)
    half_block = (count // 4, 2, block_rows, 2 * width)
    normed_turned, queries, keys, values, w_qkv, w_o = call(
        project_body,
        (steps,),
        [row_block(features), whole((1, features))] + [whole(half_block)] * 4,
        [turned_block]
        + [row_block(width)] * 3
        + [result((features, 3 * width)), result((features, width))],
        [shaped((features, seq_len), LOW)]
        + [shaped((seq_len, width), LOW)] * 3
        + [shaped((features, 3 * width), LOW), shaped((features, width), LOW)],
        [pltpu.VMEM(full_block, LOW), pltpu.VMEM(full_block, LOW)],
        prefetch=1,
        micros=7,
    )(place, x_all, gain_a, qk_own, qk_other, vo_own, vo_other)

    gu_next, ud_next, queries = together(gu_next, ud_next, queries)
    gu_own = in_bit_order(gu, gu_next, y_bit, 1)
    ud_own = in_bit_order(ud, ud_next, x_bit, 1)
    gu_other = over_x(gu_own)
    ud_other = over_y(ud_own)

    pair_block = pl.BlockSpec((seq_len, LANES), lambda p: (0, p))
    e_block = pl.BlockSpec((2, seq_len, seq_len), lambda p: (p, 0, 0))
    strip_block = pl.BlockSpec((1, 2, 2 * seq_len), lambda p: (p, 0, 0))
    table_scratch = pltpu.VMEM((2, rows, 2 * seq_len), HIGH)
    weights_e, mixed, mixed_low, inverse, part = call(
        attend_body,
        (pairs,),
        [
            pair_block,
            pair_block,
            pair_block,
            strip_block,
            pl.BlockSpec((features, LANES), lambda p: (0, p)),
        ],
        [e_block, pair_block, pair_block, pair_block, result((seq_len, features))],
        [
            shaped((2 * pairs, seq_len, seq_len), LOW),
            shaped((seq_len, width), HIGH),
            shaped((seq_len, width), LOW),
            shaped((seq_len, width), HIGH),
            shaped((seq_len, features), LOW),
        ],
        [table_scratch, pltpu.VMEM((seq_len, features), HIGH)],
        micros=20,
    )(queries, keys, values, strip, w_o)
    gu_other, ud_other, part = together(gu_other, ud_other, part)
    part_other = swapped(part)

    def moved(i, m):
        return (i + half_steps * (1 - m[2])) % steps

    def turned_row(columns):
        return pl.BlockSpec((rows, columns), lambda i, m: (moved(i, m), 0))

    moved_block = pl.BlockSpec((features, rows), lambda i, m: (0, moved(i, m)))
    send_row = pl.BlockSpec((rows, features), lambda i, m: (jnp.minimum(i, half_steps - 1), 0))
    keep_row = pl.BlockSpec((rows, features), lambda i, m: (jnp.maximum(i - half_steps, 0), 0))
    full_block = (count // 4, 2, 2, block_rows, 3 * chunk)
    half_block = (count // 4, 2, block_rows, 3 * chunk)
    normed_f_turned, g_turned, hidden, d_gate_up, dn_part, out_send, out_own = call(
        feed_body,
        (steps,),
        [turned_row(features)] * 4 + [whole((1, features))] + [whole(half_block)] * 4,
        [
            moved_block,
            moved_block,
            turned_row(units),
            turned_row(2 * units),
            turned_row(features),
            send_row,
            keep_row,
        ],
        [
            shaped((features, seq_len), LOW),
            shaped((features, seq_len), LOW),
            shaped((seq_len, units), LOW),
            shaped((seq_len, 2 * units), LOW),
            shaped((seq_len, features), LOW),
            shaped((own_rows, features), LOW),
            shaped((own_rows, features), HIGH),
        ],
        [pltpu.VMEM(full_block, LOW), pltpu.VMEM(full_block, LOW)],
        prefetch=1,
        micros=19,
    )(place, x_all, part, part_other, g_all, gain_f, gu_own, gu_other, ud_own, ud_other)
    dn_other = swapped(dn_part)

    gu_own, gu_send = weight_grads(
        place, (normed_f_turned, d_gate_up, 0, 2), (normed_f_turned, d_gate_up, 2, 1), chunk, 2, 6
    )
    gu_send, hidden, dn_other = together(gu_send, hidden, dn_other)
    gu_came = over_x(gu_send)
    ud_own, ud_send = weight_grads(
        place, (normed_f_turned, d_gate_up, 3, 1), (g_turned, hidden, 0, 2), chunk, 1, 6
    )
    ud_send, dn_other = together(ud_send, dn_other)
    ud_came = over_y(ud_send)

    d_attended, d_low_turned, d_mixed, d_gain_f = call(
        turn_body,
        (steps,),
        [turned_row(features)] * 6 + [whole((1, features)), whole((features, width))],
        [keep_row, moved_block, turned_row(width), result((1, features))],
        [
            shaped((own_rows, features), HIGH),
            shaped((features, seq_len), LOW),
            shaped((seq_len, width), LOW),
            shaped((1, features), HIGH),
        ],
        prefetch=1,
        micros=8,
    )(place, x_all, part, part_other, g_all, dn_part, dn_other, gain_f, w_o)
    out_other = swapped(out_send)

    d_query, d_key, d_value, d_strip = call(
        backward_body,
        (pairs,),
        [pair_block, pair_block, pair_block, e_block, pair_block, pair_block, pair_block],
        [pair_block, pair_block, pair_block, strip_block],
        [shaped((seq_len, width), LOW)] * 3 + [shaped((pairs, 2, 2 * seq_len), HIGH)],
        [table_scratch, pltpu.VMEM((LANES, seq_len), HIGH), pltpu.VMEM((LANES, seq_len), HIGH)],
        micros=16,
    )(queries, keys, values, weights_e, d_mixed, mixed, inverse)

    gu_came, ud_came, out_other, d_query, d_key, d_value, d_strip = together(
        gu_came, ud_came, out_other, d_query, d_key, d_value, d_strip
    )

    def next_half(own, came, bit):
        return (
            add_low(at_bit(own, bit, 1), at_bit(came, bit, 1)),
            add_low(at_bit(own, 1 - bit, 1), at_bit(came, 1 - bit, 1)),
        )

    gu_own, gu_send = next_half(gu_own, gu_came, y_bit)
    ud_own, ud_send = next_half(ud_own, ud_came, x_bit)
    gu_came = over_y(gu_send)
    ud_came = over_x(ud_send)

    qk_own, qk_send = weight_grads(
        place, (normed_turned, d_query, 0, 1), (normed_turned, d_key, 0, 1), width, 2, 5
    )
    qk_send, d_value = together(qk_send, d_value)
    vo_own, vo_send = weight_grads(
        place, (normed_turned, d_value, 0, 1), (d_low_turned, mixed_low, 0, 1), width, 1, 5
    )
    output = (out_own + out_other.astype(HIGH)).astype(LOW)

    def far_sums(own, came):
        total = add_low(own, came)
        pieces = [over_far(at_bit(total, (far_bit + k) % (count // 4), 0), k) for k in range(1, count // 4)]
        return (at_bit(total, far_bit, 0), pieces)

    gu_came, ud_came, qk_send, vo_send, d_query = together(
        gu_came, ud_came, qk_send, vo_send, d_query
    )
    qk_came = over_x(qk_send)
    vo_came = over_y(vo_send)
    gu_kept, gu_pieces = far_sums(gu_own, gu_came)
    ud_kept, ud_pieces = far_sums(ud_own, ud_came)

    dna_send, dna_own, d_gain_a = call(
        spread_body,
        (steps,),
        [turned_row(features)] + [turned_row(width)] * 3 + [whole((features, 3 * width))],
        [send_row, keep_row, result((1, features))],
        [
            shaped((own_rows, features), LOW),
            shaped((own_rows, features), HIGH),
            shaped((1, features), HIGH),
        ],
        prefetch=1,
        micros=7,
    )(place, x_all, d_query, d_key, d_value, w_qkv)
    qk_came, vo_came, dna_send, d_gain_a, d_strip = together(
        qk_came, vo_came, dna_send, d_gain_a, d_strip
    )
    dna_other = swapped(dna_send)
    qk_own, qk_send = next_half(qk_own, qk_came, y_bit)
    vo_own, vo_send = next_half(vo_own, vo_came, x_bit)
    qk_came = over_y(qk_send)
    vo_came = over_x(vo_send)

    d_bias = d_strip.reshape(local_heads, 2 * seq_len)
    my_d_table = lax.dot_general(one_hot, d_bias, (((0,), (1,)), ((), ())), precision=precise)
    d_table = lax.dynamic_update_slice_in_dim(
        jnp.zeros_like(rel_table), my_d_table, me * local_heads, 1
    )
    small = jnp.concatenate(
        [d_gain_a.reshape(features), 0.5 * d_gain_f.reshape(features), d_table.reshape(-1)]
    )
    small = jnp.pad(small, (0, -small.shape[0] % 1024)).reshape(-1, LANES)
    small = sum_all(small).reshape(-1)

    d_tokens = call(
        finish_body,
        (half_steps,),
        [row_block(features)] * 4 + [whole((1, features))],
        row_block(features),
        shaped((own_rows, features), LOW),
        micros=3.5,
    )(tokens, dna_own, dna_other, d_attended, gain_a)

    qk_came, vo_came, d_tokens, *far_came = together(
        qk_came, vo_came, d_tokens, *gu_pieces, *ud_pieces
    )
    gu_pieces, ud_pieces = far_came[: len(gu_pieces)], far_came[len(gu_pieces) :]
    qk_kept, qk_pieces = far_sums(qk_own, qk_came)
    vo_kept, vo_pieces = far_sums(vo_own, vo_came)

    def summed(kept, pieces):
        return sum((piece.astype(HIGH) for piece in pieces), kept.astype(HIGH))

    grads_gu, grads_ud = summed(gu_kept, gu_pieces), summed(ud_kept, ud_pieces)
    grads_qk, grads_vo = summed(qk_kept, qk_pieces), summed(vo_kept, vo_pieces)
    return (
        output,
        d_tokens,
        small[:features],
        grads_qk[:, :width],
        grads_qk[:, width:],
        grads_vo[:, :width],
        grads_vo[:, width:].T,
        small[2 * features : 2 * features + rel_table.size].reshape(rel_table.shape),
        small[features : 2 * features],
        grads_gu[:, :units],
        jnp.concatenate([grads_gu[:, units:], grads_ud[:, :chunk]], axis=1),
        grads_ud[:, chunk:].T,
    )


def solution(mesh):
    placed = (
        P(("dp", "mp"), None),
        P(("dp", "mp"), None),
        P(),
        P("dp", "mp"),
        P("dp", "mp"),
        P("dp", "mp"),
        P("mp", "dp"),
        P(),
        P(),
        P(),
        P("dp", "mp"),
        P("dp", "mp"),
        P("mp", "dp"),
    )
    paired = mesh.shape["mp"] == 2 and mesh.shape["dp"] % 4 == 0
    body = on_core_pair if paired else on_device
    return jax.shard_map(
        body,
        mesh=mesh,
        in_specs=placed,
        out_specs=(
            P(("dp", "mp"), None),
            P(("dp", "mp"), None),
            P(),
            P("dp", "mp"),
            P("dp", "mp"),
            P("dp", "mp"),
            P("mp", "dp"),
            P(),
            P(),
            P("dp", "mp"),
            P("dp", "mp"),
            P("mp", "dp"),
        ),
        check_vma=False,
    )
```

```python
import functools

import jax
import jax.numpy as jnp
from jax import lax
from jax.experimental import pallas as pl
from jax.experimental.pallas import tpu as pltpu
from jax.sharding import PartitionSpec as P

epsilon = 1e-06
block_limit = 512
precise = lax.Precision.HIGHEST


def as_sent(array):

    def short(part):
        return part.astype(jnp.bfloat16) if part.dtype == jnp.float32 else part

    return jax.tree.map(short, array)


def matmul_nn(left, right):
    return jnp.dot(left, right, preferred_element_type=jnp.float32)


def matmul_nt(left, right):
    return lax.dot_general(
        left, right, (((1,), (1,)), ((), ())), preferred_element_type=jnp.float32
    )


def matmul_tn(left, right):
    return lax.dot_general(
        left, right, (((0,), (0,)), ((), ())), preferred_element_type=jnp.float32
    )


def rms_parts(inputs):
    scale = lax.rsqrt(jnp.mean(inputs * inputs, axis=-1, keepdims=True) + epsilon)
    return (inputs * scale, scale)


def rms_back(d_normed, unit, scale, gain):
    d_unit = d_normed * gain
    return scale * (d_unit - unit * jnp.mean(d_unit * unit, axis=-1, keepdims=True))


def gated(gate_pre, up_pre):
    return jax.nn.gelu(gate_pre, approximate=True) * up_pre


def window_base(first_query, first_key, row_count, seq_len):
    return first_key - first_query - row_count + seq_len


def make_bias(bias_full, base, row_count, width):
    span = width + row_count - 1
    head_count = bias_full.shape[0]
    strip = lax.dynamic_slice_in_dim(bias_full, base, span, 1)
    tiled = jnp.tile(strip, (1, row_count + 1))
    window = tiled[:, row_count - 1 : row_count - 1 + row_count * (span - 1)]
    return window.reshape(head_count, row_count, span - 1)[:, :, :width]


def skew_sum(d_block, row_count, width):
    head_count = d_block.shape[0]
    span = width + row_count - 1
    padded = jnp.pad(d_block, ((0, 0), (0, 0), (row_count - 1, 0)))
    flat = padded.reshape(head_count, row_count * span)
    flat = jnp.pad(flat, ((0, 0), (0, row_count)))
    skewed = flat.reshape(head_count, row_count, span + 1)[:, :, :span]
    return jnp.sum(skewed, axis=1)


def add_window(d_bias, piece, base):
    current = lax.dynamic_slice_in_dim(d_bias, base, piece.shape[1], 1)
    return lax.dynamic_update_slice_in_dim(d_bias, current + piece, base, 1)


def sum_rows(partial_value):
    return lax.psum_scatter(
        partial_value.astype(jnp.bfloat16), "mp", scatter_dimension=0, tiled=True
    ).astype(jnp.float32)


def split_heads(queries, keys_all, values, head_count):
    row_count = queries.shape[0]
    seq_len = keys_all.shape[0]
    head_dim = queries.shape[1] // head_count
    width = min(block_limit, seq_len)
    blocks = seq_len // width
    heads_q = queries.reshape(row_count, head_count, head_dim)
    heads_k = keys_all.reshape(blocks, width, head_count, head_dim)
    heads_v = values.reshape(blocks, width, head_count, head_dim)
    starts = jnp.arange(blocks, dtype=jnp.int32) * width
    return (heads_q, heads_k, heads_v, starts, width)


def attend_forward(queries, keys_all, values, bias_full, head_count, first_row):
    row_count = queries.shape[0]
    seq_len = keys_all.shape[0]
    heads_q, heads_k, heads_v, starts, width = split_heads(queries, keys_all, values, head_count)

    def block_scores(key_block, first_key):
        raw_scores = jnp.einsum(
            "qhd,khd->hqk", heads_q, key_block, preferred_element_type=jnp.float32
        )
        base = window_base(first_row, first_key, row_count, seq_len)
        return raw_scores + make_bias(bias_full, base, row_count, width)

    def stats_step(running, pieces):
        top_now, total = running
        scores = block_scores(pieces[0], pieces[1])
        top_new = jnp.maximum(top_now, jnp.max(scores, axis=-1))
        total = total * jnp.exp(top_now - top_new) + jnp.sum(
            jnp.exp(scores - top_new[..., None]), axis=-1
        )
        return ((top_new, total), None)

    start_top = jnp.full((head_count, row_count), -jnp.inf, jnp.float32)
    start_total = jnp.zeros((head_count, row_count), jnp.float32)
    (top_all, total), _ = lax.scan(stats_step, (start_top, start_total), (heads_k, starts))
    log_total = top_all + jnp.log(total)

    def mix_step(running, pieces):
        scores = block_scores(pieces[0], pieces[2])
        probs_low = jnp.exp(scores - log_total[..., None]).astype(jnp.bfloat16)
        update = jnp.einsum(
            "hqk,khd->qhd", probs_low, pieces[1], preferred_element_type=jnp.float32
        )
        return (running + update, None)

    start_mix = jnp.zeros(heads_q.shape, jnp.float32)
    mixed_f, _ = lax.scan(mix_step, start_mix, (heads_k, heads_v, starts))
    return (mixed_f.reshape(row_count, queries.shape[1]), log_total)


def attend_backward(
    queries, keys_all, values, bias_full, head_count, first_row, log_total, deltas, d_mixed
):
    row_count = queries.shape[0]
    seq_len = keys_all.shape[0]
    heads_q, heads_k, heads_v, starts, width = split_heads(queries, keys_all, values, head_count)
    heads_d = d_mixed.reshape(heads_q.shape)

    def back_step(running, pieces):
        d_query, d_bias = running
        key_block, value_block, first_key = pieces
        base = window_base(first_row, first_key, row_count, seq_len)
        scores = jnp.einsum("qhd,khd->hqk", heads_q, key_block, preferred_element_type=jnp.float32)
        scores = scores + make_bias(bias_full, base, row_count, width)
        probs = jnp.exp(scores - log_total[..., None])
        d_probs = jnp.einsum(
            "qhd,khd->hqk", heads_d, value_block, preferred_element_type=jnp.float32
        )
        d_scores = (probs * (d_probs - deltas[..., None])).astype(jnp.bfloat16)
        d_query = d_query + jnp.einsum(
            "hqk,khd->qhd", d_scores, key_block, preferred_element_type=jnp.float32
        )
        d_bias = add_window(d_bias, skew_sum(d_scores.astype(jnp.float32), row_count, width), base)
        probs_low = probs.astype(jnp.bfloat16)
        d_value = jnp.einsum("hqk,qhd->khd", probs_low, heads_d, preferred_element_type=jnp.float32)
        d_key = jnp.einsum("hqk,qhd->khd", d_scores, heads_q, preferred_element_type=jnp.float32)
        return ((d_query, d_bias), (d_key, d_value))

    start_query = jnp.zeros(heads_q.shape, jnp.float32)
    (d_query, d_bias), kv_parts = lax.scan(
        back_step, (start_query, jnp.zeros_like(bias_full)), (heads_k, heads_v, starts)
    )
    feature_count = queries.shape[1]
    d_query = d_query.reshape(row_count, feature_count)
    return (
        d_query,
        d_bias,
        kv_parts[0].reshape(seq_len, feature_count),
        kv_parts[1].reshape(seq_len, feature_count),
    )


def on_device(
    tokens,
    cotangent,
    gain_attn,
    w_query,
    w_key,
    w_value,
    w_out,
    rel_table,
    buckets,
    gain_ffn,
    w_gate,
    w_up,
    w_down,
):
    head_count = rel_table.shape[1]
    bucket_count = rel_table.shape[0]
    inputs = tokens.astype(jnp.float32)
    row_count = inputs.shape[0]
    feature_count = inputs.shape[1]
    first_row = lax.axis_index("mp") * row_count
    attn_parts = (w_query, w_key, w_value, w_out.T)
    ffn_parts = (w_gate, w_up, w_down.T)
    ffn_cols = ()
    col_parts = lax.all_gather(as_sent(attn_parts + ffn_cols), "mp", axis=1, tiled=True)
    full_parts = lax.all_gather(as_sent(tuple(col_parts) + ffn_parts), "dp", axis=0, tiled=True)
    query_full, key_full, value_full, out_full, gate_full, up_full, down_full = full_parts
    unit_a, scale_a = rms_parts(inputs)
    normed_a = (unit_a * gain_attn).astype(jnp.bfloat16)
    queries = matmul_nn(normed_a, query_full).astype(jnp.bfloat16)
    own_keys = matmul_nn(normed_a, key_full).astype(jnp.bfloat16)
    own_values = matmul_nn(normed_a, value_full).astype(jnp.bfloat16)
    keys_all, values = (
        lax.all_gather(own_keys, "mp", axis=0, tiled=True),
        lax.all_gather(own_values, "mp", axis=0, tiled=True),
    )
    one_hot = (buckets[:, None] == jnp.arange(bucket_count, dtype=jnp.int32)[None, :]).astype(
        jnp.float32
    )
    bias_full = jnp.dot(one_hot, rel_table, precision=precise).T
    mixed_f, log_total = attend_forward(queries, keys_all, values, bias_full, head_count, first_row)
    mixed_out = mixed_f.astype(jnp.bfloat16)
    attended = inputs + matmul_nt(mixed_out, out_full)
    unit_f, scale_f = rms_parts(attended)
    normed_f = (unit_f * gain_ffn).astype(jnp.bfloat16)
    normed_seq, cot_seq = (
        lax.all_gather(normed_f, "mp", axis=0, tiled=True),
        lax.all_gather(cotangent, "mp", axis=0, tiled=True),
    )
    gate_pre = matmul_nn(normed_seq, gate_full)
    up_pre = matmul_nn(normed_seq, up_full)
    hidden = gated(gate_pre, up_pre).astype(jnp.bfloat16)
    output = attended + sum_rows(matmul_nt(hidden, down_full))
    d_hidden = matmul_nn(cot_seq, down_full)
    d_down = matmul_tn(cot_seq, hidden)
    _, pull_gate = jax.vjp(gated, gate_pre, up_pre)
    d_gate, d_up = pull_gate(d_hidden)
    d_gate = d_gate.astype(jnp.bfloat16)
    d_up = d_up.astype(jnp.bfloat16)
    d_normed_f = sum_rows(matmul_nt(d_gate, gate_full) + matmul_nt(d_up, up_full))
    d_gate_w = matmul_tn(normed_seq, d_gate)
    d_up_w = matmul_tn(normed_seq, d_up)
    d_gain_f = jnp.sum(d_normed_f * unit_f, axis=0)
    d_attended = cotangent.astype(jnp.float32) + rms_back(d_normed_f, unit_f, scale_f, gain_ffn)
    d_att_low = d_attended.astype(jnp.bfloat16)
    d_out_w = matmul_tn(d_att_low, mixed_out)
    d_mixed = matmul_nn(d_att_low, out_full).astype(jnp.bfloat16)
    head_dim = feature_count // head_count
    deltas = jnp.sum(
        (d_mixed.astype(jnp.float32) * mixed_f).reshape(row_count, head_count, head_dim), axis=-1
    ).T
    d_query, d_bias, d_keys_part, d_values_part = attend_backward(
        queries, keys_all, values, bias_full, head_count, first_row, log_total, deltas, d_mixed
    )
    d_keys_own, d_values_own = (
        lax.psum_scatter(
            d_keys_part.astype(jnp.bfloat16), "mp", scatter_dimension=0, tiled=True
        ).astype(jnp.float32),
        lax.psum_scatter(
            d_values_part.astype(jnp.bfloat16), "mp", scatter_dimension=0, tiled=True
        ).astype(jnp.float32),
    )
    d_keys_own = d_keys_own.astype(jnp.bfloat16)
    d_values_own = d_values_own.astype(jnp.bfloat16)
    d_query = d_query.astype(jnp.bfloat16)
    d_normed_a = (
        matmul_nt(d_query, query_full)
        + matmul_nt(d_keys_own, key_full)
        + matmul_nt(d_values_own, value_full)
    )
    d_query_w = matmul_tn(normed_a, d_query)
    d_key_w = matmul_tn(normed_a, d_keys_own)
    d_value_w = matmul_tn(normed_a, d_values_own)
    d_gain_a = jnp.sum(d_normed_a * unit_a, axis=0)
    d_tokens = (d_attended + rms_back(d_normed_a, unit_a, scale_a, gain_attn)).astype(jnp.bfloat16)
    d_table = jnp.dot(d_bias, one_hot, precision=precise).T
    row_grads = (
        lax.psum_scatter(
            d_query_w.astype(jnp.bfloat16), "dp", scatter_dimension=0, tiled=True
        ).astype(jnp.float32),
        lax.psum_scatter(
            d_key_w.astype(jnp.bfloat16), "dp", scatter_dimension=0, tiled=True
        ).astype(jnp.float32),
        lax.psum_scatter(
            d_value_w.astype(jnp.bfloat16), "dp", scatter_dimension=0, tiled=True
        ).astype(jnp.float32),
        lax.psum_scatter(
            d_out_w.astype(jnp.bfloat16), "dp", scatter_dimension=0, tiled=True
        ).astype(jnp.float32),
        lax.psum_scatter(
            d_gate_w.astype(jnp.bfloat16), "dp", scatter_dimension=0, tiled=True
        ).astype(jnp.float32),
        lax.psum_scatter(d_up_w.astype(jnp.bfloat16), "dp", scatter_dimension=0, tiled=True).astype(
            jnp.float32
        ),
        lax.psum_scatter(d_down.astype(jnp.bfloat16), "dp", scatter_dimension=0, tiled=True).astype(
            jnp.float32
        ),
    )
    row_grads = tuple(row_grads)
    ffn_late = ()
    col_grads = tuple(
        jax.tree.map(
            lambda part: part.astype(jnp.float32),
            lax.psum_scatter(
                as_sent(row_grads[:4] + ffn_late), "mp", scatter_dimension=1, tiled=True
            ),
        )
    )
    ffn_done = row_grads[4:]
    small_sums = lax.psum((d_gain_a, d_gain_f, d_table), ("dp", "mp"))
    return (
        output.astype(jnp.bfloat16),
        d_tokens,
        small_sums[0],
        col_grads[0],
        col_grads[1],
        col_grads[2],
        col_grads[3].T,
        small_sums[2],
        small_sums[1],
        ffn_done[0],
        ffn_done[1],
        ffn_done[2].T,
    )


MXU_ROWS = 256
LANES = 128
VMEM_LIMIT = 56 * 2**20
PEAK_PER_MICRO = 1_153_500_000
LOW = jnp.bfloat16
HIGH = jnp.float32


def call(
    body, grid, in_specs, out_specs, out_shape, scratch=(), prefetch=0, micros=5, aliases=None
):
    return pl.pallas_call(
        body,
        grid_spec=pltpu.PrefetchScalarGridSpec(
            num_scalar_prefetch=prefetch,
            grid=grid,
            in_specs=in_specs,
            out_specs=out_specs,
            scratch_shapes=list(scratch),
        ),
        out_shape=out_shape,
        input_output_aliases=aliases or {},
        compiler_params=pltpu.CompilerParams(vmem_limit_bytes=VMEM_LIMIT),
        cost_estimate=pl.CostEstimate(
            flops=int(micros * PEAK_PER_MICRO), bytes_accessed=0, transcendentals=0
        ),
    )


def shaped(shape, dtype):
    return jax.ShapeDtypeStruct(shape, dtype)


def whole(shape):
    return pl.BlockSpec(shape, lambda *_: (0,) * len(shape), pipeline_mode=pl.Buffered(1))


def result(shape):
    return pl.BlockSpec(shape, lambda *_: (0,) * len(shape))


def together(*arrays):
    return lax.optimization_barrier(arrays)


def ring_shift(steps, count):
    return [(i, (i + steps) % count) for i in range(count)]


def flip(bit, count):
    return [(i, i ^ bit) for i in range(count)]


def over_x(array):
    return lax.ppermute(array, "dp", flip(1, lax.axis_size("dp")))


def over_y(array):
    return lax.ppermute(array, "dp", flip(2, lax.axis_size("dp")))


def over_far(array, steps):
    return lax.ppermute(array, "dp", ring_shift(4 * steps, lax.axis_size("dp")))


def dp_place():
    index = lax.axis_index("dp")
    return (index // 4, (index // 2) % 2, index % 2)


def in_bit_order(own, other, bit):
    first = jnp.where(bit == 0, own, other)
    second = jnp.where(bit == 0, other, own)
    return jnp.concatenate([first, second], axis=0)


def far_pieces(shard):
    return [over_far(shard, k) for k in range(1, lax.axis_size("dp") // 4)]


def far_stack(shard, pieces):
    far = len(pieces) + 1
    place = dp_place()[0]
    stacked = jnp.zeros((far,) + shard.shape, shard.dtype)
    for k, piece in enumerate([shard] + pieces):
        stacked = lax.dynamic_update_slice(stacked, piece[None], ((place - k) % far, 0, 0))
    return stacked.reshape(-1, shard.shape[1])


def over_far_bit(array, bit):
    return lax.ppermute(array, "dp", flip(4 << bit, lax.axis_size("dp")))


def part_of(array, index, parts):
    size = array.shape[0] // parts
    return lax.dynamic_slice_in_dim(array, index * size, size, 0)


def add_low(left, right):
    return (left.astype(HIGH) + right.astype(HIGH)).astype(LOW)


def head_masks(dtype):
    lane = lax.broadcasted_iota(jnp.int32, (1, LANES), 1)
    first = (lane < LANES // 2).astype(HIGH)
    return (first.astype(dtype), (1.0 - first).astype(dtype))


def put_weights(full_ref, own_ref, other_ref, y_first, bit):
    far, rows = full_ref.shape[0], full_ref.shape[3]
    for half_ref, at in ((own_ref, bit), (other_ref, 1 - bit)):
        for near in range(2):
            for place in range(far):
                start = (near * far + place) * rows
                block = half_ref[start : start + rows, :]
                if y_first:
                    full_ref[place, near, at] = block
                else:
                    full_ref[place, at, near] = block


def put_turned(turned_ref, array, x_first, bit):
    rows = turned_ref.shape[4]
    turned = array.T
    for block in range(turned.shape[0] // rows):
        far, y_bit, x_bit = block // 4, (block // 2) % 2, block % 2
        first, second = (x_bit, y_bit) if x_first else (y_bit, x_bit)
        other = 1 - bit if first else bit
        turned_ref[other, second, far % 2, far // 2] = turned[block * rows : (block + 1) * rows]


def matrix(full_ref, start, columns):
    part = full_ref[:, :, :, :, start : start + columns]
    return part.reshape(-1, columns)


def project_body(
    place_ref,
    x_ref,
    gain_ref,
    qk_own_ref,
    qk_other_ref,
    vo_own_ref,
    vo_other_ref,
    turned_x_ref,
    turned_y_ref,
    q_ref,
    k_ref,
    v_ref,
    qkv_ref,
    wo_ref,
    qk_ref,
    vo_ref,
):
    width = q_ref.shape[1]

    @pl.when(pl.program_id(0) == 0)
    def _():
        put_weights(qk_ref, qk_own_ref, qk_other_ref, True, place_ref[1])
        put_weights(vo_ref, vo_own_ref, vo_other_ref, False, place_ref[0])
        qkv_ref[:, : 2 * width] = matrix(qk_ref, 0, 2 * width)
        qkv_ref[:, 2 * width :] = matrix(vo_ref, 0, width)
        wo_ref[...] = matrix(vo_ref, width, width)

    unit, _ = rms_parts(x_ref[...].astype(HIGH))
    normed = (unit * gain_ref[...]).astype(LOW)
    put_turned(turned_x_ref, normed, True, place_ref[1])
    put_turned(turned_y_ref, normed, False, place_ref[0])
    q_ref[...] = matmul_nn(normed, qkv_ref[:, :width]).astype(LOW)
    k_ref[...] = matmul_nn(normed, qkv_ref[:, width : 2 * width]).astype(LOW)
    v_ref[...] = matmul_nn(normed, qkv_ref[:, 2 * width :]).astype(LOW)


def attend_body(
    q_ref, k_ref, v_ref, strip_ref, wo_ref, e_ref, mixed_ref, low_ref, inv_ref, part_ref, table_ref, acc_ref
):
    pair = pl.program_id(0)
    seq_len = k_ref.shape[0]
    rows = table_ref.shape[1]
    low_masks = head_masks(LOW)
    own_lanes = tuple(mask > 0.5 for mask in head_masks(HIGH))
    for head in range(2):
        row = jnp.broadcast_to(strip_ref[0, head : head + 1, :], (rows, 2 * seq_len))
        table_ref[head] = pltpu.roll(row, 0, 1, stride=1, stride_axis=0)
    keys = k_ref[...]
    values = v_ref[...]
    values_h = tuple(values * low_masks[h] + low_masks[1 - h] for h in range(2))

    @pl.when(pair == 0)
    def _():
        acc_ref[...] = jnp.zeros_like(acc_ref)

    def scored(block, head):
        at = slice(block * rows, (block + 1) * rows)
        raw = matmul_nt(q_ref[at, :] * low_masks[head], keys)
        return raw + table_ref[head, :, seq_len - block * rows : 2 * seq_len - block * rows]

    units = [(block, head) for block in range(seq_len // rows) for head in range(2)]
    ahead = scored(*units[0])
    summed = [None, None]
    for number, (block, head) in enumerate(units):
        at = slice(block * rows, (block + 1) * rows)
        scores = ahead
        if number + 1 < len(units):
            ahead = scored(*units[number + 1])
        top = jnp.max(scores, axis=-1, keepdims=True)
        weights = jnp.exp(scores - top).astype(LOW)
        e_ref[head, at, :] = weights
        summed[head] = matmul_nn(weights, values_h[head])
        if head == 1:
            totals = jnp.where(own_lanes[0], summed[1], summed[0])
            inverse = 1.0 / pltpu.roll(totals, LANES // 2, 1)
            mixed = jnp.where(own_lanes[0], summed[0], summed[1]) * inverse
            mixed_ref[at, :] = mixed
            low_ref[at, :] = mixed.astype(LOW)
            inv_ref[at, :] = inverse
    acc_ref[...] += matmul_nt(low_ref[...], wo_ref[...])

    @pl.when(pair == pl.num_programs(0) - 1)
    def _():
        part_ref[...] = acc_ref[...].astype(LOW)


def feed_body(
    place_ref,
    x_ref,
    p_ref,
    r_ref,
    g_ref,
    gain_ref,
    gu_own_ref,
    gu_other_ref,
    ud_own_ref,
    ud_other_ref,
    turned_x_ref,
    turned_y_ref,
    g_turned_ref,
    hidden_ref,
    dgu_ref,
    dn_ref,
    send_ref,
    own_ref,
    gu_ref,
    ud_ref,
):
    step = pl.program_id(0)

    @pl.when(step == 0)
    def _():
        put_weights(gu_ref, gu_own_ref, gu_other_ref, True, place_ref[1])
        put_weights(ud_ref, ud_own_ref, ud_other_ref, False, place_ref[0])

    attended = x_ref[...].astype(HIGH) + (p_ref[...].astype(HIGH) + r_ref[...].astype(HIGH))
    unit, _ = rms_parts(attended)
    normed = (unit * gain_ref[...]).astype(LOW)
    put_turned(turned_x_ref, normed, True, place_ref[1])
    put_turned(turned_y_ref, normed, False, place_ref[0])
    cotangent = g_ref[...]
    put_turned(g_turned_ref, cotangent, False, place_ref[0])
    root = 0.7978845608028654
    columns = hidden_ref.shape[1] // 2
    out = 0.0
    d_normed = 0.0
    for part in range(2):
        w_gate = matrix(gu_ref, part * columns, columns)
        w_up = matrix(ud_ref, 0, columns) if part else matrix(gu_ref, 2 * columns, columns)
        w_down = matrix(ud_ref, (1 + part) * columns, columns)
        gate = matmul_nn(normed, w_gate)
        up = matmul_nn(normed, w_up)
        d_hidden = matmul_nn(cotangent, w_down)
        square = gate * gate
        bend = jnp.tanh(gate * (root + (root * 0.044715) * square))
        half = 0.5 + 0.5 * bend
        gelu = gate * half
        slope = half + (0.5 * gate) * (1.0 - bend * bend) * (root + (3 * root * 0.044715) * square)
        hidden = (gelu * up).astype(LOW)
        d_gate = (d_hidden * up * slope).astype(LOW)
        d_up = (d_hidden * gelu).astype(LOW)
        hidden_ref[:, part * columns : (part + 1) * columns] = hidden
        dgu_ref[:, part * columns : (part + 1) * columns] = d_gate
        dgu_ref[:, (2 + part) * columns : (3 + part) * columns] = d_up
        d_normed = d_normed + matmul_nt(d_gate, w_gate) + matmul_nt(d_up, w_up)
        out = out + matmul_nt(hidden, w_down)
    dn_ref[...] = d_normed.astype(LOW)

    @pl.when(step < pl.num_programs(0) // 2)
    def _():
        send_ref[...] = out.astype(LOW)

    @pl.when(step >= pl.num_programs(0) // 2)
    def _():
        own_ref[...] = attended + out


def grads_body(first_count, left0_ref, left1_ref, right0_ref, right1_ref, own_ref, other_ref):
    step = pl.program_id(0)
    half = own_ref.shape[0]

    def product(left_ref, right_ref):
        right = right_ref[...]
        own_ref[...] = matmul_nn(left_ref[:half, :], right).astype(LOW)
        other_ref[...] = matmul_nn(left_ref[half:, :], right).astype(LOW)

    pl.when(step < first_count)(functools.partial(product, left0_ref, right0_ref))
    pl.when(step >= first_count)(functools.partial(product, left1_ref, right1_ref))


def grads_one_body(left_ref, right_ref, own_ref, other_ref):
    half = own_ref.shape[0]
    right = right_ref[...]
    own_ref[...] = matmul_nn(left_ref[:half, :], right).astype(LOW)
    other_ref[...] = matmul_nn(left_ref[half:, :], right).astype(LOW)


def turn_body(
    place_ref,
    x_ref,
    p_ref,
    r_ref,
    g_ref,
    a_ref,
    b_ref,
    gain_ref,
    wo_ref,
    datt_ref,
    turned_ref,
    dmix_ref,
    dgain_ref,
):
    step = pl.program_id(0)
    attended = x_ref[...].astype(HIGH) + (p_ref[...].astype(HIGH) + r_ref[...].astype(HIGH))
    unit, scale = rms_parts(attended)
    d_normed = a_ref[...].astype(HIGH) + b_ref[...].astype(HIGH)
    d_gain = jnp.sum(d_normed * unit, axis=0, keepdims=True)
    d_attended = g_ref[...].astype(HIGH) + rms_back(d_normed, unit, scale, gain_ref[...])
    d_low = d_attended.astype(LOW)
    put_turned(turned_ref, d_low, False, place_ref[0])
    dmix_ref[...] = matmul_nn(d_low, wo_ref[...]).astype(LOW)

    @pl.when(step == 0)
    def _():
        dgain_ref[...] = d_gain

    @pl.when(step != 0)
    def _():
        dgain_ref[...] += d_gain

    @pl.when(step >= pl.num_programs(0) // 2)
    def _():
        datt_ref[...] = d_attended


def backward_body(
    q_ref,
    k_ref,
    v_ref,
    e_ref,
    dmix_ref,
    mixed_ref,
    inv_ref,
    dq_ref,
    dk_ref,
    dv_ref,
    strip_ref,
    table_ref,
    dkt_ref,
    dvt_ref,
):
    seq_len = k_ref.shape[0]
    rows = table_ref.shape[1]
    low_masks = head_masks(LOW)
    masks = head_masks(HIGH)
    keys = k_ref[...]
    values = v_ref[...]
    keys_h = tuple(keys * low_masks[h] for h in range(2))
    table_ref[...] = jnp.zeros_like(table_ref)
    for block in range(seq_len // rows):
        at = slice(block * rows, (block + 1) * rows)
        queries = q_ref[at, :]
        scaled = (dmix_ref[at, :].astype(HIGH) * inv_ref[at, :]).astype(LOW)
        product = scaled.astype(HIGH) * mixed_ref[at, :]
        d_query = jnp.zeros((rows, LANES), HIGH)
        d_key = jnp.zeros((LANES, seq_len), HIGH)
        d_value = jnp.zeros((LANES, seq_len), HIGH)
        for head in range(2):
            scaled_h = scaled * low_masks[head]
            delta = jnp.sum(product * masks[head], axis=-1, keepdims=True)
            weights = e_ref[head, at, :]
            d_scores = weights.astype(HIGH) * (matmul_nt(scaled_h, values) - delta)
            d_low = d_scores.astype(LOW)
            window = slice(seq_len - block * rows, 2 * seq_len - block * rows)
            table_ref[head, :, window] += d_scores
            d_query = d_query + matmul_nn(d_low, keys_h[head])
            d_key = d_key + matmul_tn(queries * low_masks[head], d_low)
            d_value = d_value + matmul_tn(scaled_h, weights)
        dq_ref[at, :] = d_query.astype(LOW)
        if block == 0:
            dkt_ref[...] = d_key
            dvt_ref[...] = d_value
        else:
            dkt_ref[...] += d_key
            dvt_ref[...] += d_value
    dk_ref[...] = dkt_ref[...].T.astype(LOW)
    dv_ref[...] = dvt_ref[...].T.astype(LOW)
    width = 2 * seq_len
    sub = lax.broadcasted_iota(jnp.int32, (8, 1), 0)
    for head in range(2):
        total = table_ref[head, 0:8, :]
        for group in range(1, rows // 8):
            part = table_ref[head, 8 * group : 8 * group + 8, :]
            total = total + pltpu.roll(part, width - 8 * group, 1)
        for bit in (1, 2, 4):
            total = jnp.where((sub & bit) != 0, pltpu.roll(total, width - bit, 1), total)
        strip_ref[0, head : head + 1, :] = jnp.sum(total, axis=0, keepdims=True)


def spread_body(
    place_ref, x_ref, dq_ref, dk_ref, dv_ref, qkv_ref, send_ref, own_ref, dgain_ref
):
    step = pl.program_id(0)
    width = dq_ref.shape[1]
    unit, _ = rms_parts(x_ref[...].astype(HIGH))
    d_normed = (
        matmul_nt(dq_ref[...], qkv_ref[:, :width])
        + matmul_nt(dk_ref[...], qkv_ref[:, width : 2 * width])
        + matmul_nt(dv_ref[...], qkv_ref[:, 2 * width :])
    )
    d_gain = jnp.sum(d_normed * unit, axis=0, keepdims=True)

    @pl.when(step == 0)
    def _():
        dgain_ref[...] = d_gain

    @pl.when(step != 0)
    def _():
        dgain_ref[...] += d_gain

    @pl.when(step < pl.num_programs(0) // 2)
    def _():
        send_ref[...] = d_normed.astype(LOW)

    @pl.when(step >= pl.num_programs(0) // 2)
    def _():
        own_ref[...] = d_normed


def finish_body(x_ref, own_ref, other_ref, datt_ref, gain_ref, out_ref):
    unit, scale = rms_parts(x_ref[...].astype(HIGH))
    d_normed = own_ref[...] + other_ref[...].astype(HIGH)
    out_ref[...] = (datt_ref[...] + rms_back(d_normed, unit, scale, gain_ref[...])).astype(LOW)


def flat_left(left):
    return left.reshape(-1, left.shape[-1])


def weight_grads(first, second, columns, micros):
    left0, right0, at0, count0 = first
    left1, right1, at1, count1 = second
    left0, left1 = flat_left(left0), flat_left(left1)
    height, depth = left0.shape
    steps = count0 + count1
    half_spec = pl.BlockSpec((height // 2, columns), lambda i: (0, i))
    return call(
        functools.partial(grads_body, count0),
        (steps,),
        [
            whole((height, depth)),
            whole((height, depth)),
            pl.BlockSpec((depth, columns), lambda i: (0, at0 + jnp.minimum(i, count0 - 1))),
            pl.BlockSpec((depth, columns), lambda i: (0, at1 + jnp.maximum(i - count0, 0))),
        ],
        [half_spec, half_spec],
        [shaped((height // 2, steps * columns), LOW)] * 2,
        micros=micros,
    )(left0, left1, right0, right1)


def weight_grads_one(left, right, columns, steps, micros):
    left = flat_left(left)
    height, depth = left.shape
    half_spec = pl.BlockSpec((height // 2, columns), lambda i: (0, i))
    return call(
        grads_one_body,
        (steps,),
        [whole((height, depth)), pl.BlockSpec((depth, columns), lambda i: (0, i))],
        [half_spec, half_spec],
        [shaped((height // 2, steps * columns), LOW)] * 2,
        micros=micros,
    )(left, right)


def on_core_pair(
    tokens,
    cotangent,
    gain_attn,
    w_query,
    w_key,
    w_value,
    w_out,
    rel_table,
    buckets,
    gain_ffn,
    w_gate,
    w_up,
    w_down,
):
    own_rows, features = tokens.shape
    seq_len = 2 * own_rows
    width = w_query.shape[1]
    units = w_gate.shape[1]
    chunk = units // 2
    pairs = width // LANES
    bucket_count, head_count = rel_table.shape
    local_heads = head_count // 2
    count = lax.axis_size("dp")
    far_bit, y_bit, x_bit = dp_place()
    me = lax.axis_index("mp")
    place = jnp.stack([y_bit, x_bit, me, far_bit]).astype(jnp.int32)
    rows = MXU_ROWS
    steps = seq_len // rows
    half_steps = steps // 2
    block_rows = w_query.shape[0]

    def swapped(array):
        return lax.ppermute(array, "mp", [(0, 1), (1, 0)])

    def in_order(array, other):
        first = jnp.where(me == 0, array, other)
        second = jnp.where(me == 0, other, array)
        return jnp.concatenate([first, second], axis=0)

    early = jnp.concatenate([w_query, w_key, w_value, w_out.T], axis=1)
    late = jnp.concatenate([w_gate, w_up, w_down.T], axis=1)
    early_pieces = far_pieces(early)
    x_other, g_other = swapped(tokens), swapped(cotangent)
    late_pieces = far_pieces(late)
    early_pieces = together(*early_pieces)
    near = far_stack(early, list(early_pieces))
    qk = near[:, : 2 * width]
    vo = near[:, 2 * width :]
    qk_next, vo_next = together(over_y(qk), over_x(vo))
    qk_own = in_bit_order(qk, qk_next, y_bit)
    vo_own = in_bit_order(vo, vo_next, x_bit)
    qk_other = over_x(qk_own)
    vo_other = over_y(vo_own)
    x_all = in_order(tokens, x_other)
    g_all = in_order(cotangent, g_other)
    qk_other, vo_other, x_all, g_all, *late_pieces = together(
        qk_other, vo_other, x_all, g_all, *late_pieces
    )
    near = far_stack(late, late_pieces)
    gu = near[:, : 3 * chunk]
    ud = near[:, 3 * chunk :]
    gu_next = over_y(gu)
    ud_next = over_x(ud)

    gain_a = gain_attn.reshape(1, features)
    gain_f = gain_ffn.reshape(1, features)

    one_hot = (buckets[:, None] == jnp.arange(bucket_count, dtype=jnp.int32)[None, :]).astype(HIGH)
    one_hot = jnp.pad(one_hot, ((1, 0), (0, 0)))
    my_table = lax.dynamic_slice_in_dim(rel_table, me * local_heads, local_heads, 1)
    strip = lax.dot_general(my_table, one_hot, (((0,), (1,)), ((), ())), precision=precise)
    strip = strip.reshape(pairs, 2, 2 * seq_len)

    def row_block(columns):
        return pl.BlockSpec((rows, columns), lambda i, *_: (i, 0))

    turned_shape = (2, 2, 2, 2, block_rows)
    turned_block = pl.BlockSpec(turned_shape + (rows,), lambda i, *_: (0, 0, 0, 0, 0, i))
    turned = shaped(turned_shape + (seq_len,), LOW)
    full_block = (count // 4, 2, 2, block_rows, 2 * width)
    half_block = (features // 2, 2 * width)
    normed_x_turned, normed_y_turned, queries, keys, values, w_qkv, w_o = call(
        project_body,
        (steps,),
        [row_block(features), whole((1, features))] + [whole(half_block)] * 4,
        [turned_block, turned_block]
        + [row_block(width)] * 3
        + [result((features, 3 * width)), result((features, width))],
        [turned, turned]
        + [shaped((seq_len, width), LOW)] * 3
        + [shaped((features, 3 * width), LOW), shaped((features, width), LOW)],
        [pltpu.VMEM(full_block, LOW), pltpu.VMEM(full_block, LOW)],
        prefetch=1,
        micros=7,
    )(place, x_all, gain_a, qk_own, qk_other, vo_own, vo_other)

    gu_next, ud_next, queries = together(gu_next, ud_next, queries)
    gu_own = in_bit_order(gu, gu_next, y_bit)
    ud_own = in_bit_order(ud, ud_next, x_bit)
    gu_other = over_x(gu_own)
    ud_other = over_y(ud_own)

    pair_block = pl.BlockSpec((seq_len, LANES), lambda p: (0, p))
    e_block = pl.BlockSpec((2, seq_len, seq_len), lambda p: (p, 0, 0))
    strip_block = pl.BlockSpec((1, 2, 2 * seq_len), lambda p: (p, 0, 0))
    table_scratch = pltpu.VMEM((2, rows, 2 * seq_len), HIGH)
    weights_e, mixed, mixed_low, inverse, part = call(
        attend_body,
        (pairs,),
        [
            pair_block,
            pair_block,
            pair_block,
            strip_block,
            pl.BlockSpec((features, LANES), lambda p: (0, p)),
        ],
        [e_block, pair_block, pair_block, pair_block, result((seq_len, features))],
        [
            shaped((2 * pairs, seq_len, seq_len), LOW),
            shaped((seq_len, width), HIGH),
            shaped((seq_len, width), LOW),
            shaped((seq_len, width), HIGH),
            shaped((seq_len, features), LOW),
        ],
        [table_scratch, pltpu.VMEM((seq_len, features), HIGH)],
        micros=20,
    )(queries, keys, values, strip, w_o)
    gu_other, ud_other, part = together(gu_other, ud_other, part)
    part_other = swapped(part)

    def moved(i, m):
        return (i + half_steps * (1 - m[2])) % steps

    def turned_row(columns):
        return pl.BlockSpec((rows, columns), lambda i, m: (moved(i, m), 0))

    moved_block = pl.BlockSpec(
        turned_shape + (rows,), lambda i, m: (0, 0, 0, 0, 0, moved(i, m))
    )
    send_row = pl.BlockSpec((rows, features), lambda i, m: (jnp.minimum(i, half_steps - 1), 0))
    keep_row = pl.BlockSpec((rows, features), lambda i, m: (jnp.maximum(i - half_steps, 0), 0))
    full_block = (count // 4, 2, 2, block_rows, 3 * chunk)
    half_block = (features // 2, 3 * chunk)
    feed_x_turned, feed_y_turned, g_turned, hidden, d_gate_up, dn_part, out_send, out_own = call(
        feed_body,
        (steps,),
        [turned_row(features)] * 4 + [whole((1, features))] + [whole(half_block)] * 4,
        [
            moved_block,
            moved_block,
            moved_block,
            turned_row(units),
            turned_row(2 * units),
            turned_row(features),
            send_row,
            keep_row,
        ],
        [
            turned,
            turned,
            turned,
            shaped((seq_len, units), LOW),
            shaped((seq_len, 2 * units), LOW),
            shaped((seq_len, features), LOW),
            shaped((own_rows, features), LOW),
            shaped((own_rows, features), HIGH),
        ],
        [pltpu.VMEM(full_block, LOW), pltpu.VMEM(full_block, LOW)],
        prefetch=1,
        micros=19,
    )(place, x_all, part, part_other, g_all, gain_f, gu_own, gu_other, ud_own, ud_other)
    dn_other = swapped(dn_part)

    gu_own, gu_send = weight_grads_one(feed_x_turned, d_gate_up, 3 * chunk // 2, 2, 5.5)
    gu_send, hidden, dn_other = together(gu_send, hidden, dn_other)
    gu_came = over_x(gu_send)
    ud_own, ud_send = weight_grads(
        (feed_y_turned, d_gate_up, 3, 1), (g_turned, hidden, 0, 2), chunk, 6.5
    )
    ud_send, dn_other = together(ud_send, dn_other)
    ud_came = over_y(ud_send)

    d_attended, d_low_turned, d_mixed, d_gain_f = call(
        turn_body,
        (steps,),
        [turned_row(features)] * 6 + [whole((1, features)), whole((features, width))],
        [keep_row, moved_block, turned_row(width), result((1, features))],
        [
            shaped((own_rows, features), HIGH),
            turned,
            shaped((seq_len, width), LOW),
            shaped((1, features), HIGH),
        ],
        prefetch=1,
        micros=8,
    )(place, x_all, part, part_other, g_all, dn_part, dn_other, gain_f, w_o)
    out_other = swapped(out_send)

    d_query, d_key, d_value, d_strip = call(
        backward_body,
        (pairs,),
        [pair_block, pair_block, pair_block, e_block, pair_block, pair_block, pair_block],
        [pair_block, pair_block, pair_block, strip_block],
        [shaped((seq_len, width), LOW)] * 3 + [shaped((pairs, 2, 2 * seq_len), HIGH)],
        [table_scratch, pltpu.VMEM((LANES, seq_len), HIGH), pltpu.VMEM((LANES, seq_len), HIGH)],
        micros=16,
    )(queries, keys, values, weights_e, d_mixed, mixed, inverse)

    gu_came, ud_came, out_other, d_query, d_key, d_value, d_strip = together(
        gu_came, ud_came, out_other, d_query, d_key, d_value, d_strip
    )

    def next_half(own, came, bit):
        return (
            add_low(part_of(own, bit, 2), part_of(came, bit, 2)),
            add_low(part_of(own, 1 - bit, 2), part_of(came, 1 - bit, 2)),
        )

    gu_own, gu_send = next_half(gu_own, gu_came, y_bit)
    ud_own, ud_send = next_half(ud_own, ud_came, x_bit)
    gu_came = over_y(gu_send)
    ud_came = over_x(ud_send)

    qk_own, qk_send = weight_grads(
        (normed_x_turned, d_query, 0, 1), (normed_x_turned, d_key, 0, 1), width, 5
    )
    qk_send, d_value = together(qk_send, d_value)
    vo_own, vo_send = weight_grads(
        (normed_y_turned, d_value, 0, 1), (d_low_turned, mixed_low, 0, 1), width, 5
    )
    output = (out_own + out_other.astype(HIGH)).astype(LOW)

    gu_came, ud_came, qk_send, vo_send, d_query = together(
        gu_came, ud_came, qk_send, vo_send, d_query
    )
    qk_came = over_x(qk_send)
    vo_came = over_y(vo_send)
    gu_own, gu_send = next_half(gu_own, gu_came, far_bit % 2)
    ud_own, ud_send = next_half(ud_own, ud_came, far_bit % 2)
    unit_own = jnp.concatenate([gu_own, ud_own], axis=1)
    unit_send = jnp.concatenate([gu_send, ud_send], axis=1)
    unit_came = over_far_bit(unit_send, 0)

    dna_send, dna_own, d_gain_a = call(
        spread_body,
        (steps,),
        [turned_row(features)] + [turned_row(width)] * 3 + [whole((features, 3 * width))],
        [send_row, keep_row, result((1, features))],
        [
            shaped((own_rows, features), LOW),
            shaped((own_rows, features), HIGH),
            shaped((1, features), HIGH),
        ],
        prefetch=1,
        micros=7,
    )(place, x_all, d_query, d_key, d_value, w_qkv)
    qk_came, vo_came, unit_came, dna_send, d_gain_a, d_strip = together(
        qk_came, vo_came, unit_came, dna_send, d_gain_a, d_strip
    )
    unit_own, unit_send = next_half(unit_own, unit_came, far_bit // 2)
    unit_came = over_far_bit(unit_send, 1)
    dna_other = swapped(dna_send)
    qk_own, qk_send = next_half(qk_own, qk_came, y_bit)
    vo_own, vo_send = next_half(vo_own, vo_came, x_bit)
    qk_came = over_y(qk_send)
    vo_came = over_x(vo_send)

    d_bias = d_strip.reshape(local_heads, 2 * seq_len)
    my_d_table = lax.dot_general(one_hot, d_bias, (((0,), (1,)), ((), ())), precision=precise)
    d_table = lax.dynamic_update_slice_in_dim(
        jnp.zeros_like(rel_table), my_d_table, me * local_heads, 1
    )
    small = jnp.concatenate(
        [d_gain_a.reshape(features), 0.5 * d_gain_f.reshape(features), d_table.reshape(-1)]
    )
    small = jnp.pad(small, (0, -small.shape[0] % 1024)).reshape(-1, LANES)
    small = small + swapped(small)
    small = small + over_x(small)
    small = small + over_y(small)

    d_tokens = call(
        finish_body,
        (half_steps,),
        [row_block(features)] * 4 + [whole((1, features))],
        row_block(features),
        shaped((own_rows, features), LOW),
        micros=3.5,
    )(tokens, dna_own, dna_other, d_attended, gain_a)

    qk_came, vo_came, unit_came, d_tokens, small = together(
        qk_came, vo_came, unit_came, d_tokens, small
    )
    head_own = jnp.concatenate([qk_own, vo_own], axis=-1)
    head_came = jnp.concatenate([qk_came, vo_came], axis=-1)
    total = add_low(head_own, head_came)

    def far_part(far):
        return part_of(total, 2 * (far % 2) + far // 2, 4)

    pieces = [over_far(far_part((far_bit + k) % 4), k) for k in range(1, 4)]
    small = small + over_far_bit(small, 0)
    small = (small + over_far_bit(small, 1)).reshape(-1)
    grads_head = sum((piece.astype(HIGH) for piece in pieces), far_part(far_bit).astype(HIGH))
    grads_qk, grads_vo = grads_head[:, : 2 * width], grads_head[:, 2 * width :]
    grads_unit = unit_own.astype(HIGH) + unit_came.astype(HIGH)
    return (
        output,
        d_tokens,
        small[:features],
        grads_qk[:, :width],
        grads_qk[:, width:],
        grads_vo[:, :width],
        grads_vo[:, width:].T,
        small[2 * features : 2 * features + rel_table.size].reshape(rel_table.shape),
        small[features : 2 * features],
        grads_unit[:, :units],
        grads_unit[:, units : 2 * units],
        grads_unit[:, 2 * units :].T,
    )


def solution(mesh):
    placed = (
        P(("dp", "mp"), None),
        P(("dp", "mp"), None),
        P(),
        P("dp", "mp"),
        P("dp", "mp"),
        P("dp", "mp"),
        P("mp", "dp"),
        P(),
        P(),
        P(),
        P("dp", "mp"),
        P("dp", "mp"),
        P("mp", "dp"),
    )
    paired = mesh.shape["mp"] == 2 and mesh.shape["dp"] == 16
    body = on_core_pair if paired else on_device
    return jax.shard_map(
        body,
        mesh=mesh,
        in_specs=placed,
        out_specs=(
            P(("dp", "mp"), None),
            P(("dp", "mp"), None),
            P(),
            P("dp", "mp"),
            P("dp", "mp"),
            P("dp", "mp"),
            P("mp", "dp"),
            P(),
            P(),
            P("dp", "mp"),
            P("dp", "mp"),
            P("mp", "dp"),
        ),
        check_vma=False,
    )
```

```python
import functools

import jax
import jax.numpy as jnp
from jax import lax
from jax.experimental import pallas as pl
from jax.experimental.pallas import tpu as pltpu
from jax.sharding import PartitionSpec as P

epsilon = 1e-06
block_limit = 512
precise = lax.Precision.HIGHEST


def as_sent(array):

    def short(part):
        return part.astype(jnp.bfloat16) if part.dtype == jnp.float32 else part

    return jax.tree.map(short, array)


def matmul_nn(left, right):
    return jnp.dot(left, right, preferred_element_type=jnp.float32)


def matmul_nt(left, right):
    return lax.dot_general(
        left, right, (((1,), (1,)), ((), ())), preferred_element_type=jnp.float32
    )


def matmul_tn(left, right):
    return lax.dot_general(
        left, right, (((0,), (0,)), ((), ())), preferred_element_type=jnp.float32
    )


def rms_parts(inputs):
    scale = lax.rsqrt(jnp.mean(inputs * inputs, axis=-1, keepdims=True) + epsilon)
    return (inputs * scale, scale)


def rms_back(d_normed, unit, scale, gain):
    d_unit = d_normed * gain
    return scale * (d_unit - unit * jnp.mean(d_unit * unit, axis=-1, keepdims=True))


def gated(gate_pre, up_pre):
    return jax.nn.gelu(gate_pre, approximate=True) * up_pre


def window_base(first_query, first_key, row_count, seq_len):
    return first_key - first_query - row_count + seq_len


def make_bias(bias_full, base, row_count, width):
    span = width + row_count - 1
    head_count = bias_full.shape[0]
    strip = lax.dynamic_slice_in_dim(bias_full, base, span, 1)
    tiled = jnp.tile(strip, (1, row_count + 1))
    window = tiled[:, row_count - 1 : row_count - 1 + row_count * (span - 1)]
    return window.reshape(head_count, row_count, span - 1)[:, :, :width]


def skew_sum(d_block, row_count, width):
    head_count = d_block.shape[0]
    span = width + row_count - 1
    padded = jnp.pad(d_block, ((0, 0), (0, 0), (row_count - 1, 0)))
    flat = padded.reshape(head_count, row_count * span)
    flat = jnp.pad(flat, ((0, 0), (0, row_count)))
    skewed = flat.reshape(head_count, row_count, span + 1)[:, :, :span]
    return jnp.sum(skewed, axis=1)


def add_window(d_bias, piece, base):
    current = lax.dynamic_slice_in_dim(d_bias, base, piece.shape[1], 1)
    return lax.dynamic_update_slice_in_dim(d_bias, current + piece, base, 1)


def sum_rows(partial_value):
    return lax.psum_scatter(
        partial_value.astype(jnp.bfloat16), "mp", scatter_dimension=0, tiled=True
    ).astype(jnp.float32)


def split_heads(queries, keys_all, values, head_count):
    row_count = queries.shape[0]
    seq_len = keys_all.shape[0]
    head_dim = queries.shape[1] // head_count
    width = min(block_limit, seq_len)
    blocks = seq_len // width
    heads_q = queries.reshape(row_count, head_count, head_dim)
    heads_k = keys_all.reshape(blocks, width, head_count, head_dim)
    heads_v = values.reshape(blocks, width, head_count, head_dim)
    starts = jnp.arange(blocks, dtype=jnp.int32) * width
    return (heads_q, heads_k, heads_v, starts, width)


def attend_forward(queries, keys_all, values, bias_full, head_count, first_row):
    row_count = queries.shape[0]
    seq_len = keys_all.shape[0]
    heads_q, heads_k, heads_v, starts, width = split_heads(queries, keys_all, values, head_count)

    def block_scores(key_block, first_key):
        raw_scores = jnp.einsum(
            "qhd,khd->hqk", heads_q, key_block, preferred_element_type=jnp.float32
        )
        base = window_base(first_row, first_key, row_count, seq_len)
        return raw_scores + make_bias(bias_full, base, row_count, width)

    def stats_step(running, pieces):
        top_now, total = running
        scores = block_scores(pieces[0], pieces[1])
        top_new = jnp.maximum(top_now, jnp.max(scores, axis=-1))
        total = total * jnp.exp(top_now - top_new) + jnp.sum(
            jnp.exp(scores - top_new[..., None]), axis=-1
        )
        return ((top_new, total), None)

    start_top = jnp.full((head_count, row_count), -jnp.inf, jnp.float32)
    start_total = jnp.zeros((head_count, row_count), jnp.float32)
    (top_all, total), _ = lax.scan(stats_step, (start_top, start_total), (heads_k, starts))
    log_total = top_all + jnp.log(total)

    def mix_step(running, pieces):
        scores = block_scores(pieces[0], pieces[2])
        probs_low = jnp.exp(scores - log_total[..., None]).astype(jnp.bfloat16)
        update = jnp.einsum(
            "hqk,khd->qhd", probs_low, pieces[1], preferred_element_type=jnp.float32
        )
        return (running + update, None)

    start_mix = jnp.zeros(heads_q.shape, jnp.float32)
    mixed_f, _ = lax.scan(mix_step, start_mix, (heads_k, heads_v, starts))
    return (mixed_f.reshape(row_count, queries.shape[1]), log_total)


def attend_backward(
    queries, keys_all, values, bias_full, head_count, first_row, log_total, deltas, d_mixed
):
    row_count = queries.shape[0]
    seq_len = keys_all.shape[0]
    heads_q, heads_k, heads_v, starts, width = split_heads(queries, keys_all, values, head_count)
    heads_d = d_mixed.reshape(heads_q.shape)

    def back_step(running, pieces):
        d_query, d_bias = running
        key_block, value_block, first_key = pieces
        base = window_base(first_row, first_key, row_count, seq_len)
        scores = jnp.einsum("qhd,khd->hqk", heads_q, key_block, preferred_element_type=jnp.float32)
        scores = scores + make_bias(bias_full, base, row_count, width)
        probs = jnp.exp(scores - log_total[..., None])
        d_probs = jnp.einsum(
            "qhd,khd->hqk", heads_d, value_block, preferred_element_type=jnp.float32
        )
        d_scores = (probs * (d_probs - deltas[..., None])).astype(jnp.bfloat16)
        d_query = d_query + jnp.einsum(
            "hqk,khd->qhd", d_scores, key_block, preferred_element_type=jnp.float32
        )
        d_bias = add_window(d_bias, skew_sum(d_scores.astype(jnp.float32), row_count, width), base)
        probs_low = probs.astype(jnp.bfloat16)
        d_value = jnp.einsum("hqk,qhd->khd", probs_low, heads_d, preferred_element_type=jnp.float32)
        d_key = jnp.einsum("hqk,qhd->khd", d_scores, heads_q, preferred_element_type=jnp.float32)
        return ((d_query, d_bias), (d_key, d_value))

    start_query = jnp.zeros(heads_q.shape, jnp.float32)
    (d_query, d_bias), kv_parts = lax.scan(
        back_step, (start_query, jnp.zeros_like(bias_full)), (heads_k, heads_v, starts)
    )
    feature_count = queries.shape[1]
    d_query = d_query.reshape(row_count, feature_count)
    return (
        d_query,
        d_bias,
        kv_parts[0].reshape(seq_len, feature_count),
        kv_parts[1].reshape(seq_len, feature_count),
    )


def on_device(
    tokens,
    cotangent,
    gain_attn,
    w_query,
    w_key,
    w_value,
    w_out,
    rel_table,
    buckets,
    gain_ffn,
    w_gate,
    w_up,
    w_down,
):
    head_count = rel_table.shape[1]
    bucket_count = rel_table.shape[0]
    inputs = tokens.astype(jnp.float32)
    row_count = inputs.shape[0]
    feature_count = inputs.shape[1]
    first_row = lax.axis_index("mp") * row_count
    attn_parts = (w_query, w_key, w_value, w_out.T)
    ffn_parts = (w_gate, w_up, w_down.T)
    ffn_cols = ()
    col_parts = lax.all_gather(as_sent(attn_parts + ffn_cols), "mp", axis=1, tiled=True)
    full_parts = lax.all_gather(as_sent(tuple(col_parts) + ffn_parts), "dp", axis=0, tiled=True)
    query_full, key_full, value_full, out_full, gate_full, up_full, down_full = full_parts
    unit_a, scale_a = rms_parts(inputs)
    normed_a = (unit_a * gain_attn).astype(jnp.bfloat16)
    queries = matmul_nn(normed_a, query_full).astype(jnp.bfloat16)
    own_keys = matmul_nn(normed_a, key_full).astype(jnp.bfloat16)
    own_values = matmul_nn(normed_a, value_full).astype(jnp.bfloat16)
    keys_all, values = (
        lax.all_gather(own_keys, "mp", axis=0, tiled=True),
        lax.all_gather(own_values, "mp", axis=0, tiled=True),
    )
    one_hot = (buckets[:, None] == jnp.arange(bucket_count, dtype=jnp.int32)[None, :]).astype(
        jnp.float32
    )
    bias_full = jnp.dot(one_hot, rel_table, precision=precise).T
    mixed_f, log_total = attend_forward(queries, keys_all, values, bias_full, head_count, first_row)
    mixed_out = mixed_f.astype(jnp.bfloat16)
    attended = inputs + matmul_nt(mixed_out, out_full)
    unit_f, scale_f = rms_parts(attended)
    normed_f = (unit_f * gain_ffn).astype(jnp.bfloat16)
    normed_seq, cot_seq = (
        lax.all_gather(normed_f, "mp", axis=0, tiled=True),
        lax.all_gather(cotangent, "mp", axis=0, tiled=True),
    )
    gate_pre = matmul_nn(normed_seq, gate_full)
    up_pre = matmul_nn(normed_seq, up_full)
    hidden = gated(gate_pre, up_pre).astype(jnp.bfloat16)
    output = attended + sum_rows(matmul_nt(hidden, down_full))
    d_hidden = matmul_nn(cot_seq, down_full)
    d_down = matmul_tn(cot_seq, hidden)
    _, pull_gate = jax.vjp(gated, gate_pre, up_pre)
    d_gate, d_up = pull_gate(d_hidden)
    d_gate = d_gate.astype(jnp.bfloat16)
    d_up = d_up.astype(jnp.bfloat16)
    d_normed_f = sum_rows(matmul_nt(d_gate, gate_full) + matmul_nt(d_up, up_full))
    d_gate_w = matmul_tn(normed_seq, d_gate)
    d_up_w = matmul_tn(normed_seq, d_up)
    d_gain_f = jnp.sum(d_normed_f * unit_f, axis=0)
    d_attended = cotangent.astype(jnp.float32) + rms_back(d_normed_f, unit_f, scale_f, gain_ffn)
    d_att_low = d_attended.astype(jnp.bfloat16)
    d_out_w = matmul_tn(d_att_low, mixed_out)
    d_mixed = matmul_nn(d_att_low, out_full).astype(jnp.bfloat16)
    head_dim = feature_count // head_count
    deltas = jnp.sum(
        (d_mixed.astype(jnp.float32) * mixed_f).reshape(row_count, head_count, head_dim), axis=-1
    ).T
    d_query, d_bias, d_keys_part, d_values_part = attend_backward(
        queries, keys_all, values, bias_full, head_count, first_row, log_total, deltas, d_mixed
    )
    d_keys_own, d_values_own = (
        lax.psum_scatter(
            d_keys_part.astype(jnp.bfloat16), "mp", scatter_dimension=0, tiled=True
        ).astype(jnp.float32),
        lax.psum_scatter(
            d_values_part.astype(jnp.bfloat16), "mp", scatter_dimension=0, tiled=True
        ).astype(jnp.float32),
    )
    d_keys_own = d_keys_own.astype(jnp.bfloat16)
    d_values_own = d_values_own.astype(jnp.bfloat16)
    d_query = d_query.astype(jnp.bfloat16)
    d_normed_a = (
        matmul_nt(d_query, query_full)
        + matmul_nt(d_keys_own, key_full)
        + matmul_nt(d_values_own, value_full)
    )
    d_query_w = matmul_tn(normed_a, d_query)
    d_key_w = matmul_tn(normed_a, d_keys_own)
    d_value_w = matmul_tn(normed_a, d_values_own)
    d_gain_a = jnp.sum(d_normed_a * unit_a, axis=0)
    d_tokens = (d_attended + rms_back(d_normed_a, unit_a, scale_a, gain_attn)).astype(jnp.bfloat16)
    d_table = jnp.dot(d_bias, one_hot, precision=precise).T
    row_grads = (
        lax.psum_scatter(
            d_query_w.astype(jnp.bfloat16), "dp", scatter_dimension=0, tiled=True
        ).astype(jnp.float32),
        lax.psum_scatter(
            d_key_w.astype(jnp.bfloat16), "dp", scatter_dimension=0, tiled=True
        ).astype(jnp.float32),
        lax.psum_scatter(
            d_value_w.astype(jnp.bfloat16), "dp", scatter_dimension=0, tiled=True
        ).astype(jnp.float32),
        lax.psum_scatter(
            d_out_w.astype(jnp.bfloat16), "dp", scatter_dimension=0, tiled=True
        ).astype(jnp.float32),
        lax.psum_scatter(
            d_gate_w.astype(jnp.bfloat16), "dp", scatter_dimension=0, tiled=True
        ).astype(jnp.float32),
        lax.psum_scatter(d_up_w.astype(jnp.bfloat16), "dp", scatter_dimension=0, tiled=True).astype(
            jnp.float32
        ),
        lax.psum_scatter(d_down.astype(jnp.bfloat16), "dp", scatter_dimension=0, tiled=True).astype(
            jnp.float32
        ),
    )
    row_grads = tuple(row_grads)
    ffn_late = ()
    col_grads = tuple(
        jax.tree.map(
            lambda part: part.astype(jnp.float32),
            lax.psum_scatter(
                as_sent(row_grads[:4] + ffn_late), "mp", scatter_dimension=1, tiled=True
            ),
        )
    )
    ffn_done = row_grads[4:]
    small_sums = lax.psum((d_gain_a, d_gain_f, d_table), ("dp", "mp"))
    return (
        output.astype(jnp.bfloat16),
        d_tokens,
        small_sums[0],
        col_grads[0],
        col_grads[1],
        col_grads[2],
        col_grads[3].T,
        small_sums[2],
        small_sums[1],
        ffn_done[0],
        ffn_done[1],
        ffn_done[2].T,
    )


MXU_ROWS = 256
LANES = 128
VMEM_LIMIT = 56 * 2**20
PEAK_PER_MICRO = 1_153_500_000
LOW = jnp.bfloat16
HIGH = jnp.float32


def call(
    body, grid, in_specs, out_specs, out_shape, scratch=(), prefetch=0, micros=5, aliases=None
):
    return pl.pallas_call(
        body,
        grid_spec=pltpu.PrefetchScalarGridSpec(
            num_scalar_prefetch=prefetch,
            grid=grid,
            in_specs=in_specs,
            out_specs=out_specs,
            scratch_shapes=list(scratch),
        ),
        out_shape=out_shape,
        input_output_aliases=aliases or {},
        compiler_params=pltpu.CompilerParams(vmem_limit_bytes=VMEM_LIMIT),
        cost_estimate=pl.CostEstimate(
            flops=int(micros * PEAK_PER_MICRO), bytes_accessed=0, transcendentals=0
        ),
    )


def shaped(shape, dtype):
    return jax.ShapeDtypeStruct(shape, dtype)


def whole(shape):
    return pl.BlockSpec(shape, lambda *_: (0,) * len(shape), pipeline_mode=pl.Buffered(1))


def result(shape):
    return pl.BlockSpec(shape, lambda *_: (0,) * len(shape))


def together(*arrays):
    return lax.optimization_barrier(arrays)


def ring_shift(steps, count):
    return [(i, (i + steps) % count) for i in range(count)]


def flip(bit, count):
    return [(i, i ^ bit) for i in range(count)]


def over_x(array):
    return lax.ppermute(array, "dp", flip(1, lax.axis_size("dp")))


def over_y(array):
    return lax.ppermute(array, "dp", flip(2, lax.axis_size("dp")))


def over_xy(array):
    return lax.ppermute(array, "dp", flip(3, lax.axis_size("dp")))


def over_far(array, steps):
    return lax.ppermute(array, "dp", ring_shift(4 * steps, lax.axis_size("dp")))


def dp_place():
    index = lax.axis_index("dp")
    return (index // 4, (index // 2) % 2, index % 2)


def in_bit_order(own, other, bit):
    first = jnp.where(bit == 0, own, other)
    second = jnp.where(bit == 0, other, own)
    return jnp.concatenate([first, second], axis=0)


def far_pieces(shard):
    return [over_far(shard, k) for k in range(1, lax.axis_size("dp") // 4)]


def far_stack(shard, pieces):
    far = len(pieces) + 1
    place = dp_place()[0]
    stacked = jnp.zeros((far,) + shard.shape, shard.dtype)
    for k, piece in enumerate([shard] + pieces):
        stacked = lax.dynamic_update_slice(stacked, piece[None], ((place - k) % far, 0, 0))
    return stacked.reshape(-1, shard.shape[1])


def over_far_bit(array, bit):
    return lax.ppermute(array, "dp", flip(4 << bit, lax.axis_size("dp")))


def part_of(array, index, parts):
    size = array.shape[0] // parts
    return lax.dynamic_slice_in_dim(array, index * size, size, 0)


def add_low(left, right):
    return (left.astype(HIGH) + right.astype(HIGH)).astype(LOW)


def in_terms(array):
    terms, rest = [], array
    for _ in range(3):
        term = lax.optimization_barrier(rest.astype(LOW))
        terms.append(term)
        rest = rest - term.astype(HIGH)
    rows = jnp.concatenate(terms, axis=0)
    return jnp.pad(rows, ((0, -rows.shape[0] % 8), (0, 0)))


def from_terms(rows, height):
    return sum(rows[i * height : (i + 1) * height].astype(HIGH) for i in range(3))


def head_masks(dtype):
    lane = lax.broadcasted_iota(jnp.int32, (1, LANES), 1)
    first = (lane < LANES // 2).astype(HIGH)
    return (first.astype(dtype), (1.0 - first).astype(dtype))


def put_weights(full_ref, own_ref, other_ref, y_first, bit):
    far, rows = full_ref.shape[0], full_ref.shape[3]
    for half_ref, at in ((own_ref, bit), (other_ref, 1 - bit)):
        for near in range(2):
            for place in range(far):
                start = (near * far + place) * rows
                block = half_ref[start : start + rows, :]
                if y_first:
                    full_ref[place, near, at] = block
                else:
                    full_ref[place, at, near] = block


def put_turned(turned_ref, array, x_first, bit):
    rows = turned_ref.shape[4]
    turned = array.T
    for block in range(turned.shape[0] // rows):
        far, y_bit, x_bit = block // 4, (block // 2) % 2, block % 2
        first, second = (x_bit, y_bit) if x_first else (y_bit, x_bit)
        other = 1 - bit if first else bit
        turned_ref[other, second, far % 2, far // 2] = turned[block * rows : (block + 1) * rows]


def matrix(full_ref, start, columns):
    part = full_ref[:, :, :, :, start : start + columns]
    return part.reshape(-1, columns)


def project_body(
    place_ref,
    x_ref,
    gain_ref,
    qk_own_ref,
    qk_other_ref,
    vo_own_ref,
    vo_other_ref,
    turned_x_ref,
    turned_y_ref,
    q_ref,
    k_ref,
    v_ref,
    qkv_ref,
    wo_ref,
    qk_ref,
    vo_ref,
):
    width = q_ref.shape[1]

    @pl.when(pl.program_id(0) == 0)
    def _():
        put_weights(qk_ref, qk_own_ref, qk_other_ref, True, place_ref[1])
        put_weights(vo_ref, vo_own_ref, vo_other_ref, False, place_ref[0])
        qkv_ref[:, : 2 * width] = matrix(qk_ref, 0, 2 * width)
        qkv_ref[:, 2 * width :] = matrix(vo_ref, 0, width)
        wo_ref[...] = matrix(vo_ref, width, width)

    unit, _ = rms_parts(x_ref[...].astype(HIGH))
    normed = (unit * gain_ref[...]).astype(LOW)
    put_turned(turned_x_ref, normed, True, place_ref[1])
    put_turned(turned_y_ref, normed, False, place_ref[0])
    q_ref[...] = matmul_nn(normed, qkv_ref[:, :width]).astype(LOW)
    k_ref[...] = matmul_nn(normed, qkv_ref[:, width : 2 * width]).astype(LOW)
    v_ref[...] = matmul_nn(normed, qkv_ref[:, 2 * width :]).astype(LOW)


def attend_body(
    q_ref, k_ref, v_ref, strip_ref, wo_ref, e_ref, mixed_ref, low_ref, inv_ref, part0_ref, part1_ref, table_ref, acc_ref
):
    pair = pl.program_id(0)
    seq_len = k_ref.shape[0]
    rows = table_ref.shape[1]
    low_masks = head_masks(LOW)
    own_lanes = tuple(mask > 0.5 for mask in head_masks(HIGH))
    for head in range(2):
        row = jnp.broadcast_to(strip_ref[0, head : head + 1, :], (rows, 2 * seq_len))
        table_ref[head] = pltpu.roll(row, 0, 1, stride=1, stride_axis=0)
    keys = k_ref[...]
    values = v_ref[...]
    values_h = tuple(values * low_masks[h] + low_masks[1 - h] for h in range(2))

    @pl.when(pair == 0)
    def _():
        acc_ref[...] = jnp.zeros_like(acc_ref)

    def scored(block, head):
        at = slice(block * rows, (block + 1) * rows)
        raw = matmul_nt(q_ref[at, :] * low_masks[head], keys)
        return raw + table_ref[head, :, seq_len - block * rows : 2 * seq_len - block * rows]

    units = [(block, head) for block in range(seq_len // rows) for head in range(2)]
    ahead = scored(*units[0])
    summed = [None, None]
    for number, (block, head) in enumerate(units):
        at = slice(block * rows, (block + 1) * rows)
        scores = ahead
        if number + 1 < len(units):
            ahead = scored(*units[number + 1])
        top = jnp.max(scores, axis=-1, keepdims=True)
        weights = jnp.exp(scores - top).astype(LOW)
        e_ref[head, at, :] = weights
        summed[head] = matmul_nn(weights, values_h[head])
        if head == 1:
            totals = jnp.where(own_lanes[0], summed[1], summed[0])
            inverse = 1.0 / pltpu.roll(totals, LANES // 2, 1)
            mixed = jnp.where(own_lanes[0], summed[0], summed[1]) * inverse
            mixed_ref[at, :] = mixed
            low_ref[at, :] = mixed.astype(LOW)
            inv_ref[at, :] = inverse
    acc_ref[...] += matmul_nt(low_ref[...], wo_ref[...])

    @pl.when(pair == pl.num_programs(0) - 1)
    def _():
        half = part0_ref.shape[0]
        part0_ref[...] = acc_ref[:half, :].astype(LOW)
        part1_ref[...] = acc_ref[half:, :].astype(LOW)


def late_half(place_ref):
    partner_first = pl.program_id(0) < pl.num_programs(0) // 2
    return partner_first == (place_ref[2] == 0)


def summed_halves(left_ref, right_ref):
    return left_ref[...].astype(HIGH) + right_ref[...].astype(HIGH)


def feed_body(
    place_ref,
    x_ref,
    p0_ref,
    p1_ref,
    r0_ref,
    r1_ref,
    g_ref,
    gain_ref,
    gu_own_ref,
    gu_other_ref,
    ud_own_ref,
    ud_other_ref,
    turned_x_ref,
    turned_y_ref,
    g_turned_ref,
    hidden_ref,
    dgu_ref,
    dn_ref,
    send_ref,
    own_ref,
    gu_ref,
    ud_ref,
):
    step = pl.program_id(0)
    late = late_half(place_ref)

    @pl.when(step == 0)
    def _():
        put_weights(gu_ref, gu_own_ref, gu_other_ref, True, place_ref[1])
        put_weights(ud_ref, ud_own_ref, ud_other_ref, False, place_ref[0])

    attended = x_ref[...].astype(HIGH) + jnp.where(
        late, summed_halves(p1_ref, r1_ref), summed_halves(p0_ref, r0_ref)
    )
    unit, _ = rms_parts(attended)
    normed = (unit * gain_ref[...]).astype(LOW)
    put_turned(turned_x_ref, normed, True, place_ref[1])
    put_turned(turned_y_ref, normed, False, place_ref[0])
    cotangent = g_ref[...]
    put_turned(g_turned_ref, cotangent, False, place_ref[0])
    root = 0.7978845608028654
    columns = hidden_ref.shape[1] // 2
    products = []
    for part in range(2):
        w_gate = matrix(gu_ref, part * columns, columns)
        w_up = matrix(ud_ref, 0, columns) if part else matrix(gu_ref, 2 * columns, columns)
        w_down = matrix(ud_ref, (1 + part) * columns, columns)
        gate = matmul_nn(normed, w_gate)
        up = matmul_nn(normed, w_up)
        d_hidden = matmul_nn(cotangent, w_down)
        products.append((gate, up, d_hidden, w_gate, w_up, w_down))
    out = 0.0
    d_normed = 0.0
    for part, (gate, up, d_hidden, w_gate, w_up, w_down) in enumerate(products):
        square = gate * gate
        bend = jnp.tanh(gate * (root + (root * 0.044715) * square))
        half = 0.5 + 0.5 * bend
        gelu = gate * half
        slope = half + (0.5 * gate) * (1.0 - bend * bend) * (root + (3 * root * 0.044715) * square)
        hidden = (gelu * up).astype(LOW)
        d_gate = (d_hidden * up * slope).astype(LOW)
        d_up = (d_hidden * gelu).astype(LOW)
        hidden_ref[:, part * columns : (part + 1) * columns] = hidden
        dgu_ref[:, part * columns : (part + 1) * columns] = d_gate
        dgu_ref[:, (2 + part) * columns : (3 + part) * columns] = d_up
        d_normed = d_normed + matmul_nt(d_gate, w_gate) + matmul_nt(d_up, w_up)
        out = out + matmul_nt(hidden, w_down)
    dn_ref[...] = d_normed.astype(LOW)

    @pl.when(step < pl.num_programs(0) // 2)
    def _():
        send_ref[...] = out.astype(LOW)

    @pl.when(step >= pl.num_programs(0) // 2)
    def _():
        own_ref[...] = attended + out


def grads_body(first_count, left0_ref, left1_ref, right0_ref, right1_ref, own_ref, other_ref):
    step = pl.program_id(0)
    half = own_ref.shape[0]

    def product(left_ref, right_ref):
        right = right_ref[...]
        own_ref[...] = matmul_nn(left_ref[:half, :], right).astype(LOW)
        other_ref[...] = matmul_nn(left_ref[half:, :], right).astype(LOW)

    pl.when(step < first_count)(functools.partial(product, left0_ref, right0_ref))
    pl.when(step >= first_count)(functools.partial(product, left1_ref, right1_ref))


def grads_one_body(left_ref, right_ref, own_ref, other_ref):
    half = own_ref.shape[0]
    right = right_ref[...]
    own_ref[...] = matmul_nn(left_ref[:half, :], right).astype(LOW)
    other_ref[...] = matmul_nn(left_ref[half:, :], right).astype(LOW)


def turn_body(
    place_ref,
    x_ref,
    p0_ref,
    p1_ref,
    r0_ref,
    r1_ref,
    g_ref,
    a_ref,
    b_ref,
    gain_ref,
    wo_ref,
    datt_ref,
    turned_ref,
    dmix_ref,
    dgain_ref,
):
    step = pl.program_id(0)
    late = late_half(place_ref)
    attended = x_ref[...].astype(HIGH) + jnp.where(
        late, summed_halves(p1_ref, r1_ref), summed_halves(p0_ref, r0_ref)
    )
    unit, scale = rms_parts(attended)
    d_normed = a_ref[...].astype(HIGH) + b_ref[...].astype(HIGH)
    d_gain = jnp.sum(d_normed * unit, axis=0, keepdims=True)
    d_attended = g_ref[...].astype(HIGH) + rms_back(d_normed, unit, scale, gain_ref[...])
    d_low = d_attended.astype(LOW)
    put_turned(turned_ref, d_low, False, place_ref[0])
    dmix_ref[...] = matmul_nn(d_low, wo_ref[...]).astype(LOW)

    @pl.when(step == 0)
    def _():
        dgain_ref[...] = d_gain

    @pl.when(step != 0)
    def _():
        dgain_ref[...] += d_gain

    @pl.when(step >= pl.num_programs(0) // 2)
    def _():
        datt_ref[...] = d_attended


def backward_body(
    q_ref,
    k_ref,
    v_ref,
    e_ref,
    dmix_ref,
    mixed_ref,
    inv_ref,
    dq_ref,
    dk_ref,
    dv_ref,
    strip_ref,
    table_ref,
    dkt_ref,
    dvt_ref,
):
    seq_len = k_ref.shape[0]
    rows = table_ref.shape[1]
    low_masks = head_masks(LOW)
    masks = head_masks(HIGH)
    keys = k_ref[...]
    values = v_ref[...]
    keys_h = tuple(keys * low_masks[h] for h in range(2))
    table_ref[...] = jnp.zeros_like(table_ref)
    for block in range(seq_len // rows):
        at = slice(block * rows, (block + 1) * rows)
        queries = q_ref[at, :]
        scaled = (dmix_ref[at, :].astype(HIGH) * inv_ref[at, :]).astype(LOW)
        product = scaled.astype(HIGH) * mixed_ref[at, :]
        d_query = jnp.zeros((rows, LANES), HIGH)
        d_key = jnp.zeros((LANES, seq_len), HIGH)
        d_value = jnp.zeros((LANES, seq_len), HIGH)
        for head in range(2):
            scaled_h = scaled * low_masks[head]
            delta = jnp.sum(product * masks[head], axis=-1, keepdims=True)
            weights = e_ref[head, at, :]
            d_scores = weights.astype(HIGH) * (matmul_nt(scaled_h, values) - delta)
            d_low = d_scores.astype(LOW)
            window = slice(seq_len - block * rows, 2 * seq_len - block * rows)
            table_ref[head, :, window] += d_scores
            d_query = d_query + matmul_nn(d_low, keys_h[head])
            d_key = d_key + matmul_tn(queries * low_masks[head], d_low)
            d_value = d_value + matmul_tn(scaled_h, weights)
        dq_ref[at, :] = d_query.astype(LOW)
        if block == 0:
            dkt_ref[...] = d_key
            dvt_ref[...] = d_value
        else:
            dkt_ref[...] += d_key
            dvt_ref[...] += d_value
    dk_ref[...] = dkt_ref[...].T.astype(LOW)
    dv_ref[...] = dvt_ref[...].T.astype(LOW)
    width = 2 * seq_len
    sub = lax.broadcasted_iota(jnp.int32, (8, 1), 0)
    for head in range(2):
        total = table_ref[head, 0:8, :]
        for group in range(1, rows // 8):
            part = table_ref[head, 8 * group : 8 * group + 8, :]
            total = total + pltpu.roll(part, width - 8 * group, 1)
        for bit in (1, 2, 4):
            total = jnp.where((sub & bit) != 0, pltpu.roll(total, width - bit, 1), total)
        strip_ref[0, head : head + 1, :] = jnp.sum(total, axis=0, keepdims=True)


def spread_body(
    place_ref, x_ref, dq_ref, dk_ref, dv_ref, qkv_ref, send_ref, own_ref, dgain_ref
):
    step = pl.program_id(0)
    width = dq_ref.shape[1]
    unit, _ = rms_parts(x_ref[...].astype(HIGH))
    d_normed = (
        matmul_nt(dq_ref[...], qkv_ref[:, :width])
        + matmul_nt(dk_ref[...], qkv_ref[:, width : 2 * width])
        + matmul_nt(dv_ref[...], qkv_ref[:, 2 * width :])
    )
    d_gain = jnp.sum(d_normed * unit, axis=0, keepdims=True)

    @pl.when(step == 0)
    def _():
        dgain_ref[...] = d_gain

    @pl.when(step != 0)
    def _():
        dgain_ref[...] += d_gain

    @pl.when(step < pl.num_programs(0) // 2)
    def _():
        send_ref[...] = d_normed.astype(LOW)

    @pl.when(step >= pl.num_programs(0) // 2)
    def _():
        own_ref[...] = d_normed


def finish_body(x_ref, own_ref, other_ref, datt_ref, gain_ref, out_ref):
    unit, scale = rms_parts(x_ref[...].astype(HIGH))
    d_normed = own_ref[...] + other_ref[...].astype(HIGH)
    out_ref[...] = (datt_ref[...] + rms_back(d_normed, unit, scale, gain_ref[...])).astype(LOW)


def flat_left(left):
    return left.reshape(-1, left.shape[-1])


def weight_grads(first, second, columns, micros):
    left0, right0, at0, count0 = first
    left1, right1, at1, count1 = second
    left0, left1 = flat_left(left0), flat_left(left1)
    height, depth = left0.shape
    steps = count0 + count1
    half_spec = pl.BlockSpec((height // 2, columns), lambda i: (0, i))
    return call(
        functools.partial(grads_body, count0),
        (steps,),
        [
            whole((height, depth)),
            whole((height, depth)),
            pl.BlockSpec((depth, columns), lambda i: (0, at0 + jnp.minimum(i, count0 - 1))),
            pl.BlockSpec((depth, columns), lambda i: (0, at1 + jnp.maximum(i - count0, 0))),
        ],
        [half_spec, half_spec],
        [shaped((height // 2, steps * columns), LOW)] * 2,
        micros=micros,
    )(left0, left1, right0, right1)


def weight_grads_one(left, right, columns, steps, micros):
    left = flat_left(left)
    height, depth = left.shape
    half_spec = pl.BlockSpec((height // 2, columns), lambda i: (0, i))
    return call(
        grads_one_body,
        (steps,),
        [whole((height, depth)), pl.BlockSpec((depth, columns), lambda i: (0, i))],
        [half_spec, half_spec],
        [shaped((height // 2, steps * columns), LOW)] * 2,
        micros=micros,
    )(left, right)


def on_core_pair(
    tokens,
    cotangent,
    gain_attn,
    w_query,
    w_key,
    w_value,
    w_out,
    rel_table,
    buckets,
    gain_ffn,
    w_gate,
    w_up,
    w_down,
):
    own_rows, features = tokens.shape
    seq_len = 2 * own_rows
    width = w_query.shape[1]
    units = w_gate.shape[1]
    chunk = units // 2
    pairs = width // LANES
    bucket_count, head_count = rel_table.shape
    local_heads = head_count // 2
    count = lax.axis_size("dp")
    far_bit, y_bit, x_bit = dp_place()
    me = lax.axis_index("mp")
    place = jnp.stack([y_bit, x_bit, me, far_bit]).astype(jnp.int32)
    rows = MXU_ROWS
    steps = seq_len // rows
    half_steps = steps // 2
    block_rows = w_query.shape[0]

    def swapped(array):
        return lax.ppermute(array, "mp", [(0, 1), (1, 0)])

    def in_order(array, other):
        first = jnp.where(me == 0, array, other)
        second = jnp.where(me == 0, other, array)
        return jnp.concatenate([first, second], axis=0)

    early = jnp.concatenate([w_query, w_key, w_value, w_out.T], axis=1)
    late = jnp.concatenate([w_gate, w_up, w_down.T], axis=1)
    early_pieces = far_pieces(early)
    x_other, g_other = swapped(tokens), swapped(cotangent)
    late_pieces = far_pieces(late)
    early_pieces = together(*early_pieces)
    near = far_stack(early, list(early_pieces))
    qk = near[:, : 2 * width]
    vo = near[:, 2 * width :]
    qk_next, vo_next = together(over_y(qk), over_x(vo))
    qk_own = in_bit_order(qk, qk_next, y_bit)
    vo_own = in_bit_order(vo, vo_next, x_bit)
    qk_other = over_x(qk_own)
    vo_other = over_y(vo_own)
    x_all = in_order(tokens, x_other)
    g_all = in_order(cotangent, g_other)
    qk_other, vo_other, x_all, g_all, *late_pieces = together(
        qk_other, vo_other, x_all, g_all, *late_pieces
    )
    near = far_stack(late, late_pieces)
    gu = near[:, : 3 * chunk]
    ud = near[:, 3 * chunk :]
    gu_next = over_y(gu)
    ud_next = over_x(ud)

    gain_a = gain_attn.reshape(1, features)
    gain_f = gain_ffn.reshape(1, features)

    one_hot = (buckets[:, None] == jnp.arange(bucket_count, dtype=jnp.int32)[None, :]).astype(HIGH)
    one_hot = jnp.pad(one_hot, ((1, 0), (0, 0)))
    my_table = lax.dynamic_slice_in_dim(rel_table, me * local_heads, local_heads, 1)
    strip = lax.dot_general(my_table, one_hot, (((0,), (1,)), ((), ())), precision=precise)
    strip = strip.reshape(pairs, 2, 2 * seq_len)

    def row_block(columns):
        return pl.BlockSpec((rows, columns), lambda i, *_: (i, 0))

    turned_shape = (2, 2, 2, 2, block_rows)
    turned_block = pl.BlockSpec(turned_shape + (rows,), lambda i, *_: (0, 0, 0, 0, 0, i))
    turned = shaped(turned_shape + (seq_len,), LOW)
    full_block = (count // 4, 2, 2, block_rows, 2 * width)
    half_block = (features // 2, 2 * width)
    normed_x_turned, normed_y_turned, queries, keys, values, w_qkv, w_o = call(
        project_body,
        (steps,),
        [row_block(features), whole((1, features))] + [whole(half_block)] * 4,
        [turned_block, turned_block]
        + [row_block(width)] * 3
        + [result((features, 3 * width)), result((features, width))],
        [turned, turned]
        + [shaped((seq_len, width), LOW)] * 3
        + [shaped((features, 3 * width), LOW), shaped((features, width), LOW)],
        [pltpu.VMEM(full_block, LOW), pltpu.VMEM(full_block, LOW)],
        prefetch=1,
        micros=7,
    )(place, x_all, gain_a, qk_own, qk_other, vo_own, vo_other)

    gu_next, ud_next, queries = together(gu_next, ud_next, queries)
    gu_own = in_bit_order(gu, gu_next, y_bit)
    ud_own = in_bit_order(ud, ud_next, x_bit)
    gu_other = over_x(gu_own)
    ud_other = over_y(ud_own)

    pair_block = pl.BlockSpec((seq_len, LANES), lambda p: (0, p))
    e_block = pl.BlockSpec((2, seq_len, seq_len), lambda p: (p, 0, 0))
    strip_block = pl.BlockSpec((1, 2, 2 * seq_len), lambda p: (p, 0, 0))
    table_scratch = pltpu.VMEM((2, rows, 2 * seq_len), HIGH)
    weights_e, mixed, mixed_low, inverse, part0, part1 = call(
        attend_body,
        (pairs,),
        [
            pair_block,
            pair_block,
            pair_block,
            strip_block,
            pl.BlockSpec((features, LANES), lambda p: (0, p)),
        ],
        [e_block, pair_block, pair_block, pair_block] + [result((own_rows, features))] * 2,
        [
            shaped((2 * pairs, seq_len, seq_len), LOW),
            shaped((seq_len, width), HIGH),
            shaped((seq_len, width), LOW),
            shaped((seq_len, width), HIGH),
            shaped((own_rows, features), LOW),
            shaped((own_rows, features), LOW),
        ],
        [table_scratch, pltpu.VMEM((seq_len, features), HIGH)],
        micros=20,
    )(queries, keys, values, strip, w_o)
    gu_other, ud_other, came0, came1 = together(
        gu_other, ud_other, swapped(part0), swapped(part1)
    )
    parts = (part0, part1, came0, came1)

    def moved(i, m):
        return (i + half_steps * (1 - m[2])) % steps

    def turned_row(columns):
        return pl.BlockSpec((rows, columns), lambda i, m: (moved(i, m), 0))

    half0_row = pl.BlockSpec(
        (rows, features), lambda i, m: (jnp.minimum(moved(i, m), half_steps - 1), 0)
    )
    half1_row = pl.BlockSpec(
        (rows, features), lambda i, m: (jnp.maximum(moved(i, m) - half_steps, 0), 0)
    )
    attended_rows = [turned_row(features)] + [half0_row, half1_row] * 2
    moved_block = pl.BlockSpec(
        turned_shape + (rows,), lambda i, m: (0, 0, 0, 0, 0, moved(i, m))
    )
    send_row = pl.BlockSpec((rows, features), lambda i, m: (jnp.minimum(i, half_steps - 1), 0))
    keep_row = pl.BlockSpec((rows, features), lambda i, m: (jnp.maximum(i - half_steps, 0), 0))
    full_block = (count // 4, 2, 2, block_rows, 3 * chunk)
    half_block = (features // 2, 3 * chunk)
    feed_x_turned, feed_y_turned, g_turned, hidden, d_gate_up, dn_part, out_send, out_own = call(
        feed_body,
        (steps,),
        attended_rows
        + [turned_row(features), whole((1, features))]
        + [whole(half_block)] * 4,
        [
            moved_block,
            moved_block,
            moved_block,
            turned_row(units),
            turned_row(2 * units),
            turned_row(features),
            send_row,
            keep_row,
        ],
        [
            turned,
            turned,
            turned,
            shaped((seq_len, units), LOW),
            shaped((seq_len, 2 * units), LOW),
            shaped((seq_len, features), LOW),
            shaped((own_rows, features), LOW),
            shaped((own_rows, features), HIGH),
        ],
        [pltpu.VMEM(full_block, LOW), pltpu.VMEM(full_block, LOW)],
        prefetch=1,
        micros=19,
    )(place, x_all, *parts, g_all, gain_f, gu_own, gu_other, ud_own, ud_other)
    dn_other = swapped(dn_part)

    gu_own, gu_send = weight_grads_one(feed_x_turned, d_gate_up, 3 * chunk // 2, 2, 5.5)
    gu_send, hidden, dn_other = together(gu_send, hidden, dn_other)
    gu_came = over_x(gu_send)
    ud_own, ud_send = weight_grads(
        (feed_y_turned, d_gate_up, 3, 1), (g_turned, hidden, 0, 2), chunk, 6.5
    )
    ud_send, dn_other = together(ud_send, dn_other)
    ud_came = over_y(ud_send)

    d_attended, d_low_turned, d_mixed, d_gain_f = call(
        turn_body,
        (steps,),
        attended_rows
        + [turned_row(features)] * 3
        + [whole((1, features)), whole((features, width))],
        [keep_row, moved_block, turned_row(width), result((1, features))],
        [
            shaped((own_rows, features), HIGH),
            turned,
            shaped((seq_len, width), LOW),
            shaped((1, features), HIGH),
        ],
        prefetch=1,
        micros=4,
    )(place, x_all, *parts, g_all, dn_part, dn_other, gain_f, w_o)
    out_other = swapped(out_send)

    d_query, d_key, d_value, d_strip = call(
        backward_body,
        (pairs,),
        [pair_block, pair_block, pair_block, e_block, pair_block, pair_block, pair_block],
        [pair_block, pair_block, pair_block, strip_block],
        [shaped((seq_len, width), LOW)] * 3 + [shaped((pairs, 2, 2 * seq_len), HIGH)],
        [table_scratch, pltpu.VMEM((LANES, seq_len), HIGH), pltpu.VMEM((LANES, seq_len), HIGH)],
        micros=4,
    )(queries, keys, values, weights_e, d_mixed, mixed, inverse)

    gu_came, ud_came, out_other, d_query, d_key, d_value, d_strip = together(
        gu_came, ud_came, out_other, d_query, d_key, d_value, d_strip
    )

    def next_half(own, came, bit):
        return (
            add_low(part_of(own, bit, 2), part_of(came, bit, 2)),
            add_low(part_of(own, 1 - bit, 2), part_of(came, 1 - bit, 2)),
        )

    gu_own, gu_send = next_half(gu_own, gu_came, y_bit)
    ud_own, ud_send = next_half(ud_own, ud_came, x_bit)
    gu_came = over_y(gu_send)
    ud_came = over_x(ud_send)

    qk_own, qk_send = weight_grads(
        (normed_x_turned, d_query, 0, 1), (normed_x_turned, d_key, 0, 1), width, 5
    )
    qk_send, d_value = together(qk_send, d_value)
    vo_own, vo_send = weight_grads(
        (normed_y_turned, d_value, 0, 1), (d_low_turned, mixed_low, 0, 1), width, 5
    )
    output = (out_own + out_other.astype(HIGH)).astype(LOW)

    gu_came, ud_came, qk_send, vo_send, d_query = together(
        gu_came, ud_came, qk_send, vo_send, d_query
    )
    qk_came = over_x(qk_send)
    vo_came = over_y(vo_send)
    gu_own, gu_send = next_half(gu_own, gu_came, far_bit % 2)
    ud_own, ud_send = next_half(ud_own, ud_came, far_bit % 2)
    unit_own = jnp.concatenate([gu_own, ud_own], axis=1)
    unit_send = jnp.concatenate([gu_send, ud_send], axis=1)
    unit_came = over_far_bit(unit_send, 0)

    dna_send, dna_own, d_gain_a = call(
        spread_body,
        (steps,),
        [turned_row(features)] + [turned_row(width)] * 3 + [whole((features, 3 * width))],
        [send_row, keep_row, result((1, features))],
        [
            shaped((own_rows, features), LOW),
            shaped((own_rows, features), HIGH),
            shaped((1, features), HIGH),
        ],
        prefetch=1,
        micros=7,
    )(place, x_all, d_query, d_key, d_value, w_qkv)
    qk_came, vo_came, unit_came, dna_send, d_gain_a, d_strip = together(
        qk_came, vo_came, unit_came, dna_send, d_gain_a, d_strip
    )
    unit_own, unit_send = next_half(unit_own, unit_came, far_bit // 2)
    unit_came = over_far_bit(unit_send, 1)
    dna_other = swapped(dna_send)
    qk_own, qk_send = next_half(qk_own, qk_came, y_bit)
    vo_own, vo_send = next_half(vo_own, vo_came, x_bit)
    qk_came = over_y(qk_send)
    vo_came = over_x(vo_send)

    d_bias = d_strip.reshape(local_heads, 2 * seq_len)
    my_d_table = lax.dot_general(one_hot, d_bias, (((0,), (1,)), ((), ())), precision=precise)
    d_table = lax.dynamic_update_slice_in_dim(
        jnp.zeros_like(rel_table), my_d_table, me * local_heads, 1
    )
    small_early = jnp.concatenate([0.5 * d_gain_f, d_table.reshape(1, -1)], axis=1)
    small_early = jnp.pad(small_early, ((0, 0), (0, -(features + small_early.shape[1]) % (4 * width))))
    small = jnp.concatenate([d_gain_a, small_early], axis=1)
    small = small.reshape(-1, 4 * width)
    small = small + swapped(small)
    small = small + over_x(small) + over_y(small) + over_xy(small)

    d_tokens = call(
        finish_body,
        (half_steps,),
        [row_block(features)] * 4 + [whole((1, features))],
        row_block(features),
        shaped((own_rows, features), LOW),
        micros=3.5,
    )(tokens, dna_own, dna_other, d_attended, gain_a)

    qk_came, vo_came, unit_came, d_tokens, small = together(
        qk_came, vo_came, unit_came, d_tokens, small
    )
    head_own = jnp.concatenate([qk_own, vo_own], axis=-1)
    head_came = jnp.concatenate([qk_came, vo_came], axis=-1)
    total = add_low(head_own, head_came)

    def far_part(far):
        return part_of(total, 2 * (far % 2) + far // 2, 4)

    small_rows = in_terms(small)
    pieces = [
        over_far(jnp.concatenate([far_part((far_bit + k) % 4), small_rows], axis=0), k)
        for k in range(1, 4)
    ]
    small = sum((from_terms(piece[block_rows:], small.shape[0]) for piece in pieces), small)
    small = small.reshape(-1)
    pieces = [piece[:block_rows] for piece in pieces]
    grads_head = sum((piece.astype(HIGH) for piece in pieces), far_part(far_bit).astype(HIGH))
    grads_qk, grads_vo = grads_head[:, : 2 * width], grads_head[:, 2 * width :]
    grads_unit = unit_own.astype(HIGH) + unit_came.astype(HIGH)
    return (
        output,
        d_tokens,
        small[:features],
        grads_qk[:, :width],
        grads_qk[:, width:],
        grads_vo[:, :width],
        grads_vo[:, width:].T,
        small[2 * features : 2 * features + rel_table.size].reshape(rel_table.shape),
        small[features : 2 * features],
        grads_unit[:, :units],
        grads_unit[:, units : 2 * units],
        grads_unit[:, 2 * units :].T,
    )


def solution(mesh):
    placed = (
        P(("dp", "mp"), None),
        P(("dp", "mp"), None),
        P(),
        P("dp", "mp"),
        P("dp", "mp"),
        P("dp", "mp"),
        P("mp", "dp"),
        P(),
        P(),
        P(),
        P("dp", "mp"),
        P("dp", "mp"),
        P("mp", "dp"),
    )
    paired = mesh.shape["mp"] == 2 and mesh.shape["dp"] == 16
    body = on_core_pair if paired else on_device
    return jax.shard_map(
        body,
        mesh=mesh,
        in_specs=placed,
        out_specs=(
            P(("dp", "mp"), None),
            P(("dp", "mp"), None),
            P(),
            P("dp", "mp"),
            P("dp", "mp"),
            P("dp", "mp"),
            P("mp", "dp"),
            P(),
            P(),
            P("dp", "mp"),
            P("dp", "mp"),
            P("mp", "dp"),
        ),
        check_vma=False,
    )
```

```python
import functools

import jax
import jax.numpy as jnp
from jax import lax
from jax.experimental import pallas as pl
from jax.experimental.pallas import tpu as pltpu
from jax.sharding import PartitionSpec as P

epsilon = 1e-06
block_limit = 512
precise = lax.Precision.HIGHEST


def as_sent(array):

    def short(part):
        return part.astype(jnp.bfloat16) if part.dtype == jnp.float32 else part

    return jax.tree.map(short, array)


def matmul_nn(left, right):
    return jnp.dot(left, right, preferred_element_type=jnp.float32)


def matmul_nt(left, right):
    return lax.dot_general(
        left, right, (((1,), (1,)), ((), ())), preferred_element_type=jnp.float32
    )


def matmul_tn(left, right):
    return lax.dot_general(
        left, right, (((0,), (0,)), ((), ())), preferred_element_type=jnp.float32
    )


def rms_parts(inputs):
    scale = lax.rsqrt(jnp.mean(inputs * inputs, axis=-1, keepdims=True) + epsilon)
    return (inputs * scale, scale)


def rms_back(d_normed, unit, scale, gain):
    d_unit = d_normed * gain
    return scale * (d_unit - unit * jnp.mean(d_unit * unit, axis=-1, keepdims=True))


def gated(gate_pre, up_pre):
    return jax.nn.gelu(gate_pre, approximate=True) * up_pre


def window_base(first_query, first_key, row_count, seq_len):
    return first_key - first_query - row_count + seq_len


def make_bias(bias_full, base, row_count, width):
    span = width + row_count - 1
    head_count = bias_full.shape[0]
    strip = lax.dynamic_slice_in_dim(bias_full, base, span, 1)
    tiled = jnp.tile(strip, (1, row_count + 1))
    window = tiled[:, row_count - 1 : row_count - 1 + row_count * (span - 1)]
    return window.reshape(head_count, row_count, span - 1)[:, :, :width]


def skew_sum(d_block, row_count, width):
    head_count = d_block.shape[0]
    span = width + row_count - 1
    padded = jnp.pad(d_block, ((0, 0), (0, 0), (row_count - 1, 0)))
    flat = padded.reshape(head_count, row_count * span)
    flat = jnp.pad(flat, ((0, 0), (0, row_count)))
    skewed = flat.reshape(head_count, row_count, span + 1)[:, :, :span]
    return jnp.sum(skewed, axis=1)


def add_window(d_bias, piece, base):
    current = lax.dynamic_slice_in_dim(d_bias, base, piece.shape[1], 1)
    return lax.dynamic_update_slice_in_dim(d_bias, current + piece, base, 1)


def sum_rows(partial_value):
    return lax.psum_scatter(
        partial_value.astype(jnp.bfloat16), "mp", scatter_dimension=0, tiled=True
    ).astype(jnp.float32)


def split_heads(queries, keys_all, values, head_count):
    row_count = queries.shape[0]
    seq_len = keys_all.shape[0]
    head_dim = queries.shape[1] // head_count
    width = min(block_limit, seq_len)
    blocks = seq_len // width
    heads_q = queries.reshape(row_count, head_count, head_dim)
    heads_k = keys_all.reshape(blocks, width, head_count, head_dim)
    heads_v = values.reshape(blocks, width, head_count, head_dim)
    starts = jnp.arange(blocks, dtype=jnp.int32) * width
    return (heads_q, heads_k, heads_v, starts, width)


def attend_forward(queries, keys_all, values, bias_full, head_count, first_row):
    row_count = queries.shape[0]
    seq_len = keys_all.shape[0]
    heads_q, heads_k, heads_v, starts, width = split_heads(queries, keys_all, values, head_count)

    def block_scores(key_block, first_key):
        raw_scores = jnp.einsum(
            "qhd,khd->hqk", heads_q, key_block, preferred_element_type=jnp.float32
        )
        base = window_base(first_row, first_key, row_count, seq_len)
        return raw_scores + make_bias(bias_full, base, row_count, width)

    def stats_step(running, pieces):
        top_now, total = running
        scores = block_scores(pieces[0], pieces[1])
        top_new = jnp.maximum(top_now, jnp.max(scores, axis=-1))
        total = total * jnp.exp(top_now - top_new) + jnp.sum(
            jnp.exp(scores - top_new[..., None]), axis=-1
        )
        return ((top_new, total), None)

    start_top = jnp.full((head_count, row_count), -jnp.inf, jnp.float32)
    start_total = jnp.zeros((head_count, row_count), jnp.float32)
    (top_all, total), _ = lax.scan(stats_step, (start_top, start_total), (heads_k, starts))
    log_total = top_all + jnp.log(total)

    def mix_step(running, pieces):
        scores = block_scores(pieces[0], pieces[2])
        probs_low = jnp.exp(scores - log_total[..., None]).astype(jnp.bfloat16)
        update = jnp.einsum(
            "hqk,khd->qhd", probs_low, pieces[1], preferred_element_type=jnp.float32
        )
        return (running + update, None)

    start_mix = jnp.zeros(heads_q.shape, jnp.float32)
    mixed_f, _ = lax.scan(mix_step, start_mix, (heads_k, heads_v, starts))
    return (mixed_f.reshape(row_count, queries.shape[1]), log_total)


def attend_backward(
    queries, keys_all, values, bias_full, head_count, first_row, log_total, deltas, d_mixed
):
    row_count = queries.shape[0]
    seq_len = keys_all.shape[0]
    heads_q, heads_k, heads_v, starts, width = split_heads(queries, keys_all, values, head_count)
    heads_d = d_mixed.reshape(heads_q.shape)

    def back_step(running, pieces):
        d_query, d_bias = running
        key_block, value_block, first_key = pieces
        base = window_base(first_row, first_key, row_count, seq_len)
        scores = jnp.einsum("qhd,khd->hqk", heads_q, key_block, preferred_element_type=jnp.float32)
        scores = scores + make_bias(bias_full, base, row_count, width)
        probs = jnp.exp(scores - log_total[..., None])
        d_probs = jnp.einsum(
            "qhd,khd->hqk", heads_d, value_block, preferred_element_type=jnp.float32
        )
        d_scores = (probs * (d_probs - deltas[..., None])).astype(jnp.bfloat16)
        d_query = d_query + jnp.einsum(
            "hqk,khd->qhd", d_scores, key_block, preferred_element_type=jnp.float32
        )
        d_bias = add_window(d_bias, skew_sum(d_scores.astype(jnp.float32), row_count, width), base)
        probs_low = probs.astype(jnp.bfloat16)
        d_value = jnp.einsum("hqk,qhd->khd", probs_low, heads_d, preferred_element_type=jnp.float32)
        d_key = jnp.einsum("hqk,qhd->khd", d_scores, heads_q, preferred_element_type=jnp.float32)
        return ((d_query, d_bias), (d_key, d_value))

    start_query = jnp.zeros(heads_q.shape, jnp.float32)
    (d_query, d_bias), kv_parts = lax.scan(
        back_step, (start_query, jnp.zeros_like(bias_full)), (heads_k, heads_v, starts)
    )
    feature_count = queries.shape[1]
    d_query = d_query.reshape(row_count, feature_count)
    return (
        d_query,
        d_bias,
        kv_parts[0].reshape(seq_len, feature_count),
        kv_parts[1].reshape(seq_len, feature_count),
    )


def on_device(
    tokens,
    cotangent,
    gain_attn,
    w_query,
    w_key,
    w_value,
    w_out,
    rel_table,
    buckets,
    gain_ffn,
    w_gate,
    w_up,
    w_down,
):
    head_count = rel_table.shape[1]
    bucket_count = rel_table.shape[0]
    inputs = tokens.astype(jnp.float32)
    row_count = inputs.shape[0]
    feature_count = inputs.shape[1]
    first_row = lax.axis_index("mp") * row_count
    attn_parts = (w_query, w_key, w_value, w_out.T)
    ffn_parts = (w_gate, w_up, w_down.T)
    ffn_cols = ()
    col_parts = lax.all_gather(as_sent(attn_parts + ffn_cols), "mp", axis=1, tiled=True)
    full_parts = lax.all_gather(as_sent(tuple(col_parts) + ffn_parts), "dp", axis=0, tiled=True)
    query_full, key_full, value_full, out_full, gate_full, up_full, down_full = full_parts
    unit_a, scale_a = rms_parts(inputs)
    normed_a = (unit_a * gain_attn).astype(jnp.bfloat16)
    queries = matmul_nn(normed_a, query_full).astype(jnp.bfloat16)
    own_keys = matmul_nn(normed_a, key_full).astype(jnp.bfloat16)
    own_values = matmul_nn(normed_a, value_full).astype(jnp.bfloat16)
    keys_all, values = (
        lax.all_gather(own_keys, "mp", axis=0, tiled=True),
        lax.all_gather(own_values, "mp", axis=0, tiled=True),
    )
    one_hot = (buckets[:, None] == jnp.arange(bucket_count, dtype=jnp.int32)[None, :]).astype(
        jnp.float32
    )
    bias_full = jnp.dot(one_hot, rel_table, precision=precise).T
    mixed_f, log_total = attend_forward(queries, keys_all, values, bias_full, head_count, first_row)
    mixed_out = mixed_f.astype(jnp.bfloat16)
    attended = inputs + matmul_nt(mixed_out, out_full)
    unit_f, scale_f = rms_parts(attended)
    normed_f = (unit_f * gain_ffn).astype(jnp.bfloat16)
    normed_seq, cot_seq = (
        lax.all_gather(normed_f, "mp", axis=0, tiled=True),
        lax.all_gather(cotangent, "mp", axis=0, tiled=True),
    )
    gate_pre = matmul_nn(normed_seq, gate_full)
    up_pre = matmul_nn(normed_seq, up_full)
    hidden = gated(gate_pre, up_pre).astype(jnp.bfloat16)
    output = attended + sum_rows(matmul_nt(hidden, down_full))
    d_hidden = matmul_nn(cot_seq, down_full)
    d_down = matmul_tn(cot_seq, hidden)
    _, pull_gate = jax.vjp(gated, gate_pre, up_pre)
    d_gate, d_up = pull_gate(d_hidden)
    d_gate = d_gate.astype(jnp.bfloat16)
    d_up = d_up.astype(jnp.bfloat16)
    d_normed_f = sum_rows(matmul_nt(d_gate, gate_full) + matmul_nt(d_up, up_full))
    d_gate_w = matmul_tn(normed_seq, d_gate)
    d_up_w = matmul_tn(normed_seq, d_up)
    d_gain_f = jnp.sum(d_normed_f * unit_f, axis=0)
    d_attended = cotangent.astype(jnp.float32) + rms_back(d_normed_f, unit_f, scale_f, gain_ffn)
    d_att_low = d_attended.astype(jnp.bfloat16)
    d_out_w = matmul_tn(d_att_low, mixed_out)
    d_mixed = matmul_nn(d_att_low, out_full).astype(jnp.bfloat16)
    head_dim = feature_count // head_count
    deltas = jnp.sum(
        (d_mixed.astype(jnp.float32) * mixed_f).reshape(row_count, head_count, head_dim), axis=-1
    ).T
    d_query, d_bias, d_keys_part, d_values_part = attend_backward(
        queries, keys_all, values, bias_full, head_count, first_row, log_total, deltas, d_mixed
    )
    d_keys_own, d_values_own = (
        lax.psum_scatter(
            d_keys_part.astype(jnp.bfloat16), "mp", scatter_dimension=0, tiled=True
        ).astype(jnp.float32),
        lax.psum_scatter(
            d_values_part.astype(jnp.bfloat16), "mp", scatter_dimension=0, tiled=True
        ).astype(jnp.float32),
    )
    d_keys_own = d_keys_own.astype(jnp.bfloat16)
    d_values_own = d_values_own.astype(jnp.bfloat16)
    d_query = d_query.astype(jnp.bfloat16)
    d_normed_a = (
        matmul_nt(d_query, query_full)
        + matmul_nt(d_keys_own, key_full)
        + matmul_nt(d_values_own, value_full)
    )
    d_query_w = matmul_tn(normed_a, d_query)
    d_key_w = matmul_tn(normed_a, d_keys_own)
    d_value_w = matmul_tn(normed_a, d_values_own)
    d_gain_a = jnp.sum(d_normed_a * unit_a, axis=0)
    d_tokens = (d_attended + rms_back(d_normed_a, unit_a, scale_a, gain_attn)).astype(jnp.bfloat16)
    d_table = jnp.dot(d_bias, one_hot, precision=precise).T
    row_grads = (
        lax.psum_scatter(
            d_query_w.astype(jnp.bfloat16), "dp", scatter_dimension=0, tiled=True
        ).astype(jnp.float32),
        lax.psum_scatter(
            d_key_w.astype(jnp.bfloat16), "dp", scatter_dimension=0, tiled=True
        ).astype(jnp.float32),
        lax.psum_scatter(
            d_value_w.astype(jnp.bfloat16), "dp", scatter_dimension=0, tiled=True
        ).astype(jnp.float32),
        lax.psum_scatter(
            d_out_w.astype(jnp.bfloat16), "dp", scatter_dimension=0, tiled=True
        ).astype(jnp.float32),
        lax.psum_scatter(
            d_gate_w.astype(jnp.bfloat16), "dp", scatter_dimension=0, tiled=True
        ).astype(jnp.float32),
        lax.psum_scatter(d_up_w.astype(jnp.bfloat16), "dp", scatter_dimension=0, tiled=True).astype(
            jnp.float32
        ),
        lax.psum_scatter(d_down.astype(jnp.bfloat16), "dp", scatter_dimension=0, tiled=True).astype(
            jnp.float32
        ),
    )
    row_grads = tuple(row_grads)
    ffn_late = ()
    col_grads = tuple(
        jax.tree.map(
            lambda part: part.astype(jnp.float32),
            lax.psum_scatter(
                as_sent(row_grads[:4] + ffn_late), "mp", scatter_dimension=1, tiled=True
            ),
        )
    )
    ffn_done = row_grads[4:]
    small_sums = lax.psum((d_gain_a, d_gain_f, d_table), ("dp", "mp"))
    return (
        output.astype(jnp.bfloat16),
        d_tokens,
        small_sums[0],
        col_grads[0],
        col_grads[1],
        col_grads[2],
        col_grads[3].T,
        small_sums[2],
        small_sums[1],
        ffn_done[0],
        ffn_done[1],
        ffn_done[2].T,
    )


MXU_ROWS = 256
LANES = 128
VMEM_LIMIT = 56 * 2**20
PEAK_PER_MICRO = 1_153_500_000
LOW = jnp.bfloat16
HIGH = jnp.float32


def call(
    body, grid, in_specs, out_specs, out_shape, scratch=(), prefetch=0, micros=5, aliases=None
):
    return pl.pallas_call(
        body,
        grid_spec=pltpu.PrefetchScalarGridSpec(
            num_scalar_prefetch=prefetch,
            grid=grid,
            in_specs=in_specs,
            out_specs=out_specs,
            scratch_shapes=list(scratch),
        ),
        out_shape=out_shape,
        input_output_aliases=aliases or {},
        compiler_params=pltpu.CompilerParams(vmem_limit_bytes=VMEM_LIMIT),
        cost_estimate=pl.CostEstimate(
            flops=int(micros * PEAK_PER_MICRO), bytes_accessed=0, transcendentals=0
        ),
    )


def shaped(shape, dtype):
    return jax.ShapeDtypeStruct(shape, dtype)


def whole(shape):
    return pl.BlockSpec(shape, lambda *_: (0,) * len(shape), pipeline_mode=pl.Buffered(1))


def result(shape):
    return pl.BlockSpec(shape, lambda *_: (0,) * len(shape))


def together(*arrays):
    return lax.optimization_barrier(arrays)


def ring_shift(steps, count):
    return [(i, (i + steps) % count) for i in range(count)]


def flip(bit, count):
    return [(i, i ^ bit) for i in range(count)]


def over_x(array):
    return lax.ppermute(array, "dp", flip(1, lax.axis_size("dp")))


def over_y(array):
    return lax.ppermute(array, "dp", flip(2, lax.axis_size("dp")))


def over_xy(array):
    return lax.ppermute(array, "dp", flip(3, lax.axis_size("dp")))


def over_far(array, steps):
    return lax.ppermute(array, "dp", ring_shift(4 * steps, lax.axis_size("dp")))


def dp_place():
    index = lax.axis_index("dp")
    return (index // 4, (index // 2) % 2, index % 2)


def in_bit_order(own, other, bit):
    first = jnp.where(bit == 0, own, other)
    second = jnp.where(bit == 0, other, own)
    return jnp.concatenate([first, second], axis=0)


def far_pieces(shard):
    return [over_far(shard, k) for k in range(1, lax.axis_size("dp") // 4)]


def far_stack(shard, pieces):
    far = len(pieces) + 1
    place = dp_place()[0]
    stacked = jnp.zeros((far,) + shard.shape, shard.dtype)
    for k, piece in enumerate([shard] + pieces):
        stacked = lax.dynamic_update_slice(stacked, piece[None], ((place - k) % far, 0, 0))
    return stacked.reshape(-1, shard.shape[1])


def over_far_bit(array, bit):
    return lax.ppermute(array, "dp", flip(4 << bit, lax.axis_size("dp")))


def part_of(array, index, parts):
    size = array.shape[0] // parts
    return lax.dynamic_slice_in_dim(array, index * size, size, 0)


def add_low(left, right):
    return (left.astype(HIGH) + right.astype(HIGH)).astype(LOW)


def in_terms(array):
    terms, rest = [], array
    for _ in range(3):
        term = lax.optimization_barrier(rest.astype(LOW))
        terms.append(term)
        rest = rest - term.astype(HIGH)
    rows = jnp.concatenate(terms, axis=0)
    return jnp.pad(rows, ((0, -rows.shape[0] % 8), (0, 0)))


def from_terms(rows, height):
    return sum(rows[i * height : (i + 1) * height].astype(HIGH) for i in range(3))


def head_masks(dtype):
    lane = lax.broadcasted_iota(jnp.int32, (1, LANES), 1)
    first = (lane < LANES // 2).astype(HIGH)
    return (first.astype(dtype), (1.0 - first).astype(dtype))


def put_weights(full_ref, own_ref, other_ref, y_first, bit):
    far, rows = full_ref.shape[0], full_ref.shape[3]
    for half_ref, at in ((own_ref, bit), (other_ref, 1 - bit)):
        for near in range(2):
            for place in range(far):
                start = (near * far + place) * rows
                block = half_ref[start : start + rows, :]
                if y_first:
                    full_ref[place, near, at] = block
                else:
                    full_ref[place, at, near] = block


def put_turned(turned_ref, array, x_first, bit, lanes=slice(None)):
    rows = turned_ref.shape[4]
    turned = array.T
    for block in range(turned.shape[0] // rows):
        far, y_bit, x_bit = block // 4, (block // 2) % 2, block % 2
        first, second = (x_bit, y_bit) if x_first else (y_bit, x_bit)
        other = 1 - bit if first else bit
        turned_ref[other, second, far % 2, far // 2, :, lanes] = turned[
            block * rows : (block + 1) * rows
        ]


def matrix(full_ref, start, columns):
    part = full_ref[:, :, :, :, start : start + columns]
    return part.reshape(-1, columns)


def project_body(
    place_ref,
    x_ref,
    gain_ref,
    qk_own_ref,
    qk_other_ref,
    vo_own_ref,
    vo_other_ref,
    turned_x_ref,
    turned_y_ref,
    q_ref,
    k_ref,
    v_ref,
    qkv_ref,
    wo_ref,
    qk_ref,
    vo_ref,
):
    width = q_ref.shape[1]

    @pl.when(pl.program_id(0) == 0)
    def _():
        put_weights(qk_ref, qk_own_ref, qk_other_ref, True, place_ref[1])
        put_weights(vo_ref, vo_own_ref, vo_other_ref, False, place_ref[0])
        qkv_ref[:, : 2 * width] = matrix(qk_ref, 0, 2 * width)
        qkv_ref[:, 2 * width :] = matrix(vo_ref, 0, width)
        wo_ref[...] = matrix(vo_ref, width, width)

    unit, _ = rms_parts(x_ref[...].astype(HIGH))
    normed = (unit * gain_ref[...]).astype(LOW)
    put_turned(turned_x_ref, normed, True, place_ref[1])
    put_turned(turned_y_ref, normed, False, place_ref[0])
    q_ref[...] = matmul_nn(normed, qkv_ref[:, :width]).astype(LOW)
    k_ref[...] = matmul_nn(normed, qkv_ref[:, width : 2 * width]).astype(LOW)
    v_ref[...] = matmul_nn(normed, qkv_ref[:, 2 * width :]).astype(LOW)


def attend_body(
    q_ref, k_ref, v_ref, strip_ref, wo_ref, e_ref, mixed_ref, low_ref, inv_ref, part0_ref, part1_ref, table_ref, acc_ref
):
    pair = pl.program_id(0)
    seq_len = k_ref.shape[0]
    rows = table_ref.shape[1]
    low_masks = head_masks(LOW)
    own_lanes = tuple(mask > 0.5 for mask in head_masks(HIGH))
    for head in range(2):
        row = jnp.broadcast_to(strip_ref[0, head : head + 1, :], (rows, 2 * seq_len))
        table_ref[head] = pltpu.roll(row, 0, 1, stride=1, stride_axis=0)
    keys = k_ref[...]
    values = v_ref[...]
    values_h = tuple(values * low_masks[h] + low_masks[1 - h] for h in range(2))

    @pl.when(pair == 0)
    def _():
        acc_ref[...] = jnp.zeros_like(acc_ref)

    def scored(block, head):
        at = slice(block * rows, (block + 1) * rows)
        raw = matmul_nt(q_ref[at, :] * low_masks[head], keys)
        return raw + table_ref[head, :, seq_len - block * rows : 2 * seq_len - block * rows]

    units = [(block, head) for block in range(seq_len // rows) for head in range(2)]
    ahead = scored(*units[0])
    summed = [None, None]
    for number, (block, head) in enumerate(units):
        at = slice(block * rows, (block + 1) * rows)
        scores = ahead
        if number + 1 < len(units):
            ahead = scored(*units[number + 1])
        top = jnp.max(scores, axis=-1, keepdims=True)
        weights = jnp.exp(scores - top).astype(LOW)
        e_ref[head, at, :] = weights
        summed[head] = matmul_nn(weights, values_h[head])
        if head == 1:
            totals = jnp.where(own_lanes[0], summed[1], summed[0])
            inverse = 1.0 / pltpu.roll(totals, LANES // 2, 1)
            mixed = jnp.where(own_lanes[0], summed[0], summed[1]) * inverse
            mixed_ref[at, :] = mixed
            low_ref[at, :] = mixed.astype(LOW)
            inv_ref[at, :] = inverse
    acc_ref[...] += matmul_nt(low_ref[...], wo_ref[...])

    @pl.when(pair == pl.num_programs(0) - 1)
    def _():
        half = part0_ref.shape[0]
        part0_ref[...] = acc_ref[:half, :].astype(LOW)
        part1_ref[...] = acc_ref[half:, :].astype(LOW)


def summed_halves(left_ref, right_ref):
    return left_ref[...].astype(HIGH) + right_ref[...].astype(HIGH)


def feed_body(
    row_steps,
    place_ref,
    x_ref,
    p0_ref,
    p1_ref,
    r0_ref,
    r1_ref,
    g_ref,
    gain_ref,
    gu_own_ref,
    gu_other_ref,
    ud_own_ref,
    ud_other_ref,
    unit_ref,
    scale_ref,
    dn_ref,
    send_ref,
    own_ref,
    dgu_own_ref,
    dgu_other_ref,
    dud_own_ref,
    dud_other_ref,
    gu_ref,
    ud_ref,
    turned_x_ref,
    turned_y_ref,
    g_turned_ref,
    hidden_ref,
    dgate_up_ref,
):
    step = pl.program_id(0)
    columns = hidden_ref.shape[1] // 2
    pl.when(step < row_steps)(
        functools.partial(
            feed_rows,
            step,
            row_steps,
            place_ref,
            (x_ref, p0_ref, p1_ref, r0_ref, r1_ref, g_ref, gain_ref),
            (gu_own_ref, gu_other_ref, ud_own_ref, ud_other_ref),
            (unit_ref, scale_ref, dn_ref, send_ref, own_ref),
            (gu_ref, ud_ref, turned_x_ref, turned_y_ref, g_turned_ref, hidden_ref, dgate_up_ref),
        )
    )

    def product(left_ref, right, own_out_ref, other_out_ref):
        for half, out_ref in enumerate((own_out_ref, other_out_ref)):
            left = left_ref[half].reshape(out_ref.shape[0], -1)
            out_ref[...] = matmul_nn(left, right).astype(LOW)

    for block in range(6):

        @pl.when(step == row_steps + block)
        def _(block=block):
            if block < 3:
                right = dgate_up_ref[:, block * columns : (block + 1) * columns]
                product(turned_x_ref, right, dgu_own_ref, dgu_other_ref)
            elif block == 3:
                right = dgate_up_ref[:, block * columns : (block + 1) * columns]
                product(turned_y_ref, right, dud_own_ref, dud_other_ref)
            else:
                right = hidden_ref[:, (block - 4) * columns : (block - 3) * columns]
                product(g_turned_ref, right, dud_own_ref, dud_other_ref)


def feed_rows(step, row_steps, place_ref, inputs, weights, outputs, scratch):
    x_ref, p0_ref, p1_ref, r0_ref, r1_ref, g_ref, gain_ref = inputs
    gu_own_ref, gu_other_ref, ud_own_ref, ud_other_ref = weights
    unit_ref, scale_ref, dn_ref, send_ref, own_ref = outputs
    gu_ref, ud_ref, turned_x_ref, turned_y_ref, g_turned_ref, hidden_ref, dgate_up_ref = scratch
    rows = x_ref.shape[0]
    late = (step < row_steps // 2) == (place_ref[2] == 0)
    position = lax.rem(step + (row_steps // 2) * (1 - place_ref[2]), row_steps)
    at = pl.ds(pl.multiple_of(position * rows, rows), rows)

    @pl.when(step == 0)
    def _():
        put_weights(gu_ref, gu_own_ref, gu_other_ref, True, place_ref[1])
        put_weights(ud_ref, ud_own_ref, ud_other_ref, False, place_ref[0])

    attended = x_ref[...].astype(HIGH) + jnp.where(
        late, summed_halves(p1_ref, r1_ref), summed_halves(p0_ref, r0_ref)
    )
    unit, scale = rms_parts(attended)
    normed = (unit * gain_ref[...]).astype(LOW)
    unit_ref[...] = unit.astype(LOW)
    scale_ref[...] = jnp.broadcast_to(scale, scale_ref.shape)
    put_turned(turned_x_ref, normed, True, place_ref[1], at)
    put_turned(turned_y_ref, normed, False, place_ref[0], at)
    cotangent = g_ref[...]
    put_turned(g_turned_ref, cotangent, False, place_ref[0], at)
    root = 0.7978845608028654
    columns = hidden_ref.shape[1] // 2
    products = []
    for part in range(2):
        w_gate = matrix(gu_ref, part * columns, columns)
        w_up = matrix(ud_ref, 0, columns) if part else matrix(gu_ref, 2 * columns, columns)
        w_down = matrix(ud_ref, (1 + part) * columns, columns)
        gate = matmul_nn(normed, w_gate)
        up = matmul_nn(normed, w_up)
        d_hidden = matmul_nn(cotangent, w_down)
        products.append((gate, up, d_hidden, w_gate, w_up, w_down))
    out = 0.0
    d_normed = 0.0
    for part, (gate, up, d_hidden, w_gate, w_up, w_down) in enumerate(products):
        square = gate * gate
        bend = jnp.tanh(gate * (root + (root * 0.044715) * square))
        half = 0.5 + 0.5 * bend
        gelu = gate * half
        slope = half + (0.5 * gate) * (1.0 - bend * bend) * (root + (3 * root * 0.044715) * square)
        hidden = (gelu * up).astype(LOW)
        d_gate = (d_hidden * up * slope).astype(LOW)
        d_up = (d_hidden * gelu).astype(LOW)
        hidden_ref[at, part * columns : (part + 1) * columns] = hidden
        dgate_up_ref[at, part * columns : (part + 1) * columns] = d_gate
        dgate_up_ref[at, (2 + part) * columns : (3 + part) * columns] = d_up
        d_normed = d_normed + matmul_nt(d_gate, w_gate) + matmul_nt(d_up, w_up)
        out = out + matmul_nt(hidden, w_down)
    dn_ref[...] = d_normed.astype(LOW)

    @pl.when(step < row_steps // 2)
    def _():
        send_ref[...] = out.astype(LOW)

    @pl.when(step >= row_steps // 2)
    def _():
        own_ref[...] = attended + out


def grads_body(first_count, left0_ref, left1_ref, right0_ref, right1_ref, own_ref, other_ref):
    step = pl.program_id(0)
    half = own_ref.shape[0]

    def product(left_ref, right_ref):
        right = right_ref[...]
        own_ref[...] = matmul_nn(left_ref[:half, :], right).astype(LOW)
        other_ref[...] = matmul_nn(left_ref[half:, :], right).astype(LOW)

    pl.when(step < first_count)(functools.partial(product, left0_ref, right0_ref))
    pl.when(step >= first_count)(functools.partial(product, left1_ref, right1_ref))


def turn_body(
    place_ref,
    unit_ref,
    scale_ref,
    g_ref,
    a_ref,
    b_ref,
    gain_ref,
    wo_ref,
    datt_ref,
    turned_ref,
    dmix_ref,
    dgain_ref,
):
    step = pl.program_id(0)
    unit = unit_ref[...].astype(HIGH)
    scale = scale_ref[:, :1]
    d_normed = a_ref[...].astype(HIGH) + b_ref[...].astype(HIGH)
    d_gain = jnp.sum(d_normed * unit, axis=0, keepdims=True)
    d_attended = g_ref[...].astype(HIGH) + rms_back(d_normed, unit, scale, gain_ref[...])
    d_low = d_attended.astype(LOW)
    put_turned(turned_ref, d_low, False, place_ref[0])
    dmix_ref[...] = matmul_nn(d_low, wo_ref[...]).astype(LOW)

    @pl.when(step == 0)
    def _():
        dgain_ref[...] = d_gain

    @pl.when(step != 0)
    def _():
        dgain_ref[...] += d_gain

    @pl.when(step >= pl.num_programs(0) // 2)
    def _():
        datt_ref[...] = d_attended


def backward_body(
    q_ref,
    k_ref,
    v_ref,
    e_ref,
    dmix_ref,
    mixed_ref,
    inv_ref,
    dq_ref,
    dk_ref,
    dv_ref,
    strip_ref,
    table_ref,
    dkt_ref,
    dvt_ref,
):
    seq_len = k_ref.shape[0]
    rows = table_ref.shape[1]
    low_masks = head_masks(LOW)
    masks = head_masks(HIGH)
    keys = k_ref[...]
    values = v_ref[...]
    keys_h = tuple(keys * low_masks[h] for h in range(2))
    table_ref[...] = jnp.zeros_like(table_ref)
    for block in range(seq_len // rows):
        at = slice(block * rows, (block + 1) * rows)
        queries = q_ref[at, :]
        scaled = (dmix_ref[at, :].astype(HIGH) * inv_ref[at, :]).astype(LOW)
        product = scaled.astype(HIGH) * mixed_ref[at, :]
        d_query = jnp.zeros((rows, LANES), HIGH)
        d_key = jnp.zeros((LANES, seq_len), HIGH)
        d_value = jnp.zeros((LANES, seq_len), HIGH)
        for head in range(2):
            scaled_h = scaled * low_masks[head]
            delta = jnp.sum(product * masks[head], axis=-1, keepdims=True)
            weights = e_ref[head, at, :]
            d_scores = weights.astype(HIGH) * (matmul_nt(scaled_h, values) - delta)
            d_low = d_scores.astype(LOW)
            window = slice(seq_len - block * rows, 2 * seq_len - block * rows)
            table_ref[head, :, window] += d_scores
            d_query = d_query + matmul_nn(d_low, keys_h[head])
            d_key = d_key + matmul_tn(queries * low_masks[head], d_low)
            d_value = d_value + matmul_tn(scaled_h, weights)
        dq_ref[at, :] = d_query.astype(LOW)
        if block == 0:
            dkt_ref[...] = d_key
            dvt_ref[...] = d_value
        else:
            dkt_ref[...] += d_key
            dvt_ref[...] += d_value
    dk_ref[...] = dkt_ref[...].T.astype(LOW)
    dv_ref[...] = dvt_ref[...].T.astype(LOW)
    width = 2 * seq_len
    sub = lax.broadcasted_iota(jnp.int32, (8, 1), 0)
    for head in range(2):
        total = table_ref[head, 0:8, :]
        for group in range(1, rows // 8):
            part = table_ref[head, 8 * group : 8 * group + 8, :]
            total = total + pltpu.roll(part, width - 8 * group, 1)
        for bit in (1, 2, 4):
            total = jnp.where((sub & bit) != 0, pltpu.roll(total, width - bit, 1), total)
        strip_ref[0, head : head + 1, :] = jnp.sum(total, axis=0, keepdims=True)


def spread_body(
    place_ref, x_ref, dq_ref, dk_ref, dv_ref, qkv_ref, send_ref, own_ref, dgain_ref
):
    step = pl.program_id(0)
    width = dq_ref.shape[1]
    unit, _ = rms_parts(x_ref[...].astype(HIGH))
    d_normed = (
        matmul_nt(dq_ref[...], qkv_ref[:, :width])
        + matmul_nt(dk_ref[...], qkv_ref[:, width : 2 * width])
        + matmul_nt(dv_ref[...], qkv_ref[:, 2 * width :])
    )
    d_gain = jnp.sum(d_normed * unit, axis=0, keepdims=True)

    @pl.when(step == 0)
    def _():
        dgain_ref[...] = d_gain

    @pl.when(step != 0)
    def _():
        dgain_ref[...] += d_gain

    @pl.when(step < pl.num_programs(0) // 2)
    def _():
        send_ref[...] = d_normed.astype(LOW)

    @pl.when(step >= pl.num_programs(0) // 2)
    def _():
        own_ref[...] = d_normed


def finish_body(x_ref, own_ref, other_ref, datt_ref, gain_ref, out_ref):
    unit, scale = rms_parts(x_ref[...].astype(HIGH))
    d_normed = own_ref[...] + other_ref[...].astype(HIGH)
    out_ref[...] = (datt_ref[...] + rms_back(d_normed, unit, scale, gain_ref[...])).astype(LOW)


def flat_left(left):
    return left.reshape(-1, left.shape[-1])


def weight_grads(first, second, columns, micros):
    left0, right0, at0, count0 = first
    left1, right1, at1, count1 = second
    left0, left1 = flat_left(left0), flat_left(left1)
    height, depth = left0.shape
    steps = count0 + count1
    half_spec = pl.BlockSpec((height // 2, columns), lambda i: (0, i))
    return call(
        functools.partial(grads_body, count0),
        (steps,),
        [
            whole((height, depth)),
            whole((height, depth)),
            pl.BlockSpec((depth, columns), lambda i: (0, at0 + jnp.minimum(i, count0 - 1))),
            pl.BlockSpec((depth, columns), lambda i: (0, at1 + jnp.maximum(i - count0, 0))),
        ],
        [half_spec, half_spec],
        [shaped((height // 2, steps * columns), LOW)] * 2,
        micros=micros,
    )(left0, left1, right0, right1)


def on_core_pair(
    tokens,
    cotangent,
    gain_attn,
    w_query,
    w_key,
    w_value,
    w_out,
    rel_table,
    buckets,
    gain_ffn,
    w_gate,
    w_up,
    w_down,
):
    own_rows, features = tokens.shape
    seq_len = 2 * own_rows
    width = w_query.shape[1]
    units = w_gate.shape[1]
    chunk = units // 2
    pairs = width // LANES
    bucket_count, head_count = rel_table.shape
    local_heads = head_count // 2
    count = lax.axis_size("dp")
    far_bit, y_bit, x_bit = dp_place()
    me = lax.axis_index("mp")
    place = jnp.stack([y_bit, x_bit, me, far_bit]).astype(jnp.int32)
    rows = MXU_ROWS
    steps = seq_len // rows
    half_steps = steps // 2
    block_rows = w_query.shape[0]

    def swapped(array):
        return lax.ppermute(array, "mp", [(0, 1), (1, 0)])

    def in_order(array, other):
        first = jnp.where(me == 0, array, other)
        second = jnp.where(me == 0, other, array)
        return jnp.concatenate([first, second], axis=0)

    early = jnp.concatenate([w_query, w_key, w_value, w_out.T], axis=1)
    late = jnp.concatenate([w_gate, w_up, w_down.T], axis=1)
    early_pieces = far_pieces(early)
    x_other, g_other = swapped(tokens), swapped(cotangent)
    late_pieces = far_pieces(late)
    early_pieces = together(*early_pieces)
    near = far_stack(early, list(early_pieces))
    qk = near[:, : 2 * width]
    vo = near[:, 2 * width :]
    qk_next, vo_next = together(over_y(qk), over_x(vo))
    qk_own = in_bit_order(qk, qk_next, y_bit)
    vo_own = in_bit_order(vo, vo_next, x_bit)
    qk_other = over_x(qk_own)
    vo_other = over_y(vo_own)
    x_all = in_order(tokens, x_other)
    g_all = in_order(cotangent, g_other)
    qk_other, vo_other, x_all, g_all, *late_pieces = together(
        qk_other, vo_other, x_all, g_all, *late_pieces
    )
    near = far_stack(late, late_pieces)
    gu = near[:, : 3 * chunk]
    ud = near[:, 3 * chunk :]
    gu_next = over_y(gu)
    ud_next = over_x(ud)

    gain_a = gain_attn.reshape(1, features)
    gain_f = gain_ffn.reshape(1, features)

    one_hot = (buckets[:, None] == jnp.arange(bucket_count, dtype=jnp.int32)[None, :]).astype(HIGH)
    one_hot = jnp.pad(one_hot, ((1, 0), (0, 0)))
    my_table = lax.dynamic_slice_in_dim(rel_table, me * local_heads, local_heads, 1)
    strip = lax.dot_general(my_table, one_hot, (((0,), (1,)), ((), ())), precision=precise)
    strip = strip.reshape(pairs, 2, 2 * seq_len)

    def row_block(columns):
        return pl.BlockSpec((rows, columns), lambda i, *_: (i, 0))

    turned_shape = (2, 2, 2, 2, block_rows)
    turned_block = pl.BlockSpec(turned_shape + (rows,), lambda i, *_: (0, 0, 0, 0, 0, i))
    turned = shaped(turned_shape + (seq_len,), LOW)
    full_block = (count // 4, 2, 2, block_rows, 2 * width)
    half_block = (features // 2, 2 * width)
    normed_x_turned, normed_y_turned, queries, keys, values, w_qkv, w_o = call(
        project_body,
        (steps,),
        [row_block(features), whole((1, features))] + [whole(half_block)] * 4,
        [turned_block, turned_block]
        + [row_block(width)] * 3
        + [result((features, 3 * width)), result((features, width))],
        [turned, turned]
        + [shaped((seq_len, width), LOW)] * 3
        + [shaped((features, 3 * width), LOW), shaped((features, width), LOW)],
        [pltpu.VMEM(full_block, LOW), pltpu.VMEM(full_block, LOW)],
        prefetch=1,
        micros=7,
    )(place, x_all, gain_a, qk_own, qk_other, vo_own, vo_other)

    gu_next, ud_next, queries = together(gu_next, ud_next, queries)
    gu_own = in_bit_order(gu, gu_next, y_bit)
    ud_own = in_bit_order(ud, ud_next, x_bit)
    gu_other = over_x(gu_own)
    ud_other = over_y(ud_own)

    pair_block = pl.BlockSpec((seq_len, LANES), lambda p: (0, p))
    e_block = pl.BlockSpec((2, seq_len, seq_len), lambda p: (p, 0, 0))
    strip_block = pl.BlockSpec((1, 2, 2 * seq_len), lambda p: (p, 0, 0))
    table_scratch = pltpu.VMEM((2, rows, 2 * seq_len), HIGH)
    weights_e, mixed, mixed_low, inverse, part0, part1 = call(
        attend_body,
        (pairs,),
        [
            pair_block,
            pair_block,
            pair_block,
            strip_block,
            pl.BlockSpec((features, LANES), lambda p: (0, p)),
        ],
        [e_block, pair_block, pair_block, pair_block] + [result((own_rows, features))] * 2,
        [
            shaped((2 * pairs, seq_len, seq_len), LOW),
            shaped((seq_len, width), HIGH),
            shaped((seq_len, width), LOW),
            shaped((seq_len, width), HIGH),
            shaped((own_rows, features), LOW),
            shaped((own_rows, features), LOW),
        ],
        [table_scratch, pltpu.VMEM((seq_len, features), HIGH)],
        micros=20,
    )(queries, keys, values, strip, w_o)
    gu_other, ud_other, came0, came1 = together(
        gu_other, ud_other, swapped(part0), swapped(part1)
    )
    parts = (part0, part1, came0, came1)

    def moved(i, m):
        return (jnp.minimum(i, steps - 1) + half_steps * (1 - m[2])) % steps

    def turned_row(columns):
        return pl.BlockSpec((rows, columns), lambda i, m: (moved(i, m), 0))

    half0_row = pl.BlockSpec(
        (rows, features), lambda i, m: (jnp.minimum(moved(i, m), half_steps - 1), 0)
    )
    half1_row = pl.BlockSpec(
        (rows, features), lambda i, m: (jnp.maximum(moved(i, m) - half_steps, 0), 0)
    )
    moved_block = pl.BlockSpec(turned_shape + (rows,), lambda i, m: (0, 0, 0, 0, 0, moved(i, m)))
    send_row = pl.BlockSpec((rows, features), lambda i, m: (jnp.minimum(i, half_steps - 1), 0))
    keep_row = pl.BlockSpec(
        (rows, features),
        lambda i, m: (jnp.clip(i - half_steps, 0, half_steps - 1), 0),
    )

    def grads_block(first):
        return pl.BlockSpec(
            (features // 2, chunk), lambda i, m: (0, jnp.clip(i - steps - first, 0, 2))
        )

    full_block = (count // 4, 2, 2, block_rows, 3 * chunk)
    half_block = (features // 2, 3 * chunk)
    half_grads = shaped((features // 2, 3 * chunk), LOW)
    unit_f, scale_f, dn_part, out_send, out_own, gu_own, gu_send, ud_own, ud_send = call(
        functools.partial(feed_body, steps),
        (steps + 6,),
        [turned_row(features)]
        + [half0_row, half1_row] * 2
        + [turned_row(features), whole((1, features))]
        + [whole(half_block)] * 4,
        [turned_row(features), turned_row(LANES), turned_row(features), send_row, keep_row]
        + [grads_block(0)] * 2
        + [grads_block(3)] * 2,
        [
            shaped((seq_len, features), LOW),
            shaped((seq_len, LANES), HIGH),
            shaped((seq_len, features), LOW),
            shaped((own_rows, features), LOW),
            shaped((own_rows, features), HIGH),
        ]
        + [half_grads] * 4,
        [pltpu.VMEM(full_block, LOW), pltpu.VMEM(full_block, LOW)]
        + [pltpu.VMEM(turned_shape + (seq_len,), LOW)] * 3
        + [pltpu.VMEM((seq_len, units), LOW), pltpu.VMEM((seq_len, 2 * units), LOW)],
        prefetch=1,
        micros=28,
    )(place, x_all, *parts, g_all, gain_f, gu_own, gu_other, ud_own, ud_other)
    dn_other = swapped(dn_part)
    gu_came = over_x(gu_send)
    ud_came = over_y(ud_send)

    d_attended, d_low_turned, d_mixed, d_gain_f = call(
        turn_body,
        (steps,),
        [turned_row(features), turned_row(LANES)]
        + [turned_row(features)] * 3
        + [whole((1, features)), whole((features, width))],
        [keep_row, moved_block, turned_row(width), result((1, features))],
        [
            shaped((own_rows, features), HIGH),
            turned,
            shaped((seq_len, width), LOW),
            shaped((1, features), HIGH),
        ],
        prefetch=1,
        micros=4,
    )(place, unit_f, scale_f, g_all, dn_part, dn_other, gain_f, w_o)
    out_other = swapped(out_send)

    d_query, d_key, d_value, d_strip = call(
        backward_body,
        (pairs,),
        [pair_block, pair_block, pair_block, e_block, pair_block, pair_block, pair_block],
        [pair_block, pair_block, pair_block, strip_block],
        [shaped((seq_len, width), LOW)] * 3 + [shaped((pairs, 2, 2 * seq_len), HIGH)],
        [table_scratch, pltpu.VMEM((LANES, seq_len), HIGH), pltpu.VMEM((LANES, seq_len), HIGH)],
        micros=4,
    )(queries, keys, values, weights_e, d_mixed, mixed, inverse)

    gu_came, ud_came, out_other, d_query, d_key, d_value, d_strip = together(
        gu_came, ud_came, out_other, d_query, d_key, d_value, d_strip
    )

    def next_half(own, came, bit):
        return (
            add_low(part_of(own, bit, 2), part_of(came, bit, 2)),
            add_low(part_of(own, 1 - bit, 2), part_of(came, 1 - bit, 2)),
        )

    gu_own, gu_send = next_half(gu_own, gu_came, y_bit)
    ud_own, ud_send = next_half(ud_own, ud_came, x_bit)
    gu_came = over_y(gu_send)
    ud_came = over_x(ud_send)

    qk_own, qk_send = weight_grads(
        (normed_x_turned, d_query, 0, 1), (normed_x_turned, d_key, 0, 1), width, 5
    )
    qk_send, d_value = together(qk_send, d_value)
    vo_own, vo_send = weight_grads(
        (normed_y_turned, d_value, 0, 1), (d_low_turned, mixed_low, 0, 1), width, 5
    )
    output = (out_own + out_other.astype(HIGH)).astype(LOW)

    gu_came, ud_came, qk_send, vo_send, d_query = together(
        gu_came, ud_came, qk_send, vo_send, d_query
    )
    qk_came = over_x(qk_send)
    vo_came = over_y(vo_send)
    gu_own, gu_send = next_half(gu_own, gu_came, far_bit % 2)
    ud_own, ud_send = next_half(ud_own, ud_came, far_bit % 2)
    unit_own = jnp.concatenate([gu_own, ud_own], axis=1)
    unit_send = jnp.concatenate([gu_send, ud_send], axis=1)
    unit_came = over_far_bit(unit_send, 0)

    dna_send, dna_own, d_gain_a = call(
        spread_body,
        (steps,),
        [turned_row(features)] + [turned_row(width)] * 3 + [whole((features, 3 * width))],
        [send_row, keep_row, result((1, features))],
        [
            shaped((own_rows, features), LOW),
            shaped((own_rows, features), HIGH),
            shaped((1, features), HIGH),
        ],
        prefetch=1,
        micros=7,
    )(place, x_all, d_query, d_key, d_value, w_qkv)
    qk_came, vo_came, unit_came, dna_send, d_gain_a, d_strip = together(
        qk_came, vo_came, unit_came, dna_send, d_gain_a, d_strip
    )
    unit_own, unit_send = next_half(unit_own, unit_came, far_bit // 2)
    unit_came = over_far_bit(unit_send, 1)
    dna_other = swapped(dna_send)
    qk_own, qk_send = next_half(qk_own, qk_came, y_bit)
    vo_own, vo_send = next_half(vo_own, vo_came, x_bit)
    qk_came = over_y(qk_send)
    vo_came = over_x(vo_send)

    d_bias = d_strip.reshape(local_heads, 2 * seq_len)
    my_d_table = lax.dot_general(one_hot, d_bias, (((0,), (1,)), ((), ())), precision=precise)
    d_table = lax.dynamic_update_slice_in_dim(
        jnp.zeros_like(rel_table), my_d_table, me * local_heads, 1
    )
    small_early = jnp.concatenate([0.5 * d_gain_f, d_table.reshape(1, -1)], axis=1)
    small_early = jnp.pad(small_early, ((0, 0), (0, -(features + small_early.shape[1]) % (4 * width))))
    small = jnp.concatenate([d_gain_a, small_early], axis=1)
    small = small.reshape(-1, 4 * width)
    small = small + swapped(small)
    small = small + over_x(small) + over_y(small) + over_xy(small)

    d_tokens = call(
        finish_body,
        (half_steps,),
        [row_block(features)] * 4 + [whole((1, features))],
        row_block(features),
        shaped((own_rows, features), LOW),
        micros=3.5,
    )(tokens, dna_own, dna_other, d_attended, gain_a)

    qk_came, vo_came, unit_came, d_tokens, small = together(
        qk_came, vo_came, unit_came, d_tokens, small
    )
    head_own = jnp.concatenate([qk_own, vo_own], axis=-1)
    head_came = jnp.concatenate([qk_came, vo_came], axis=-1)
    total = add_low(head_own, head_came)

    def far_part(far):
        return part_of(total, 2 * (far % 2) + far // 2, 4)

    small_rows = in_terms(small)
    pieces = [
        over_far(jnp.concatenate([far_part((far_bit + k) % 4), small_rows], axis=0), k)
        for k in range(1, 4)
    ]
    small = sum((from_terms(piece[block_rows:], small.shape[0]) for piece in pieces), small)
    small = small.reshape(-1)
    pieces = [piece[:block_rows] for piece in pieces]
    grads_head = sum((piece.astype(HIGH) for piece in pieces), far_part(far_bit).astype(HIGH))
    grads_qk, grads_vo = grads_head[:, : 2 * width], grads_head[:, 2 * width :]
    grads_unit = unit_own.astype(HIGH) + unit_came.astype(HIGH)
    return (
        output,
        d_tokens,
        small[:features],
        grads_qk[:, :width],
        grads_qk[:, width:],
        grads_vo[:, :width],
        grads_vo[:, width:].T,
        small[2 * features : 2 * features + rel_table.size].reshape(rel_table.shape),
        small[features : 2 * features],
        grads_unit[:, :units],
        grads_unit[:, units : 2 * units],
        grads_unit[:, 2 * units :].T,
    )


def solution(mesh):
    placed = (
        P(("dp", "mp"), None),
        P(("dp", "mp"), None),
        P(),
        P("dp", "mp"),
        P("dp", "mp"),
        P("dp", "mp"),
        P("mp", "dp"),
        P(),
        P(),
        P(),
        P("dp", "mp"),
        P("dp", "mp"),
        P("mp", "dp"),
    )
    paired = mesh.shape["mp"] == 2 and mesh.shape["dp"] == 16
    body = on_core_pair if paired else on_device
    return jax.shard_map(
        body,
        mesh=mesh,
        in_specs=placed,
        out_specs=(
            P(("dp", "mp"), None),
            P(("dp", "mp"), None),
            P(),
            P("dp", "mp"),
            P("dp", "mp"),
            P("dp", "mp"),
            P("mp", "dp"),
            P(),
            P(),
            P("dp", "mp"),
            P("dp", "mp"),
            P("mp", "dp"),
        ),
        check_vma=False,
    )
```

```python
import functools

import jax
import jax.numpy as jnp
from jax import lax
from jax.experimental import pallas as pl
from jax.experimental.pallas import tpu as pltpu
from jax.sharding import PartitionSpec as P

epsilon = 1e-06
block_limit = 512
precise = lax.Precision.HIGHEST


def as_sent(array):

    def short(part):
        return part.astype(jnp.bfloat16) if part.dtype == jnp.float32 else part

    return jax.tree.map(short, array)


def matmul_nn(left, right):
    return jnp.dot(left, right, preferred_element_type=jnp.float32)


def matmul_nt(left, right):
    return lax.dot_general(
        left, right, (((1,), (1,)), ((), ())), preferred_element_type=jnp.float32
    )


def matmul_tn(left, right):
    return lax.dot_general(
        left, right, (((0,), (0,)), ((), ())), preferred_element_type=jnp.float32
    )


def rms_parts(inputs):
    scale = lax.rsqrt(jnp.mean(inputs * inputs, axis=-1, keepdims=True) + epsilon)
    return (inputs * scale, scale)


def rms_back(d_normed, unit, scale, gain):
    d_unit = d_normed * gain
    return scale * (d_unit - unit * jnp.mean(d_unit * unit, axis=-1, keepdims=True))


def gated(gate_pre, up_pre):
    return jax.nn.gelu(gate_pre, approximate=True) * up_pre


def window_base(first_query, first_key, row_count, seq_len):
    return first_key - first_query - row_count + seq_len


def make_bias(bias_full, base, row_count, width):
    span = width + row_count - 1
    head_count = bias_full.shape[0]
    strip = lax.dynamic_slice_in_dim(bias_full, base, span, 1)
    tiled = jnp.tile(strip, (1, row_count + 1))
    window = tiled[:, row_count - 1 : row_count - 1 + row_count * (span - 1)]
    return window.reshape(head_count, row_count, span - 1)[:, :, :width]


def skew_sum(d_block, row_count, width):
    head_count = d_block.shape[0]
    span = width + row_count - 1
    padded = jnp.pad(d_block, ((0, 0), (0, 0), (row_count - 1, 0)))
    flat = padded.reshape(head_count, row_count * span)
    flat = jnp.pad(flat, ((0, 0), (0, row_count)))
    skewed = flat.reshape(head_count, row_count, span + 1)[:, :, :span]
    return jnp.sum(skewed, axis=1)


def add_window(d_bias, piece, base):
    current = lax.dynamic_slice_in_dim(d_bias, base, piece.shape[1], 1)
    return lax.dynamic_update_slice_in_dim(d_bias, current + piece, base, 1)


def sum_rows(partial_value):
    return lax.psum_scatter(
        partial_value.astype(jnp.bfloat16), "mp", scatter_dimension=0, tiled=True
    ).astype(jnp.float32)


def split_heads(queries, keys_all, values, head_count):
    row_count = queries.shape[0]
    seq_len = keys_all.shape[0]
    head_dim = queries.shape[1] // head_count
    width = min(block_limit, seq_len)
    blocks = seq_len // width
    heads_q = queries.reshape(row_count, head_count, head_dim)
    heads_k = keys_all.reshape(blocks, width, head_count, head_dim)
    heads_v = values.reshape(blocks, width, head_count, head_dim)
    starts = jnp.arange(blocks, dtype=jnp.int32) * width
    return (heads_q, heads_k, heads_v, starts, width)


def attend_forward(queries, keys_all, values, bias_full, head_count, first_row):
    row_count = queries.shape[0]
    seq_len = keys_all.shape[0]
    heads_q, heads_k, heads_v, starts, width = split_heads(queries, keys_all, values, head_count)

    def block_scores(key_block, first_key):
        raw_scores = jnp.einsum(
            "qhd,khd->hqk", heads_q, key_block, preferred_element_type=jnp.float32
        )
        base = window_base(first_row, first_key, row_count, seq_len)
        return raw_scores + make_bias(bias_full, base, row_count, width)

    def stats_step(running, pieces):
        top_now, total = running
        scores = block_scores(pieces[0], pieces[1])
        top_new = jnp.maximum(top_now, jnp.max(scores, axis=-1))
        total = total * jnp.exp(top_now - top_new) + jnp.sum(
            jnp.exp(scores - top_new[..., None]), axis=-1
        )
        return ((top_new, total), None)

    start_top = jnp.full((head_count, row_count), -jnp.inf, jnp.float32)
    start_total = jnp.zeros((head_count, row_count), jnp.float32)
    (top_all, total), _ = lax.scan(stats_step, (start_top, start_total), (heads_k, starts))
    log_total = top_all + jnp.log(total)

    def mix_step(running, pieces):
        scores = block_scores(pieces[0], pieces[2])
        probs_low = jnp.exp(scores - log_total[..., None]).astype(jnp.bfloat16)
        update = jnp.einsum(
            "hqk,khd->qhd", probs_low, pieces[1], preferred_element_type=jnp.float32
        )
        return (running + update, None)

    start_mix = jnp.zeros(heads_q.shape, jnp.float32)
    mixed_f, _ = lax.scan(mix_step, start_mix, (heads_k, heads_v, starts))
    return (mixed_f.reshape(row_count, queries.shape[1]), log_total)


def attend_backward(
    queries, keys_all, values, bias_full, head_count, first_row, log_total, deltas, d_mixed
):
    row_count = queries.shape[0]
    seq_len = keys_all.shape[0]
    heads_q, heads_k, heads_v, starts, width = split_heads(queries, keys_all, values, head_count)
    heads_d = d_mixed.reshape(heads_q.shape)

    def back_step(running, pieces):
        d_query, d_bias = running
        key_block, value_block, first_key = pieces
        base = window_base(first_row, first_key, row_count, seq_len)
        scores = jnp.einsum("qhd,khd->hqk", heads_q, key_block, preferred_element_type=jnp.float32)
        scores = scores + make_bias(bias_full, base, row_count, width)
        probs = jnp.exp(scores - log_total[..., None])
        d_probs = jnp.einsum(
            "qhd,khd->hqk", heads_d, value_block, preferred_element_type=jnp.float32
        )
        d_scores = (probs * (d_probs - deltas[..., None])).astype(jnp.bfloat16)
        d_query = d_query + jnp.einsum(
            "hqk,khd->qhd", d_scores, key_block, preferred_element_type=jnp.float32
        )
        d_bias = add_window(d_bias, skew_sum(d_scores.astype(jnp.float32), row_count, width), base)
        probs_low = probs.astype(jnp.bfloat16)
        d_value = jnp.einsum("hqk,qhd->khd", probs_low, heads_d, preferred_element_type=jnp.float32)
        d_key = jnp.einsum("hqk,qhd->khd", d_scores, heads_q, preferred_element_type=jnp.float32)
        return ((d_query, d_bias), (d_key, d_value))

    start_query = jnp.zeros(heads_q.shape, jnp.float32)
    (d_query, d_bias), kv_parts = lax.scan(
        back_step, (start_query, jnp.zeros_like(bias_full)), (heads_k, heads_v, starts)
    )
    feature_count = queries.shape[1]
    d_query = d_query.reshape(row_count, feature_count)
    return (
        d_query,
        d_bias,
        kv_parts[0].reshape(seq_len, feature_count),
        kv_parts[1].reshape(seq_len, feature_count),
    )


def on_device(
    tokens,
    cotangent,
    gain_attn,
    w_query,
    w_key,
    w_value,
    w_out,
    rel_table,
    buckets,
    gain_ffn,
    w_gate,
    w_up,
    w_down,
):
    head_count = rel_table.shape[1]
    bucket_count = rel_table.shape[0]
    inputs = tokens.astype(jnp.float32)
    row_count = inputs.shape[0]
    feature_count = inputs.shape[1]
    first_row = lax.axis_index("mp") * row_count
    attn_parts = (w_query, w_key, w_value, w_out.T)
    ffn_parts = (w_gate, w_up, w_down.T)
    ffn_cols = ()
    col_parts = lax.all_gather(as_sent(attn_parts + ffn_cols), "mp", axis=1, tiled=True)
    full_parts = lax.all_gather(as_sent(tuple(col_parts) + ffn_parts), "dp", axis=0, tiled=True)
    query_full, key_full, value_full, out_full, gate_full, up_full, down_full = full_parts
    unit_a, scale_a = rms_parts(inputs)
    normed_a = (unit_a * gain_attn).astype(jnp.bfloat16)
    queries = matmul_nn(normed_a, query_full).astype(jnp.bfloat16)
    own_keys = matmul_nn(normed_a, key_full).astype(jnp.bfloat16)
    own_values = matmul_nn(normed_a, value_full).astype(jnp.bfloat16)
    keys_all, values = (
        lax.all_gather(own_keys, "mp", axis=0, tiled=True),
        lax.all_gather(own_values, "mp", axis=0, tiled=True),
    )
    one_hot = (buckets[:, None] == jnp.arange(bucket_count, dtype=jnp.int32)[None, :]).astype(
        jnp.float32
    )
    bias_full = jnp.dot(one_hot, rel_table, precision=precise).T
    mixed_f, log_total = attend_forward(queries, keys_all, values, bias_full, head_count, first_row)
    mixed_out = mixed_f.astype(jnp.bfloat16)
    attended = inputs + matmul_nt(mixed_out, out_full)
    unit_f, scale_f = rms_parts(attended)
    normed_f = (unit_f * gain_ffn).astype(jnp.bfloat16)
    normed_seq, cot_seq = (
        lax.all_gather(normed_f, "mp", axis=0, tiled=True),
        lax.all_gather(cotangent, "mp", axis=0, tiled=True),
    )
    gate_pre = matmul_nn(normed_seq, gate_full)
    up_pre = matmul_nn(normed_seq, up_full)
    hidden = gated(gate_pre, up_pre).astype(jnp.bfloat16)
    output = attended + sum_rows(matmul_nt(hidden, down_full))
    d_hidden = matmul_nn(cot_seq, down_full)
    d_down = matmul_tn(cot_seq, hidden)
    _, pull_gate = jax.vjp(gated, gate_pre, up_pre)
    d_gate, d_up = pull_gate(d_hidden)
    d_gate = d_gate.astype(jnp.bfloat16)
    d_up = d_up.astype(jnp.bfloat16)
    d_normed_f = sum_rows(matmul_nt(d_gate, gate_full) + matmul_nt(d_up, up_full))
    d_gate_w = matmul_tn(normed_seq, d_gate)
    d_up_w = matmul_tn(normed_seq, d_up)
    d_gain_f = jnp.sum(d_normed_f * unit_f, axis=0)
    d_attended = cotangent.astype(jnp.float32) + rms_back(d_normed_f, unit_f, scale_f, gain_ffn)
    d_att_low = d_attended.astype(jnp.bfloat16)
    d_out_w = matmul_tn(d_att_low, mixed_out)
    d_mixed = matmul_nn(d_att_low, out_full).astype(jnp.bfloat16)
    head_dim = feature_count // head_count
    deltas = jnp.sum(
        (d_mixed.astype(jnp.float32) * mixed_f).reshape(row_count, head_count, head_dim), axis=-1
    ).T
    d_query, d_bias, d_keys_part, d_values_part = attend_backward(
        queries, keys_all, values, bias_full, head_count, first_row, log_total, deltas, d_mixed
    )
    d_keys_own, d_values_own = (
        lax.psum_scatter(
            d_keys_part.astype(jnp.bfloat16), "mp", scatter_dimension=0, tiled=True
        ).astype(jnp.float32),
        lax.psum_scatter(
            d_values_part.astype(jnp.bfloat16), "mp", scatter_dimension=0, tiled=True
        ).astype(jnp.float32),
    )
    d_keys_own = d_keys_own.astype(jnp.bfloat16)
    d_values_own = d_values_own.astype(jnp.bfloat16)
    d_query = d_query.astype(jnp.bfloat16)
    d_normed_a = (
        matmul_nt(d_query, query_full)
        + matmul_nt(d_keys_own, key_full)
        + matmul_nt(d_values_own, value_full)
    )
    d_query_w = matmul_tn(normed_a, d_query)
    d_key_w = matmul_tn(normed_a, d_keys_own)
    d_value_w = matmul_tn(normed_a, d_values_own)
    d_gain_a = jnp.sum(d_normed_a * unit_a, axis=0)
    d_tokens = (d_attended + rms_back(d_normed_a, unit_a, scale_a, gain_attn)).astype(jnp.bfloat16)
    d_table = jnp.dot(d_bias, one_hot, precision=precise).T
    row_grads = (
        lax.psum_scatter(
            d_query_w.astype(jnp.bfloat16), "dp", scatter_dimension=0, tiled=True
        ).astype(jnp.float32),
        lax.psum_scatter(
            d_key_w.astype(jnp.bfloat16), "dp", scatter_dimension=0, tiled=True
        ).astype(jnp.float32),
        lax.psum_scatter(
            d_value_w.astype(jnp.bfloat16), "dp", scatter_dimension=0, tiled=True
        ).astype(jnp.float32),
        lax.psum_scatter(
            d_out_w.astype(jnp.bfloat16), "dp", scatter_dimension=0, tiled=True
        ).astype(jnp.float32),
        lax.psum_scatter(
            d_gate_w.astype(jnp.bfloat16), "dp", scatter_dimension=0, tiled=True
        ).astype(jnp.float32),
        lax.psum_scatter(d_up_w.astype(jnp.bfloat16), "dp", scatter_dimension=0, tiled=True).astype(
            jnp.float32
        ),
        lax.psum_scatter(d_down.astype(jnp.bfloat16), "dp", scatter_dimension=0, tiled=True).astype(
            jnp.float32
        ),
    )
    row_grads = tuple(row_grads)
    ffn_late = ()
    col_grads = tuple(
        jax.tree.map(
            lambda part: part.astype(jnp.float32),
            lax.psum_scatter(
                as_sent(row_grads[:4] + ffn_late), "mp", scatter_dimension=1, tiled=True
            ),
        )
    )
    ffn_done = row_grads[4:]
    small_sums = lax.psum((d_gain_a, d_gain_f, d_table), ("dp", "mp"))
    return (
        output.astype(jnp.bfloat16),
        d_tokens,
        small_sums[0],
        col_grads[0],
        col_grads[1],
        col_grads[2],
        col_grads[3].T,
        small_sums[2],
        small_sums[1],
        ffn_done[0],
        ffn_done[1],
        ffn_done[2].T,
    )


MXU_ROWS = 256
LANES = 128
VMEM_LIMIT = 56 * 2**20
PEAK_PER_MICRO = 1_153_500_000
LOW = jnp.bfloat16
HIGH = jnp.float32


def call(
    body, grid, in_specs, out_specs, out_shape, scratch=(), prefetch=0, micros=5, aliases=None
):
    return pl.pallas_call(
        body,
        grid_spec=pltpu.PrefetchScalarGridSpec(
            num_scalar_prefetch=prefetch,
            grid=grid,
            in_specs=in_specs,
            out_specs=out_specs,
            scratch_shapes=list(scratch),
        ),
        out_shape=out_shape,
        input_output_aliases=aliases or {},
        compiler_params=pltpu.CompilerParams(vmem_limit_bytes=VMEM_LIMIT),
        cost_estimate=pl.CostEstimate(
            flops=int(micros * PEAK_PER_MICRO), bytes_accessed=0, transcendentals=0
        ),
    )


def shaped(shape, dtype):
    return jax.ShapeDtypeStruct(shape, dtype)


def whole(shape):
    return pl.BlockSpec(shape, lambda *_: (0,) * len(shape), pipeline_mode=pl.Buffered(1))


def result(shape):
    return pl.BlockSpec(shape, lambda *_: (0,) * len(shape))


def together(*arrays):
    return lax.optimization_barrier(arrays)


def ring_shift(steps, count):
    return [(i, (i + steps) % count) for i in range(count)]


def flip(bit, count):
    return [(i, i ^ bit) for i in range(count)]


def over_x(array):
    return lax.ppermute(array, "dp", flip(1, lax.axis_size("dp")))


def over_y(array):
    return lax.ppermute(array, "dp", flip(2, lax.axis_size("dp")))


def over_xy(array):
    return lax.ppermute(array, "dp", flip(3, lax.axis_size("dp")))


def over_far(array, steps):
    return lax.ppermute(array, "dp", ring_shift(4 * steps, lax.axis_size("dp")))


def dp_place():
    index = lax.axis_index("dp")
    return (index // 4, (index // 2) % 2, index % 2)


def in_bit_order(own, other, bit):
    first = jnp.where(bit == 0, own, other)
    second = jnp.where(bit == 0, other, own)
    return jnp.concatenate([first, second], axis=0)


def far_pieces(shard):
    return [over_far(shard, k) for k in range(1, lax.axis_size("dp") // 4)]


def far_stack(shard, pieces):
    far = len(pieces) + 1
    place = dp_place()[0]
    stacked = jnp.zeros((far,) + shard.shape, shard.dtype)
    for k, piece in enumerate([shard] + pieces):
        stacked = lax.dynamic_update_slice(stacked, piece[None], ((place - k) % far, 0, 0))
    return stacked.reshape(-1, shard.shape[1])


def over_far_bit(array, bit):
    return lax.ppermute(array, "dp", flip(4 << bit, lax.axis_size("dp")))


def part_of(array, index, parts):
    size = array.shape[0] // parts
    return lax.dynamic_slice_in_dim(array, index * size, size, 0)


def add_low(left, right):
    return (left.astype(HIGH) + right.astype(HIGH)).astype(LOW)


def in_terms(array):
    terms, rest = [], array
    for _ in range(3):
        term = lax.optimization_barrier(rest.astype(LOW))
        terms.append(term)
        rest = rest - term.astype(HIGH)
    rows = jnp.concatenate(terms, axis=0)
    return jnp.pad(rows, ((0, -rows.shape[0] % 8), (0, 0)))


def from_terms(rows, height):
    return sum(rows[i * height : (i + 1) * height].astype(HIGH) for i in range(3))


def head_masks(dtype):
    lane = lax.broadcasted_iota(jnp.int32, (1, LANES), 1)
    first = (lane < LANES // 2).astype(HIGH)
    return (first.astype(dtype), (1.0 - first).astype(dtype))


def put_weights(full_ref, own_ref, other_ref, y_first, bit):
    far, rows = full_ref.shape[0], full_ref.shape[3]
    for half_ref, at in ((own_ref, bit), (other_ref, 1 - bit)):
        for near in range(2):
            for place in range(far):
                start = (near * far + place) * rows
                block = half_ref[start : start + rows, :]
                if y_first:
                    full_ref[place, near, at] = block
                else:
                    full_ref[place, at, near] = block


def put_turned(turned_ref, array, x_first, bit, lanes=slice(None)):
    rows = turned_ref.shape[4]
    turned = array.T
    for block in range(turned.shape[0] // rows):
        far, y_bit, x_bit = block // 4, (block // 2) % 2, block % 2
        first, second = (x_bit, y_bit) if x_first else (y_bit, x_bit)
        other = 1 - bit if first else bit
        turned_ref[other, second, far % 2, far // 2, :, lanes] = turned[
            block * rows : (block + 1) * rows
        ]


def matrix(full_ref, start, columns):
    part = full_ref[:, :, :, :, start : start + columns]
    return part.reshape(-1, columns)


def project_body(
    place_ref,
    x_ref,
    gain_ref,
    qk_own_ref,
    qk_other_ref,
    vo_own_ref,
    vo_other_ref,
    turned_x_ref,
    turned_y_ref,
    q_ref,
    k_ref,
    v_ref,
    qkv_ref,
    wo_ref,
    qk_ref,
    vo_ref,
):
    width = q_ref.shape[1]

    @pl.when(pl.program_id(0) == 0)
    def _():
        put_weights(qk_ref, qk_own_ref, qk_other_ref, True, place_ref[1])
        put_weights(vo_ref, vo_own_ref, vo_other_ref, False, place_ref[0])
        qkv_ref[:, : 2 * width] = matrix(qk_ref, 0, 2 * width)
        qkv_ref[:, 2 * width :] = matrix(vo_ref, 0, width)
        wo_ref[...] = matrix(vo_ref, width, width)

    unit, _ = rms_parts(x_ref[...].astype(HIGH))
    normed = (unit * gain_ref[...]).astype(LOW)
    put_turned(turned_x_ref, normed, True, place_ref[1])
    put_turned(turned_y_ref, normed, False, place_ref[0])
    q_ref[...] = matmul_nn(normed, qkv_ref[:, :width]).astype(LOW)
    k_ref[...] = matmul_nn(normed, qkv_ref[:, width : 2 * width]).astype(LOW)
    v_ref[...] = matmul_nn(normed, qkv_ref[:, 2 * width :]).astype(LOW)


def attend_body(
    q_ref, k_ref, v_ref, strip_ref, wo_ref, e_ref, mixed_ref, low_ref, inv_ref, part0_ref, part1_ref, table_ref, acc_ref
):
    pair = pl.program_id(0)
    seq_len = k_ref.shape[0]
    rows = table_ref.shape[1]
    low_masks = head_masks(LOW)
    own_lanes = tuple(mask > 0.5 for mask in head_masks(HIGH))
    for head in range(2):
        row = jnp.broadcast_to(strip_ref[0, head : head + 1, :], (rows, 2 * seq_len))
        table_ref[head] = pltpu.roll(row, 0, 1, stride=1, stride_axis=0)
    keys = k_ref[...]
    values = v_ref[...]
    values_h = tuple(values * low_masks[h] + low_masks[1 - h] for h in range(2))

    @pl.when(pair == 0)
    def _():
        acc_ref[...] = jnp.zeros_like(acc_ref)

    def scored(block, head):
        at = slice(block * rows, (block + 1) * rows)
        raw = matmul_nt(q_ref[at, :] * low_masks[head], keys)
        return raw + table_ref[head, :, seq_len - block * rows : 2 * seq_len - block * rows]

    units = [(block, head) for block in range(seq_len // rows) for head in range(2)]
    ahead = scored(*units[0])
    summed = [None, None]
    for number, (block, head) in enumerate(units):
        at = slice(block * rows, (block + 1) * rows)
        scores = ahead
        if number + 1 < len(units):
            ahead = scored(*units[number + 1])
        top = jnp.max(scores, axis=-1, keepdims=True)
        weights = jnp.exp(scores - top).astype(LOW)
        e_ref[head, at, :] = weights
        summed[head] = matmul_nn(weights, values_h[head])
        if head == 1:
            totals = jnp.where(own_lanes[0], summed[1], summed[0])
            inverse = 1.0 / pltpu.roll(totals, LANES // 2, 1)
            mixed = jnp.where(own_lanes[0], summed[0], summed[1]) * inverse
            mixed_ref[at, :] = mixed
            low_ref[at, :] = mixed.astype(LOW)
            inv_ref[at, :] = inverse
    acc_ref[...] += matmul_nt(low_ref[...], wo_ref[...])

    @pl.when(pair == pl.num_programs(0) - 1)
    def _():
        half = part0_ref.shape[0]
        part0_ref[...] = acc_ref[:half, :].astype(LOW)
        part1_ref[...] = acc_ref[half:, :].astype(LOW)


def summed_halves(left_ref, right_ref):
    return left_ref[...].astype(HIGH) + right_ref[...].astype(HIGH)


def feed_body(
    row_steps,
    place_ref,
    x_ref,
    p0_ref,
    p1_ref,
    r0_ref,
    r1_ref,
    g_ref,
    gain_ref,
    gu_own_ref,
    gu_other_ref,
    ud_own_ref,
    ud_other_ref,
    unit_ref,
    scale_ref,
    dn_ref,
    send_ref,
    own_ref,
    dgu_own_ref,
    dgu_other_ref,
    dud_own_ref,
    dud_other_ref,
    gu_ref,
    ud_ref,
    turned_x_ref,
    turned_y_ref,
    g_turned_ref,
    hidden_ref,
    dgate_up_ref,
):
    step = pl.program_id(0)
    columns = hidden_ref.shape[1] // 2
    pl.when(step < row_steps)(
        functools.partial(
            feed_rows,
            step,
            row_steps,
            place_ref,
            (x_ref, p0_ref, p1_ref, r0_ref, r1_ref, g_ref, gain_ref),
            (gu_own_ref, gu_other_ref, ud_own_ref, ud_other_ref),
            (unit_ref, scale_ref, dn_ref, send_ref, own_ref),
            (gu_ref, ud_ref, turned_x_ref, turned_y_ref, g_turned_ref, hidden_ref, dgate_up_ref),
        )
    )

    def product(left_ref, right, own_out_ref, other_out_ref):
        for half, out_ref in enumerate((own_out_ref, other_out_ref)):
            left = left_ref[half].reshape(out_ref.shape[0], -1)
            out_ref[...] = matmul_nn(left, right).astype(LOW)

    for block in range(6):

        @pl.when(step == row_steps + block)
        def _(block=block):
            if block < 3:
                right = dgate_up_ref[:, block * columns : (block + 1) * columns]
                product(turned_x_ref, right, dgu_own_ref, dgu_other_ref)
            elif block == 3:
                right = dgate_up_ref[:, block * columns : (block + 1) * columns]
                product(turned_y_ref, right, dud_own_ref, dud_other_ref)
            else:
                right = hidden_ref[:, (block - 4) * columns : (block - 3) * columns]
                product(g_turned_ref, right, dud_own_ref, dud_other_ref)


def feed_rows(step, row_steps, place_ref, inputs, weights, outputs, scratch):
    x_ref, p0_ref, p1_ref, r0_ref, r1_ref, g_ref, gain_ref = inputs
    gu_own_ref, gu_other_ref, ud_own_ref, ud_other_ref = weights
    unit_ref, scale_ref, dn_ref, send_ref, own_ref = outputs
    gu_ref, ud_ref, turned_x_ref, turned_y_ref, g_turned_ref, hidden_ref, dgate_up_ref = scratch
    rows = x_ref.shape[0]
    late = (step < row_steps // 2) == (place_ref[2] == 0)
    position = lax.rem(step + (row_steps // 2) * (1 - place_ref[2]), row_steps)
    at = pl.ds(pl.multiple_of(position * rows, rows), rows)

    @pl.when(step == 0)
    def _():
        put_weights(gu_ref, gu_own_ref, gu_other_ref, True, place_ref[1])
        put_weights(ud_ref, ud_own_ref, ud_other_ref, False, place_ref[0])

    attended = x_ref[...].astype(HIGH) + jnp.where(
        late, summed_halves(p1_ref, r1_ref), summed_halves(p0_ref, r0_ref)
    )
    unit, scale = rms_parts(attended)
    normed = (unit * gain_ref[...]).astype(LOW)
    unit_ref[...] = unit.astype(LOW)
    scale_ref[...] = jnp.broadcast_to(scale, scale_ref.shape)
    put_turned(turned_x_ref, normed, True, place_ref[1], at)
    put_turned(turned_y_ref, normed, False, place_ref[0], at)
    cotangent = g_ref[...]
    put_turned(g_turned_ref, cotangent, False, place_ref[0], at)
    root = 0.7978845608028654
    columns = hidden_ref.shape[1] // 2
    products = []
    for part in range(2):
        w_gate = matrix(gu_ref, part * columns, columns)
        w_up = matrix(ud_ref, 0, columns) if part else matrix(gu_ref, 2 * columns, columns)
        w_down = matrix(ud_ref, (1 + part) * columns, columns)
        gate = matmul_nn(normed, w_gate)
        up = matmul_nn(normed, w_up)
        d_hidden = matmul_nn(cotangent, w_down)
        products.append((gate, up, d_hidden, w_gate, w_up, w_down))
    out = 0.0
    d_normed = 0.0
    for part, (gate, up, d_hidden, w_gate, w_up, w_down) in enumerate(products):
        square = gate * gate
        bend = jnp.tanh(gate * (root + (root * 0.044715) * square))
        half = 0.5 + 0.5 * bend
        gelu = gate * half
        slope = half + (0.5 * gate) * (1.0 - bend * bend) * (root + (3 * root * 0.044715) * square)
        hidden = (gelu * up).astype(LOW)
        d_gate = (d_hidden * up * slope).astype(LOW)
        d_up = (d_hidden * gelu).astype(LOW)
        hidden_ref[at, part * columns : (part + 1) * columns] = hidden
        dgate_up_ref[at, part * columns : (part + 1) * columns] = d_gate
        dgate_up_ref[at, (2 + part) * columns : (3 + part) * columns] = d_up
        d_normed = d_normed + matmul_nt(d_gate, w_gate) + matmul_nt(d_up, w_up)
        out = out + matmul_nt(hidden, w_down)
    dn_ref[...] = d_normed.astype(LOW)

    @pl.when(step < row_steps // 2)
    def _():
        send_ref[...] = out.astype(LOW)

    @pl.when(step >= row_steps // 2)
    def _():
        own_ref[...] = attended + out


def grads_body(first_count, left0_ref, left1_ref, right0_ref, right1_ref, own_ref, other_ref):
    step = pl.program_id(0)
    half = own_ref.shape[0]

    def product(left_ref, right_ref):
        right = right_ref[...]
        own_ref[...] = matmul_nn(left_ref[:half, :], right).astype(LOW)
        other_ref[...] = matmul_nn(left_ref[half:, :], right).astype(LOW)

    pl.when(step < first_count)(functools.partial(product, left0_ref, right0_ref))
    pl.when(step >= first_count)(functools.partial(product, left1_ref, right1_ref))


def turn_body(
    place_ref,
    unit_ref,
    scale_ref,
    g_ref,
    a_ref,
    b_ref,
    gain_ref,
    wo_ref,
    datt_ref,
    turned_ref,
    dmix_ref,
    dgain_ref,
):
    step = pl.program_id(0)
    unit = unit_ref[...].astype(HIGH)
    scale = scale_ref[:, :1]
    d_normed = a_ref[...].astype(HIGH) + b_ref[...].astype(HIGH)
    d_gain = jnp.sum(d_normed * unit, axis=0, keepdims=True)
    d_attended = g_ref[...].astype(HIGH) + rms_back(d_normed, unit, scale, gain_ref[...])
    d_low = d_attended.astype(LOW)
    put_turned(turned_ref, d_low, False, place_ref[0])
    dmix_ref[...] = matmul_nn(d_low, wo_ref[...]).astype(LOW)

    @pl.when(step == 0)
    def _():
        dgain_ref[...] = d_gain

    @pl.when(step != 0)
    def _():
        dgain_ref[...] += d_gain

    @pl.when(step >= pl.num_programs(0) // 2)
    def _():
        datt_ref[...] = d_attended


def backward_body(
    q_ref,
    k_ref,
    v_ref,
    e_ref,
    dmix_ref,
    mixed_ref,
    inv_ref,
    dq_ref,
    dk_ref,
    dv_ref,
    strip_ref,
    table_ref,
    dkt_ref,
    dvt_ref,
):
    seq_len = k_ref.shape[0]
    rows = table_ref.shape[1]
    low_masks = head_masks(LOW)
    masks = head_masks(HIGH)
    keys = k_ref[...]
    values = v_ref[...]
    keys_h = tuple(keys * low_masks[h] for h in range(2))
    table_ref[...] = jnp.zeros_like(table_ref)
    for block in range(seq_len // rows):
        at = slice(block * rows, (block + 1) * rows)
        queries = q_ref[at, :]
        scaled = (dmix_ref[at, :].astype(HIGH) * inv_ref[at, :]).astype(LOW)
        product = scaled.astype(HIGH) * mixed_ref[at, :]
        d_query = jnp.zeros((rows, LANES), HIGH)
        d_key = jnp.zeros((LANES, seq_len), HIGH)
        d_value = jnp.zeros((LANES, seq_len), HIGH)
        for head in range(2):
            scaled_h = scaled * low_masks[head]
            delta = jnp.sum(product * masks[head], axis=-1, keepdims=True)
            weights = e_ref[head, at, :]
            d_scores = weights.astype(HIGH) * (matmul_nt(scaled_h, values) - delta)
            d_low = d_scores.astype(LOW)
            window = slice(seq_len - block * rows, 2 * seq_len - block * rows)
            table_ref[head, :, window] += d_scores
            d_query = d_query + matmul_nn(d_low, keys_h[head])
            d_key = d_key + matmul_tn(queries * low_masks[head], d_low)
            d_value = d_value + matmul_tn(scaled_h, weights)
        dq_ref[at, :] = d_query.astype(LOW)
        if block == 0:
            dkt_ref[...] = d_key
            dvt_ref[...] = d_value
        else:
            dkt_ref[...] += d_key
            dvt_ref[...] += d_value
    dk_ref[...] = dkt_ref[...].T.astype(LOW)
    dv_ref[...] = dvt_ref[...].T.astype(LOW)
    width = 2 * seq_len
    sub = lax.broadcasted_iota(jnp.int32, (8, 1), 0)
    for head in range(2):
        total = table_ref[head, 0:8, :]
        for group in range(1, rows // 8):
            part = table_ref[head, 8 * group : 8 * group + 8, :]
            total = total + pltpu.roll(part, width - 8 * group, 1)
        for bit in (1, 2, 4):
            total = jnp.where((sub & bit) != 0, pltpu.roll(total, width - bit, 1), total)
        strip_ref[0, head : head + 1, :] = jnp.sum(total, axis=0, keepdims=True)


def spread_body(
    place_ref, x_ref, dq_ref, dk_ref, dv_ref, qkv_ref, send_ref, own_ref, dgain_ref
):
    step = pl.program_id(0)
    width = dq_ref.shape[1]
    unit, _ = rms_parts(x_ref[...].astype(HIGH))
    d_normed = (
        matmul_nt(dq_ref[...], qkv_ref[:, :width])
        + matmul_nt(dk_ref[...], qkv_ref[:, width : 2 * width])
        + matmul_nt(dv_ref[...], qkv_ref[:, 2 * width :])
    )
    d_gain = jnp.sum(d_normed * unit, axis=0, keepdims=True)

    @pl.when(step == 0)
    def _():
        dgain_ref[...] = d_gain

    @pl.when(step != 0)
    def _():
        dgain_ref[...] += d_gain

    @pl.when(step < pl.num_programs(0) // 2)
    def _():
        send_ref[...] = d_normed.astype(LOW)

    @pl.when(step >= pl.num_programs(0) // 2)
    def _():
        own_ref[...] = d_normed


def finish_body(x_ref, own_ref, other_ref, datt_ref, gain_ref, out_ref):
    unit, scale = rms_parts(x_ref[...].astype(HIGH))
    d_normed = own_ref[...] + other_ref[...].astype(HIGH)
    out_ref[...] = (datt_ref[...] + rms_back(d_normed, unit, scale, gain_ref[...])).astype(LOW)


def flat_left(left):
    return left.reshape(-1, left.shape[-1])


def weight_grads(first, second, columns, micros):
    left0, right0, at0, count0 = first
    left1, right1, at1, count1 = second
    left0, left1 = flat_left(left0), flat_left(left1)
    height, depth = left0.shape
    steps = count0 + count1
    half_spec = pl.BlockSpec((height // 2, columns), lambda i: (0, i))
    return call(
        functools.partial(grads_body, count0),
        (steps,),
        [
            whole((height, depth)),
            whole((height, depth)),
            pl.BlockSpec((depth, columns), lambda i: (0, at0 + jnp.minimum(i, count0 - 1))),
            pl.BlockSpec((depth, columns), lambda i: (0, at1 + jnp.maximum(i - count0, 0))),
        ],
        [half_spec, half_spec],
        [shaped((height // 2, steps * columns), LOW)] * 2,
        micros=micros,
    )(left0, left1, right0, right1)


def on_core_pair(
    tokens,
    cotangent,
    gain_attn,
    w_query,
    w_key,
    w_value,
    w_out,
    rel_table,
    buckets,
    gain_ffn,
    w_gate,
    w_up,
    w_down,
):
    own_rows, features = tokens.shape
    seq_len = 2 * own_rows
    width = w_query.shape[1]
    units = w_gate.shape[1]
    chunk = units // 2
    pairs = width // LANES
    bucket_count, head_count = rel_table.shape
    local_heads = head_count // 2
    count = lax.axis_size("dp")
    far_bit, y_bit, x_bit = dp_place()
    me = lax.axis_index("mp")
    place = jnp.stack([y_bit, x_bit, me, far_bit]).astype(jnp.int32)
    rows = MXU_ROWS
    steps = seq_len // rows
    half_steps = steps // 2
    block_rows = w_query.shape[0]

    def swapped(array):
        return lax.ppermute(array, "mp", [(0, 1), (1, 0)])

    def in_order(array, other):
        first = jnp.where(me == 0, array, other)
        second = jnp.where(me == 0, other, array)
        return jnp.concatenate([first, second], axis=0)

    early = jnp.concatenate([w_query, w_key, w_value, w_out.T], axis=1)
    late = jnp.concatenate([w_gate, w_up, w_down.T], axis=1)
    early_pieces = far_pieces(early)
    x_other, g_other = swapped(tokens), swapped(cotangent)
    late_pieces = far_pieces(late)
    early_pieces = together(*early_pieces)
    near = far_stack(early, list(early_pieces))
    qk = near[:, : 2 * width]
    vo = near[:, 2 * width :]
    qk_next, vo_next = together(over_y(qk), over_x(vo))
    qk_own = in_bit_order(qk, qk_next, y_bit)
    vo_own = in_bit_order(vo, vo_next, x_bit)
    qk_other = over_x(qk_own)
    vo_other = over_y(vo_own)
    x_all = in_order(tokens, x_other)
    g_all = in_order(cotangent, g_other)
    qk_other, vo_other, x_all, g_all, *late_pieces = together(
        qk_other, vo_other, x_all, g_all, *late_pieces
    )
    near = far_stack(late, late_pieces)
    gu = near[:, : 3 * chunk]
    ud = near[:, 3 * chunk :]
    gu_next = over_y(gu)
    ud_next = over_x(ud)

    gain_a = gain_attn.reshape(1, features)
    gain_f = gain_ffn.reshape(1, features)

    one_hot = (buckets[:, None] == jnp.arange(bucket_count, dtype=jnp.int32)[None, :]).astype(HIGH)
    one_hot = jnp.pad(one_hot, ((1, 0), (0, 0)))
    my_table = lax.dynamic_slice_in_dim(rel_table, me * local_heads, local_heads, 1)
    strip = lax.dot_general(my_table, one_hot, (((0,), (1,)), ((), ())), precision=precise)
    strip = strip.reshape(pairs, 2, 2 * seq_len)

    def row_block(columns):
        return pl.BlockSpec((rows, columns), lambda i, *_: (i, 0))

    turned_shape = (2, 2, 2, 2, block_rows)
    turned_block = pl.BlockSpec(turned_shape + (rows,), lambda i, *_: (0, 0, 0, 0, 0, i))
    turned = shaped(turned_shape + (seq_len,), LOW)
    full_block = (count // 4, 2, 2, block_rows, 2 * width)
    half_block = (features // 2, 2 * width)
    normed_x_turned, normed_y_turned, queries, keys, values, w_qkv, w_o = call(
        project_body,
        (steps,),
        [row_block(features), whole((1, features))] + [whole(half_block)] * 4,
        [turned_block, turned_block]
        + [row_block(width)] * 3
        + [result((features, 3 * width)), result((features, width))],
        [turned, turned]
        + [shaped((seq_len, width), LOW)] * 3
        + [shaped((features, 3 * width), LOW), shaped((features, width), LOW)],
        [pltpu.VMEM(full_block, LOW), pltpu.VMEM(full_block, LOW)],
        prefetch=1,
        micros=7,
    )(place, x_all, gain_a, qk_own, qk_other, vo_own, vo_other)

    gu_next, ud_next, queries = together(gu_next, ud_next, queries)
    gu_own = in_bit_order(gu, gu_next, y_bit)
    ud_own = in_bit_order(ud, ud_next, x_bit)
    gu_other = over_x(gu_own)
    ud_other = over_y(ud_own)

    pair_block = pl.BlockSpec((seq_len, LANES), lambda p: (0, p))
    e_block = pl.BlockSpec((2, seq_len, seq_len), lambda p: (p, 0, 0))
    strip_block = pl.BlockSpec((1, 2, 2 * seq_len), lambda p: (p, 0, 0))
    table_scratch = pltpu.VMEM((2, rows, 2 * seq_len), HIGH)
    weights_e, mixed, mixed_low, inverse, part0, part1 = call(
        attend_body,
        (pairs,),
        [
            pair_block,
            pair_block,
            pair_block,
            strip_block,
            pl.BlockSpec((features, LANES), lambda p: (0, p)),
        ],
        [e_block, pair_block, pair_block, pair_block] + [result((own_rows, features))] * 2,
        [
            shaped((2 * pairs, seq_len, seq_len), LOW),
            shaped((seq_len, width), HIGH),
            shaped((seq_len, width), LOW),
            shaped((seq_len, width), HIGH),
            shaped((own_rows, features), LOW),
            shaped((own_rows, features), LOW),
        ],
        [table_scratch, pltpu.VMEM((seq_len, features), HIGH)],
        micros=20,
    )(queries, keys, values, strip, w_o)
    gu_other, ud_other, came0, came1 = together(
        gu_other, ud_other, swapped(part0), swapped(part1)
    )
    parts = (part0, part1, came0, came1)

    def moved(i, m):
        return (jnp.minimum(i, steps - 1) + half_steps * (1 - m[2])) % steps

    def turned_row(columns):
        return pl.BlockSpec((rows, columns), lambda i, m: (moved(i, m), 0))

    half0_row = pl.BlockSpec(
        (rows, features), lambda i, m: (jnp.minimum(moved(i, m), half_steps - 1), 0)
    )
    half1_row = pl.BlockSpec(
        (rows, features), lambda i, m: (jnp.maximum(moved(i, m) - half_steps, 0), 0)
    )
    moved_block = pl.BlockSpec(turned_shape + (rows,), lambda i, m: (0, 0, 0, 0, 0, moved(i, m)))
    send_row = pl.BlockSpec((rows, features), lambda i, m: (jnp.minimum(i, half_steps - 1), 0))
    keep_row = pl.BlockSpec(
        (rows, features),
        lambda i, m: (jnp.clip(i - half_steps, 0, half_steps - 1), 0),
    )

    def grads_block(first):
        return pl.BlockSpec(
            (features // 2, chunk), lambda i, m: (0, jnp.clip(i - steps - first, 0, 2))
        )

    full_block = (count // 4, 2, 2, block_rows, 3 * chunk)
    half_block = (features // 2, 3 * chunk)
    half_grads = shaped((features // 2, 3 * chunk), LOW)
    unit_f, scale_f, dn_part, out_send, out_own, gu_own, gu_send, ud_own, ud_send = call(
        functools.partial(feed_body, steps),
        (steps + 6,),
        [turned_row(features)]
        + [half0_row, half1_row] * 2
        + [turned_row(features), whole((1, features))]
        + [whole(half_block)] * 4,
        [turned_row(features), turned_row(LANES), turned_row(features), send_row, keep_row]
        + [grads_block(0)] * 2
        + [grads_block(3)] * 2,
        [
            shaped((seq_len, features), LOW),
            shaped((seq_len, LANES), HIGH),
            shaped((seq_len, features), LOW),
            shaped((own_rows, features), LOW),
            shaped((own_rows, features), HIGH),
        ]
        + [half_grads] * 4,
        [pltpu.VMEM(full_block, LOW), pltpu.VMEM(full_block, LOW)]
        + [pltpu.VMEM(turned_shape + (seq_len,), LOW)] * 3
        + [pltpu.VMEM((seq_len, units), LOW), pltpu.VMEM((seq_len, 2 * units), LOW)],
        prefetch=1,
        micros=28,
    )(place, x_all, *parts, g_all, gain_f, gu_own, gu_other, ud_own, ud_other)
    dn_other = swapped(dn_part)
    gu_came = over_x(gu_send)
    ud_came = over_y(ud_send)

    d_attended, d_low_turned, d_mixed, d_gain_f = call(
        turn_body,
        (steps,),
        [turned_row(features), turned_row(LANES)]
        + [turned_row(features)] * 3
        + [whole((1, features)), whole((features, width))],
        [keep_row, moved_block, turned_row(width), result((1, features))],
        [
            shaped((own_rows, features), HIGH),
            turned,
            shaped((seq_len, width), LOW),
            shaped((1, features), HIGH),
        ],
        prefetch=1,
        micros=4,
    )(place, unit_f, scale_f, g_all, dn_part, dn_other, gain_f, w_o)
    out_other = swapped(out_send)

    d_query, d_key, d_value, d_strip = call(
        backward_body,
        (pairs,),
        [pair_block, pair_block, pair_block, e_block, pair_block, pair_block, pair_block],
        [pair_block, pair_block, pair_block, strip_block],
        [shaped((seq_len, width), LOW)] * 3 + [shaped((pairs, 2, 2 * seq_len), HIGH)],
        [table_scratch, pltpu.VMEM((LANES, seq_len), HIGH), pltpu.VMEM((LANES, seq_len), HIGH)],
        micros=4,
    )(queries, keys, values, weights_e, d_mixed, mixed, inverse)

    gu_came, ud_came, out_other, d_query, d_key, d_value, d_strip = together(
        gu_came, ud_came, out_other, d_query, d_key, d_value, d_strip
    )

    def next_half(own, came, bit):
        return (
            add_low(part_of(own, bit, 2), part_of(came, bit, 2)),
            add_low(part_of(own, 1 - bit, 2), part_of(came, 1 - bit, 2)),
        )

    gu_own, gu_send = next_half(gu_own, gu_came, y_bit)
    ud_own, ud_send = next_half(ud_own, ud_came, x_bit)
    gu_came = over_y(gu_send)
    ud_came = over_x(ud_send)

    qk_own, qk_send = weight_grads(
        (normed_x_turned, d_query, 0, 1), (normed_x_turned, d_key, 0, 1), width, 5
    )
    qk_send, d_value = together(qk_send, d_value)
    vo_own, vo_send = weight_grads(
        (normed_y_turned, d_value, 0, 1), (d_low_turned, mixed_low, 0, 1), width, 5
    )
    output = (out_own + out_other.astype(HIGH)).astype(LOW)

    gu_came, ud_came, qk_send, vo_send, d_query = together(
        gu_came, ud_came, qk_send, vo_send, d_query
    )
    qk_came = over_x(qk_send)
    vo_came = over_y(vo_send)
    gu_own, gu_send = next_half(gu_own, gu_came, far_bit % 2)
    gu_came = over_far_bit(gu_send, 0)

    def inner_part(array, index):
        blocks = array.reshape(2, 2, block_rows, -1)
        return lax.dynamic_index_in_dim(blocks, index, 1, False).reshape(2 * block_rows, -1)

    ud_send = add_low(inner_part(ud_own, 1 - far_bit // 2), inner_part(ud_came, 1 - far_bit // 2))
    ud_own = add_low(inner_part(ud_own, far_bit // 2), inner_part(ud_came, far_bit // 2))
    ud_came = over_far_bit(ud_send, 1)

    dna_send, dna_own, d_gain_a = call(
        spread_body,
        (steps,),
        [turned_row(features)] + [turned_row(width)] * 3 + [whole((features, 3 * width))],
        [send_row, keep_row, result((1, features))],
        [
            shaped((own_rows, features), LOW),
            shaped((own_rows, features), HIGH),
            shaped((1, features), HIGH),
        ],
        prefetch=1,
        micros=2,
    )(place, x_all, d_query, d_key, d_value, w_qkv)
    qk_came, vo_came, gu_came, ud_came, dna_send, d_gain_a, d_strip = together(
        qk_came, vo_came, gu_came, ud_came, dna_send, d_gain_a, d_strip
    )
    gu_own, gu_send = next_half(gu_own, gu_came, far_bit // 2)
    ud_own, ud_send = next_half(ud_own, ud_came, far_bit % 2)
    gu_came = over_far_bit(gu_send, 1)
    ud_came = over_far_bit(ud_send, 0)
    dna_other = swapped(dna_send)
    qk_own, qk_send = next_half(qk_own, qk_came, y_bit)
    vo_own, vo_send = next_half(vo_own, vo_came, x_bit)
    qk_came = over_y(qk_send)
    vo_came = over_x(vo_send)

    d_bias = d_strip.reshape(local_heads, 2 * seq_len)
    my_d_table = lax.dot_general(one_hot, d_bias, (((0,), (1,)), ((), ())), precision=precise)
    d_table = lax.dynamic_update_slice_in_dim(
        jnp.zeros_like(rel_table), my_d_table, me * local_heads, 1
    )
    small_early = jnp.concatenate([0.5 * d_gain_f, d_table.reshape(1, -1)], axis=1)
    small_early = jnp.pad(small_early, ((0, 0), (0, -(features + small_early.shape[1]) % (4 * width))))
    small = jnp.concatenate([d_gain_a, small_early], axis=1)
    small = small.reshape(-1, 4 * width)
    small = small + swapped(small)
    small = small + over_x(small) + over_y(small) + over_xy(small)

    d_tokens = call(
        finish_body,
        (half_steps,),
        [row_block(features)] * 4 + [whole((1, features))],
        row_block(features),
        shaped((own_rows, features), LOW),
        micros=3.5,
    )(tokens, dna_own, dna_other, d_attended, gain_a)

    qk_came, vo_came, gu_came, ud_came, small = together(
        qk_came, vo_came, gu_came, ud_came, small
    )
    head_own = jnp.concatenate([qk_own, vo_own], axis=-1)
    head_came = jnp.concatenate([qk_came, vo_came], axis=-1)
    total = add_low(head_own, head_came)

    def far_part(far):
        return part_of(total, 2 * (far % 2) + far // 2, 4)

    small_rows = in_terms(small)
    pieces = [
        over_far(jnp.concatenate([far_part((far_bit + k) % 4), small_rows], axis=0), k)
        for k in range(1, 4)
    ]
    *pieces, d_tokens = together(*pieces, d_tokens)
    small = sum((from_terms(piece[block_rows:], small.shape[0]) for piece in pieces), small)
    small = small.reshape(-1)
    pieces = [piece[:block_rows] for piece in pieces]
    grads_head = sum((piece.astype(HIGH) for piece in pieces), far_part(far_bit).astype(HIGH))
    grads_qk, grads_vo = grads_head[:, : 2 * width], grads_head[:, 2 * width :]
    grads_gu = gu_own.astype(HIGH) + gu_came.astype(HIGH)
    grads_ud = ud_own.astype(HIGH) + ud_came.astype(HIGH)
    return (
        output,
        d_tokens,
        small[:features],
        grads_qk[:, :width],
        grads_qk[:, width:],
        grads_vo[:, :width],
        grads_vo[:, width:].T,
        small[2 * features : 2 * features + rel_table.size].reshape(rel_table.shape),
        small[features : 2 * features],
        grads_gu[:, :units],
        jnp.concatenate([grads_gu[:, units:], grads_ud[:, :chunk]], axis=1),
        grads_ud[:, chunk:].T,
    )


def solution(mesh):
    placed = (
        P(("dp", "mp"), None),
        P(("dp", "mp"), None),
        P(),
        P("dp", "mp"),
        P("dp", "mp"),
        P("dp", "mp"),
        P("mp", "dp"),
        P(),
        P(),
        P(),
        P("dp", "mp"),
        P("dp", "mp"),
        P("mp", "dp"),
    )
    paired = mesh.shape["mp"] == 2 and mesh.shape["dp"] == 16
    body = on_core_pair if paired else on_device
    return jax.shard_map(
        body,
        mesh=mesh,
        in_specs=placed,
        out_specs=(
            P(("dp", "mp"), None),
            P(("dp", "mp"), None),
            P(),
            P("dp", "mp"),
            P("dp", "mp"),
            P("dp", "mp"),
            P("mp", "dp"),
            P(),
            P(),
            P("dp", "mp"),
            P("dp", "mp"),
            P("mp", "dp"),
        ),
        check_vma=False,
    )
```

```python
import functools

import jax
import jax.numpy as jnp
from jax import lax
from jax.experimental import pallas as pl
from jax.experimental.pallas import tpu as pltpu
from jax.sharding import PartitionSpec as P

epsilon = 1e-06
block_limit = 512
precise = lax.Precision.HIGHEST


def as_sent(array):

    def short(part):
        return part.astype(jnp.bfloat16) if part.dtype == jnp.float32 else part

    return jax.tree.map(short, array)


def matmul_nn(left, right):
    return jnp.dot(left, right, preferred_element_type=jnp.float32)


def matmul_nt(left, right):
    return lax.dot_general(
        left, right, (((1,), (1,)), ((), ())), preferred_element_type=jnp.float32
    )


def matmul_tn(left, right):
    return lax.dot_general(
        left, right, (((0,), (0,)), ((), ())), preferred_element_type=jnp.float32
    )


def rms_parts(inputs):
    scale = lax.rsqrt(jnp.mean(inputs * inputs, axis=-1, keepdims=True) + epsilon)
    return (inputs * scale, scale)


def rms_back(d_normed, unit, scale, gain):
    d_unit = d_normed * gain
    return scale * (d_unit - unit * jnp.mean(d_unit * unit, axis=-1, keepdims=True))


def gated(gate_pre, up_pre):
    return jax.nn.gelu(gate_pre, approximate=True) * up_pre


def window_base(first_query, first_key, row_count, seq_len):
    return first_key - first_query - row_count + seq_len


def make_bias(bias_full, base, row_count, width):
    span = width + row_count - 1
    head_count = bias_full.shape[0]
    strip = lax.dynamic_slice_in_dim(bias_full, base, span, 1)
    tiled = jnp.tile(strip, (1, row_count + 1))
    window = tiled[:, row_count - 1 : row_count - 1 + row_count * (span - 1)]
    return window.reshape(head_count, row_count, span - 1)[:, :, :width]


def skew_sum(d_block, row_count, width):
    head_count = d_block.shape[0]
    span = width + row_count - 1
    padded = jnp.pad(d_block, ((0, 0), (0, 0), (row_count - 1, 0)))
    flat = padded.reshape(head_count, row_count * span)
    flat = jnp.pad(flat, ((0, 0), (0, row_count)))
    skewed = flat.reshape(head_count, row_count, span + 1)[:, :, :span]
    return jnp.sum(skewed, axis=1)


def add_window(d_bias, piece, base):
    current = lax.dynamic_slice_in_dim(d_bias, base, piece.shape[1], 1)
    return lax.dynamic_update_slice_in_dim(d_bias, current + piece, base, 1)


def sum_rows(partial_value):
    return lax.psum_scatter(
        partial_value.astype(jnp.bfloat16), "mp", scatter_dimension=0, tiled=True
    ).astype(jnp.float32)


def split_heads(queries, keys_all, values, head_count):
    row_count = queries.shape[0]
    seq_len = keys_all.shape[0]
    head_dim = queries.shape[1] // head_count
    width = min(block_limit, seq_len)
    blocks = seq_len // width
    heads_q = queries.reshape(row_count, head_count, head_dim)
    heads_k = keys_all.reshape(blocks, width, head_count, head_dim)
    heads_v = values.reshape(blocks, width, head_count, head_dim)
    starts = jnp.arange(blocks, dtype=jnp.int32) * width
    return (heads_q, heads_k, heads_v, starts, width)


def attend_forward(queries, keys_all, values, bias_full, head_count, first_row):
    row_count = queries.shape[0]
    seq_len = keys_all.shape[0]
    heads_q, heads_k, heads_v, starts, width = split_heads(queries, keys_all, values, head_count)

    def block_scores(key_block, first_key):
        raw_scores = jnp.einsum(
            "qhd,khd->hqk", heads_q, key_block, preferred_element_type=jnp.float32
        )
        base = window_base(first_row, first_key, row_count, seq_len)
        return raw_scores + make_bias(bias_full, base, row_count, width)

    def stats_step(running, pieces):
        top_now, total = running
        scores = block_scores(pieces[0], pieces[1])
        top_new = jnp.maximum(top_now, jnp.max(scores, axis=-1))
        total = total * jnp.exp(top_now - top_new) + jnp.sum(
            jnp.exp(scores - top_new[..., None]), axis=-1
        )
        return ((top_new, total), None)

    start_top = jnp.full((head_count, row_count), -jnp.inf, jnp.float32)
    start_total = jnp.zeros((head_count, row_count), jnp.float32)
    (top_all, total), _ = lax.scan(stats_step, (start_top, start_total), (heads_k, starts))
    log_total = top_all + jnp.log(total)

    def mix_step(running, pieces):
        scores = block_scores(pieces[0], pieces[2])
        probs_low = jnp.exp(scores - log_total[..., None]).astype(jnp.bfloat16)
        update = jnp.einsum(
            "hqk,khd->qhd", probs_low, pieces[1], preferred_element_type=jnp.float32
        )
        return (running + update, None)

    start_mix = jnp.zeros(heads_q.shape, jnp.float32)
    mixed_f, _ = lax.scan(mix_step, start_mix, (heads_k, heads_v, starts))
    return (mixed_f.reshape(row_count, queries.shape[1]), log_total)


def attend_backward(
    queries, keys_all, values, bias_full, head_count, first_row, log_total, deltas, d_mixed
):
    row_count = queries.shape[0]
    seq_len = keys_all.shape[0]
    heads_q, heads_k, heads_v, starts, width = split_heads(queries, keys_all, values, head_count)
    heads_d = d_mixed.reshape(heads_q.shape)

    def back_step(running, pieces):
        d_query, d_bias = running
        key_block, value_block, first_key = pieces
        base = window_base(first_row, first_key, row_count, seq_len)
        scores = jnp.einsum("qhd,khd->hqk", heads_q, key_block, preferred_element_type=jnp.float32)
        scores = scores + make_bias(bias_full, base, row_count, width)
        probs = jnp.exp(scores - log_total[..., None])
        d_probs = jnp.einsum(
            "qhd,khd->hqk", heads_d, value_block, preferred_element_type=jnp.float32
        )
        d_scores = (probs * (d_probs - deltas[..., None])).astype(jnp.bfloat16)
        d_query = d_query + jnp.einsum(
            "hqk,khd->qhd", d_scores, key_block, preferred_element_type=jnp.float32
        )
        d_bias = add_window(d_bias, skew_sum(d_scores.astype(jnp.float32), row_count, width), base)
        probs_low = probs.astype(jnp.bfloat16)
        d_value = jnp.einsum("hqk,qhd->khd", probs_low, heads_d, preferred_element_type=jnp.float32)
        d_key = jnp.einsum("hqk,qhd->khd", d_scores, heads_q, preferred_element_type=jnp.float32)
        return ((d_query, d_bias), (d_key, d_value))

    start_query = jnp.zeros(heads_q.shape, jnp.float32)
    (d_query, d_bias), kv_parts = lax.scan(
        back_step, (start_query, jnp.zeros_like(bias_full)), (heads_k, heads_v, starts)
    )
    feature_count = queries.shape[1]
    d_query = d_query.reshape(row_count, feature_count)
    return (
        d_query,
        d_bias,
        kv_parts[0].reshape(seq_len, feature_count),
        kv_parts[1].reshape(seq_len, feature_count),
    )


def on_device(
    tokens,
    cotangent,
    gain_attn,
    w_query,
    w_key,
    w_value,
    w_out,
    rel_table,
    buckets,
    gain_ffn,
    w_gate,
    w_up,
    w_down,
):
    head_count = rel_table.shape[1]
    bucket_count = rel_table.shape[0]
    inputs = tokens.astype(jnp.float32)
    row_count = inputs.shape[0]
    feature_count = inputs.shape[1]
    first_row = lax.axis_index("mp") * row_count
    attn_parts = (w_query, w_key, w_value, w_out.T)
    ffn_parts = (w_gate, w_up, w_down.T)
    ffn_cols = ()
    col_parts = lax.all_gather(as_sent(attn_parts + ffn_cols), "mp", axis=1, tiled=True)
    full_parts = lax.all_gather(as_sent(tuple(col_parts) + ffn_parts), "dp", axis=0, tiled=True)
    query_full, key_full, value_full, out_full, gate_full, up_full, down_full = full_parts
    unit_a, scale_a = rms_parts(inputs)
    normed_a = (unit_a * gain_attn).astype(jnp.bfloat16)
    queries = matmul_nn(normed_a, query_full).astype(jnp.bfloat16)
    own_keys = matmul_nn(normed_a, key_full).astype(jnp.bfloat16)
    own_values = matmul_nn(normed_a, value_full).astype(jnp.bfloat16)
    keys_all, values = (
        lax.all_gather(own_keys, "mp", axis=0, tiled=True),
        lax.all_gather(own_values, "mp", axis=0, tiled=True),
    )
    one_hot = (buckets[:, None] == jnp.arange(bucket_count, dtype=jnp.int32)[None, :]).astype(
        jnp.float32
    )
    bias_full = jnp.dot(one_hot, rel_table, precision=precise).T
    mixed_f, log_total = attend_forward(queries, keys_all, values, bias_full, head_count, first_row)
    mixed_out = mixed_f.astype(jnp.bfloat16)
    attended = inputs + matmul_nt(mixed_out, out_full)
    unit_f, scale_f = rms_parts(attended)
    normed_f = (unit_f * gain_ffn).astype(jnp.bfloat16)
    normed_seq, cot_seq = (
        lax.all_gather(normed_f, "mp", axis=0, tiled=True),
        lax.all_gather(cotangent, "mp", axis=0, tiled=True),
    )
    gate_pre = matmul_nn(normed_seq, gate_full)
    up_pre = matmul_nn(normed_seq, up_full)
    hidden = gated(gate_pre, up_pre).astype(jnp.bfloat16)
    output = attended + sum_rows(matmul_nt(hidden, down_full))
    d_hidden = matmul_nn(cot_seq, down_full)
    d_down = matmul_tn(cot_seq, hidden)
    _, pull_gate = jax.vjp(gated, gate_pre, up_pre)
    d_gate, d_up = pull_gate(d_hidden)
    d_gate = d_gate.astype(jnp.bfloat16)
    d_up = d_up.astype(jnp.bfloat16)
    d_normed_f = sum_rows(matmul_nt(d_gate, gate_full) + matmul_nt(d_up, up_full))
    d_gate_w = matmul_tn(normed_seq, d_gate)
    d_up_w = matmul_tn(normed_seq, d_up)
    d_gain_f = jnp.sum(d_normed_f * unit_f, axis=0)
    d_attended = cotangent.astype(jnp.float32) + rms_back(d_normed_f, unit_f, scale_f, gain_ffn)
    d_att_low = d_attended.astype(jnp.bfloat16)
    d_out_w = matmul_tn(d_att_low, mixed_out)
    d_mixed = matmul_nn(d_att_low, out_full).astype(jnp.bfloat16)
    head_dim = feature_count // head_count
    deltas = jnp.sum(
        (d_mixed.astype(jnp.float32) * mixed_f).reshape(row_count, head_count, head_dim), axis=-1
    ).T
    d_query, d_bias, d_keys_part, d_values_part = attend_backward(
        queries, keys_all, values, bias_full, head_count, first_row, log_total, deltas, d_mixed
    )
    d_keys_own, d_values_own = (
        lax.psum_scatter(
            d_keys_part.astype(jnp.bfloat16), "mp", scatter_dimension=0, tiled=True
        ).astype(jnp.float32),
        lax.psum_scatter(
            d_values_part.astype(jnp.bfloat16), "mp", scatter_dimension=0, tiled=True
        ).astype(jnp.float32),
    )
    d_keys_own = d_keys_own.astype(jnp.bfloat16)
    d_values_own = d_values_own.astype(jnp.bfloat16)
    d_query = d_query.astype(jnp.bfloat16)
    d_normed_a = (
        matmul_nt(d_query, query_full)
        + matmul_nt(d_keys_own, key_full)
        + matmul_nt(d_values_own, value_full)
    )
    d_query_w = matmul_tn(normed_a, d_query)
    d_key_w = matmul_tn(normed_a, d_keys_own)
    d_value_w = matmul_tn(normed_a, d_values_own)
    d_gain_a = jnp.sum(d_normed_a * unit_a, axis=0)
    d_tokens = (d_attended + rms_back(d_normed_a, unit_a, scale_a, gain_attn)).astype(jnp.bfloat16)
    d_table = jnp.dot(d_bias, one_hot, precision=precise).T
    row_grads = (
        lax.psum_scatter(
            d_query_w.astype(jnp.bfloat16), "dp", scatter_dimension=0, tiled=True
        ).astype(jnp.float32),
        lax.psum_scatter(
            d_key_w.astype(jnp.bfloat16), "dp", scatter_dimension=0, tiled=True
        ).astype(jnp.float32),
        lax.psum_scatter(
            d_value_w.astype(jnp.bfloat16), "dp", scatter_dimension=0, tiled=True
        ).astype(jnp.float32),
        lax.psum_scatter(
            d_out_w.astype(jnp.bfloat16), "dp", scatter_dimension=0, tiled=True
        ).astype(jnp.float32),
        lax.psum_scatter(
            d_gate_w.astype(jnp.bfloat16), "dp", scatter_dimension=0, tiled=True
        ).astype(jnp.float32),
        lax.psum_scatter(d_up_w.astype(jnp.bfloat16), "dp", scatter_dimension=0, tiled=True).astype(
            jnp.float32
        ),
        lax.psum_scatter(d_down.astype(jnp.bfloat16), "dp", scatter_dimension=0, tiled=True).astype(
            jnp.float32
        ),
    )
    row_grads = tuple(row_grads)
    ffn_late = ()
    col_grads = tuple(
        jax.tree.map(
            lambda part: part.astype(jnp.float32),
            lax.psum_scatter(
                as_sent(row_grads[:4] + ffn_late), "mp", scatter_dimension=1, tiled=True
            ),
        )
    )
    ffn_done = row_grads[4:]
    small_sums = lax.psum((d_gain_a, d_gain_f, d_table), ("dp", "mp"))
    return (
        output.astype(jnp.bfloat16),
        d_tokens,
        small_sums[0],
        col_grads[0],
        col_grads[1],
        col_grads[2],
        col_grads[3].T,
        small_sums[2],
        small_sums[1],
        ffn_done[0],
        ffn_done[1],
        ffn_done[2].T,
    )


MXU_ROWS = 256
LANES = 128
VMEM_LIMIT = 56 * 2**20
PEAK_PER_MICRO = 1_153_500_000
LOW = jnp.bfloat16
HIGH = jnp.float32


def call(
    body, grid, in_specs, out_specs, out_shape, scratch=(), prefetch=0, micros=5, aliases=None
):
    return pl.pallas_call(
        body,
        grid_spec=pltpu.PrefetchScalarGridSpec(
            num_scalar_prefetch=prefetch,
            grid=grid,
            in_specs=in_specs,
            out_specs=out_specs,
            scratch_shapes=list(scratch),
        ),
        out_shape=out_shape,
        input_output_aliases=aliases or {},
        compiler_params=pltpu.CompilerParams(vmem_limit_bytes=VMEM_LIMIT),
        cost_estimate=pl.CostEstimate(
            flops=int(micros * PEAK_PER_MICRO), bytes_accessed=0, transcendentals=0
        ),
    )


def shaped(shape, dtype):
    return jax.ShapeDtypeStruct(shape, dtype)


def whole(shape):
    return pl.BlockSpec(shape, lambda *_: (0,) * len(shape), pipeline_mode=pl.Buffered(1))


def result(shape):
    return pl.BlockSpec(shape, lambda *_: (0,) * len(shape))


def together(*arrays):
    return lax.optimization_barrier(arrays)


def ring_shift(steps, count):
    return [(i, (i + steps) % count) for i in range(count)]


def flip(bit, count):
    return [(i, i ^ bit) for i in range(count)]


def over_x(array):
    return lax.ppermute(array, "dp", flip(1, lax.axis_size("dp")))


def over_y(array):
    return lax.ppermute(array, "dp", flip(2, lax.axis_size("dp")))


def over_xy(array):
    return lax.ppermute(array, "dp", flip(3, lax.axis_size("dp")))


def over_far(array, steps):
    return lax.ppermute(array, "dp", ring_shift(4 * steps, lax.axis_size("dp")))


def dp_place():
    index = lax.axis_index("dp")
    return (index // 4, (index // 2) % 2, index % 2)


def in_bit_order(own, other, bit):
    first = jnp.where(bit == 0, own, other)
    second = jnp.where(bit == 0, other, own)
    return jnp.concatenate([first, second], axis=0)


def far_pieces(shard):
    return [over_far(shard, k) for k in range(1, lax.axis_size("dp") // 4)]


def far_stack(shard, pieces):
    far = len(pieces) + 1
    place = dp_place()[0]
    stacked = jnp.zeros((far,) + shard.shape, shard.dtype)
    for k, piece in enumerate([shard] + pieces):
        stacked = lax.dynamic_update_slice(stacked, piece[None], ((place - k) % far, 0, 0))
    return stacked.reshape(-1, shard.shape[1])


def over_far_bit(array, bit):
    return lax.ppermute(array, "dp", flip(4 << bit, lax.axis_size("dp")))


def part_of(array, index, parts):
    size = array.shape[0] // parts
    return lax.dynamic_slice_in_dim(array, index * size, size, 0)


def add_low(left, right):
    return (left.astype(HIGH) + right.astype(HIGH)).astype(LOW)


def in_terms(array):
    terms, rest = [], array
    for _ in range(3):
        term = lax.optimization_barrier(rest.astype(LOW))
        terms.append(term)
        rest = rest - term.astype(HIGH)
    rows = jnp.concatenate(terms, axis=0)
    return jnp.pad(rows, ((0, -rows.shape[0] % 8), (0, 0)))


def from_terms(rows, height):
    return sum(rows[i * height : (i + 1) * height].astype(HIGH) for i in range(3))


def head_masks(dtype):
    lane = lax.broadcasted_iota(jnp.int32, (1, LANES), 1)
    first = (lane < LANES // 2).astype(HIGH)
    return (first.astype(dtype), (1.0 - first).astype(dtype))


def put_weights(full_ref, own_ref, other_ref, y_first, bit):
    far, rows = full_ref.shape[0], full_ref.shape[3]
    for half_ref, at in ((own_ref, bit), (other_ref, 1 - bit)):
        for near in range(2):
            for place in range(far):
                start = (near * far + place) * rows
                block = half_ref[start : start + rows, :]
                if y_first:
                    full_ref[place, near, at] = block
                else:
                    full_ref[place, at, near] = block


def put_turned(turned_ref, array, x_first, bit, lanes=slice(None)):
    rows = turned_ref.shape[4]
    turned = array.T
    for block in range(turned.shape[0] // rows):
        far, y_bit, x_bit = block // 4, (block // 2) % 2, block % 2
        first, second = (x_bit, y_bit) if x_first else (y_bit, x_bit)
        other = 1 - bit if first else bit
        turned_ref[other, second, far % 2, far // 2, :, lanes] = turned[
            block * rows : (block + 1) * rows
        ]


def matrix(full_ref, start, columns):
    part = full_ref[:, :, :, :, start : start + columns]
    return part.reshape(-1, columns)


def project_body(
    place_ref,
    x_ref,
    gain_ref,
    qk_own_ref,
    qk_other_ref,
    vo_own_ref,
    vo_other_ref,
    turned_x_ref,
    turned_y_ref,
    q_ref,
    k_ref,
    v_ref,
    qkv_ref,
    wo_ref,
    qk_ref,
    vo_ref,
):
    width = q_ref.shape[1]

    @pl.when(pl.program_id(0) == 0)
    def _():
        put_weights(qk_ref, qk_own_ref, qk_other_ref, True, place_ref[1])
        put_weights(vo_ref, vo_own_ref, vo_other_ref, False, place_ref[0])
        qkv_ref[:, : 2 * width] = matrix(qk_ref, 0, 2 * width)
        qkv_ref[:, 2 * width :] = matrix(vo_ref, 0, width)
        wo_ref[...] = matrix(vo_ref, width, width)

    unit, _ = rms_parts(x_ref[...].astype(HIGH))
    normed = (unit * gain_ref[...]).astype(LOW)
    put_turned(turned_x_ref, normed, True, place_ref[1])
    put_turned(turned_y_ref, normed, False, place_ref[0])
    q_ref[...] = matmul_nn(normed, qkv_ref[:, :width]).astype(LOW)
    k_ref[...] = matmul_nn(normed, qkv_ref[:, width : 2 * width]).astype(LOW)
    v_ref[...] = matmul_nn(normed, qkv_ref[:, 2 * width :]).astype(LOW)


def attend_body(
    q_ref, k_ref, v_ref, strip_ref, wo_ref, e_ref, mixed_ref, low_ref, inv_ref, part0_ref, part1_ref, table_ref, acc_ref
):
    pair = pl.program_id(0)
    seq_len = k_ref.shape[0]
    rows = table_ref.shape[1]
    low_masks = head_masks(LOW)
    own_lanes = tuple(mask > 0.5 for mask in head_masks(HIGH))
    for head in range(2):
        row = jnp.broadcast_to(strip_ref[0, head : head + 1, :], (rows, 2 * seq_len))
        table_ref[head] = pltpu.roll(row, 0, 1, stride=1, stride_axis=0)
    keys = k_ref[...]
    values = v_ref[...]
    values_h = tuple(values * low_masks[h] + low_masks[1 - h] for h in range(2))

    @pl.when(pair == 0)
    def _():
        acc_ref[...] = jnp.zeros_like(acc_ref)

    def scored(block, head):
        at = slice(block * rows, (block + 1) * rows)
        raw = matmul_nt(q_ref[at, :] * low_masks[head], keys)
        return raw + table_ref[head, :, seq_len - block * rows : 2 * seq_len - block * rows]

    units = [(block, head) for block in range(seq_len // rows) for head in range(2)]
    ahead = scored(*units[0])
    summed = [None, None]
    for number, (block, head) in enumerate(units):
        at = slice(block * rows, (block + 1) * rows)
        scores = ahead
        if number + 1 < len(units):
            ahead = scored(*units[number + 1])
        top = jnp.max(scores, axis=-1, keepdims=True)
        weights = jnp.exp(scores - top).astype(LOW)
        e_ref[head, at, :] = weights
        summed[head] = matmul_nn(weights, values_h[head])
        if head == 1:
            totals = jnp.where(own_lanes[0], summed[1], summed[0])
            inverse = 1.0 / pltpu.roll(totals, LANES // 2, 1)
            mixed = jnp.where(own_lanes[0], summed[0], summed[1]) * inverse
            mixed_ref[at, :] = mixed
            low_ref[at, :] = mixed.astype(LOW)
            inv_ref[at, :] = inverse
    acc_ref[...] += matmul_nt(low_ref[...], wo_ref[...])

    @pl.when(pair == pl.num_programs(0) - 1)
    def _():
        half = part0_ref.shape[0]
        part0_ref[...] = acc_ref[:half, :].astype(LOW)
        part1_ref[...] = acc_ref[half:, :].astype(LOW)


def summed_halves(left_ref, right_ref):
    return left_ref[...].astype(HIGH) + right_ref[...].astype(HIGH)


def feed_body(
    row_steps,
    place_ref,
    x_ref,
    p0_ref,
    p1_ref,
    r0_ref,
    r1_ref,
    g_ref,
    gain_ref,
    gu_own_ref,
    gu_other_ref,
    ud_own_ref,
    ud_other_ref,
    unit_ref,
    scale_ref,
    dn_ref,
    send_ref,
    own_ref,
    dgu_own_ref,
    dgu_other_ref,
    dud_own_ref,
    dud_other_ref,
    gu_ref,
    ud_ref,
    turned_x_ref,
    turned_y_ref,
    g_turned_ref,
    hidden_ref,
    dgate_up_ref,
):
    step = pl.program_id(0)
    columns = hidden_ref.shape[1] // 2
    pl.when(step < row_steps)(
        functools.partial(
            feed_rows,
            step,
            row_steps,
            place_ref,
            (x_ref, p0_ref, p1_ref, r0_ref, r1_ref, g_ref, gain_ref),
            (gu_own_ref, gu_other_ref, ud_own_ref, ud_other_ref),
            (unit_ref, scale_ref, dn_ref, send_ref, own_ref),
            (gu_ref, ud_ref, turned_x_ref, turned_y_ref, g_turned_ref, hidden_ref, dgate_up_ref),
        )
    )

    def product(left_ref, right, own_out_ref, other_out_ref):
        for half, out_ref in enumerate((own_out_ref, other_out_ref)):
            left = left_ref[half].reshape(out_ref.shape[0], -1)
            out_ref[...] = matmul_nn(left, right).astype(LOW)

    for block in range(6):

        @pl.when(step == row_steps + block)
        def _(block=block):
            if block < 3:
                right = dgate_up_ref[:, block * columns : (block + 1) * columns]
                product(turned_x_ref, right, dgu_own_ref, dgu_other_ref)
            elif block == 3:
                right = dgate_up_ref[:, block * columns : (block + 1) * columns]
                product(turned_y_ref, right, dud_own_ref, dud_other_ref)
            else:
                right = hidden_ref[:, (block - 4) * columns : (block - 3) * columns]
                product(g_turned_ref, right, dud_own_ref, dud_other_ref)


def feed_rows(step, row_steps, place_ref, inputs, weights, outputs, scratch):
    x_ref, p0_ref, p1_ref, r0_ref, r1_ref, g_ref, gain_ref = inputs
    gu_own_ref, gu_other_ref, ud_own_ref, ud_other_ref = weights
    unit_ref, scale_ref, dn_ref, send_ref, own_ref = outputs
    gu_ref, ud_ref, turned_x_ref, turned_y_ref, g_turned_ref, hidden_ref, dgate_up_ref = scratch
    rows = x_ref.shape[0]
    late = (step < row_steps // 2) == (place_ref[2] == 0)
    position = lax.rem(step + (row_steps // 2) * (1 - place_ref[2]), row_steps)
    at = pl.ds(pl.multiple_of(position * rows, rows), rows)

    @pl.when(step == 0)
    def _():
        put_weights(gu_ref, gu_own_ref, gu_other_ref, True, place_ref[1])
        put_weights(ud_ref, ud_own_ref, ud_other_ref, False, place_ref[0])

    attended = x_ref[...].astype(HIGH) + jnp.where(
        late, summed_halves(p1_ref, r1_ref), summed_halves(p0_ref, r0_ref)
    )
    unit, scale = rms_parts(attended)
    normed = (unit * gain_ref[...]).astype(LOW)
    unit_ref[...] = unit.astype(LOW)
    scale_ref[...] = jnp.broadcast_to(scale, scale_ref.shape)
    put_turned(turned_x_ref, normed, True, place_ref[1], at)
    put_turned(turned_y_ref, normed, False, place_ref[0], at)
    cotangent = g_ref[...]
    put_turned(g_turned_ref, cotangent, False, place_ref[0], at)
    root = 0.7978845608028654
    columns = hidden_ref.shape[1] // 2
    products = []
    for part in range(2):
        w_gate = matrix(gu_ref, part * columns, columns)
        w_up = matrix(ud_ref, 0, columns) if part else matrix(gu_ref, 2 * columns, columns)
        w_down = matrix(ud_ref, (1 + part) * columns, columns)
        gate = matmul_nn(normed, w_gate)
        up = matmul_nn(normed, w_up)
        d_hidden = matmul_nn(cotangent, w_down)
        products.append((gate, up, d_hidden, w_gate, w_up, w_down))
    out = 0.0
    d_normed = 0.0
    for part, (gate, up, d_hidden, w_gate, w_up, w_down) in enumerate(products):
        square = gate * gate
        bend = jnp.tanh(gate * (root + (root * 0.044715) * square))
        half = 0.5 + 0.5 * bend
        gelu = gate * half
        slope = half + (0.5 * gate) * (1.0 - bend * bend) * (root + (3 * root * 0.044715) * square)
        hidden = (gelu * up).astype(LOW)
        d_gate = (d_hidden * up * slope).astype(LOW)
        d_up = (d_hidden * gelu).astype(LOW)
        hidden_ref[at, part * columns : (part + 1) * columns] = hidden
        dgate_up_ref[at, part * columns : (part + 1) * columns] = d_gate
        dgate_up_ref[at, (2 + part) * columns : (3 + part) * columns] = d_up
        d_normed = d_normed + matmul_nt(d_gate, w_gate) + matmul_nt(d_up, w_up)
        out = out + matmul_nt(hidden, w_down)
    dn_ref[...] = d_normed.astype(LOW)

    @pl.when(step < row_steps // 2)
    def _():
        send_ref[...] = out.astype(LOW)

    @pl.when(step >= row_steps // 2)
    def _():
        own_ref[...] = attended + out


def grads_body(first_count, left0_ref, left1_ref, right0_ref, right1_ref, own_ref, other_ref):
    step = pl.program_id(0)
    half = own_ref.shape[0]

    def product(left_ref, right_ref):
        right = right_ref[...]
        own_ref[...] = matmul_nn(left_ref[:half, :], right).astype(LOW)
        other_ref[...] = matmul_nn(left_ref[half:, :], right).astype(LOW)

    pl.when(step < first_count)(functools.partial(product, left0_ref, right0_ref))
    pl.when(step >= first_count)(functools.partial(product, left1_ref, right1_ref))


def turn_body(
    place_ref,
    unit_ref,
    scale_ref,
    g_ref,
    a_ref,
    b_ref,
    gain_ref,
    wo_ref,
    datt_ref,
    turned_ref,
    dmix_ref,
    dgain_ref,
):
    step = pl.program_id(0)
    unit = unit_ref[...].astype(HIGH)
    scale = scale_ref[:, :1]
    d_normed = a_ref[...].astype(HIGH) + b_ref[...].astype(HIGH)
    d_gain = jnp.sum(d_normed * unit, axis=0, keepdims=True)
    d_attended = g_ref[...].astype(HIGH) + rms_back(d_normed, unit, scale, gain_ref[...])
    d_low = d_attended.astype(LOW)
    put_turned(turned_ref, d_low, False, place_ref[0])
    dmix_ref[...] = matmul_nn(d_low, wo_ref[...]).astype(LOW)

    @pl.when(step == 0)
    def _():
        dgain_ref[...] = d_gain

    @pl.when(step != 0)
    def _():
        dgain_ref[...] += d_gain

    @pl.when(step >= pl.num_programs(0) // 2)
    def _():
        datt_ref[...] = d_attended


def backward_body(
    q_ref,
    k_ref,
    v_ref,
    e_ref,
    dmix_ref,
    mixed_ref,
    inv_ref,
    dq_ref,
    dk_ref,
    dv_ref,
    strip_ref,
    table_ref,
    dkt_ref,
    dvt_ref,
):
    seq_len = k_ref.shape[0]
    rows = table_ref.shape[1]
    low_masks = head_masks(LOW)
    masks = head_masks(HIGH)
    keys = k_ref[...]
    values = v_ref[...]
    keys_h = tuple(keys * low_masks[h] for h in range(2))
    table_ref[...] = jnp.zeros_like(table_ref)
    for block in range(seq_len // rows):
        at = slice(block * rows, (block + 1) * rows)
        queries = q_ref[at, :]
        scaled = (dmix_ref[at, :].astype(HIGH) * inv_ref[at, :]).astype(LOW)
        product = scaled.astype(HIGH) * mixed_ref[at, :]
        d_query = jnp.zeros((rows, LANES), HIGH)
        d_key = jnp.zeros((LANES, seq_len), HIGH)
        d_value = jnp.zeros((LANES, seq_len), HIGH)
        for head in range(2):
            scaled_h = scaled * low_masks[head]
            delta = jnp.sum(product * masks[head], axis=-1, keepdims=True)
            weights = e_ref[head, at, :]
            d_scores = weights.astype(HIGH) * (matmul_nt(scaled_h, values) - delta)
            d_low = d_scores.astype(LOW)
            window = slice(seq_len - block * rows, 2 * seq_len - block * rows)
            table_ref[head, :, window] += d_scores
            d_query = d_query + matmul_nn(d_low, keys_h[head])
            d_key = d_key + matmul_tn(queries * low_masks[head], d_low)
            d_value = d_value + matmul_tn(scaled_h, weights)
        dq_ref[at, :] = d_query.astype(LOW)
        if block == 0:
            dkt_ref[...] = d_key
            dvt_ref[...] = d_value
        else:
            dkt_ref[...] += d_key
            dvt_ref[...] += d_value
    dk_ref[...] = dkt_ref[...].T.astype(LOW)
    dv_ref[...] = dvt_ref[...].T.astype(LOW)
    width = 2 * seq_len
    sub = lax.broadcasted_iota(jnp.int32, (8, 1), 0)
    for head in range(2):
        total = table_ref[head, 0:8, :]
        for group in range(1, rows // 8):
            part = table_ref[head, 8 * group : 8 * group + 8, :]
            total = total + pltpu.roll(part, width - 8 * group, 1)
        for bit in (1, 2, 4):
            total = jnp.where((sub & bit) != 0, pltpu.roll(total, width - bit, 1), total)
        strip_ref[0, head : head + 1, :] = jnp.sum(total, axis=0, keepdims=True)


def spread_body(
    place_ref, x_ref, dq_ref, dk_ref, dv_ref, qkv_ref, send_ref, own_ref, dgain_ref
):
    step = pl.program_id(0)
    width = dq_ref.shape[1]
    unit, _ = rms_parts(x_ref[...].astype(HIGH))
    d_normed = (
        matmul_nt(dq_ref[...], qkv_ref[:, :width])
        + matmul_nt(dk_ref[...], qkv_ref[:, width : 2 * width])
        + matmul_nt(dv_ref[...], qkv_ref[:, 2 * width :])
    )
    d_gain = jnp.sum(d_normed * unit, axis=0, keepdims=True)

    @pl.when(step == 0)
    def _():
        dgain_ref[...] = d_gain

    @pl.when(step != 0)
    def _():
        dgain_ref[...] += d_gain

    @pl.when(step < pl.num_programs(0) // 2)
    def _():
        send_ref[...] = d_normed.astype(LOW)

    @pl.when(step >= pl.num_programs(0) // 2)
    def _():
        own_ref[...] = d_normed


def finish_body(x_ref, own_ref, other_ref, datt_ref, gain_ref, out_ref):
    unit, scale = rms_parts(x_ref[...].astype(HIGH))
    d_normed = own_ref[...] + other_ref[...].astype(HIGH)
    out_ref[...] = (datt_ref[...] + rms_back(d_normed, unit, scale, gain_ref[...])).astype(LOW)


def flat_left(left):
    return left.reshape(-1, left.shape[-1])


def weight_grads(first, second, columns, micros):
    left0, right0, at0, count0 = first
    left1, right1, at1, count1 = second
    left0, left1 = flat_left(left0), flat_left(left1)
    height, depth = left0.shape
    steps = count0 + count1
    half_spec = pl.BlockSpec((height // 2, columns), lambda i: (0, i))
    return call(
        functools.partial(grads_body, count0),
        (steps,),
        [
            whole((height, depth)),
            whole((height, depth)),
            pl.BlockSpec((depth, columns), lambda i: (0, at0 + jnp.minimum(i, count0 - 1))),
            pl.BlockSpec((depth, columns), lambda i: (0, at1 + jnp.maximum(i - count0, 0))),
        ],
        [half_spec, half_spec],
        [shaped((height // 2, steps * columns), LOW)] * 2,
        micros=micros,
    )(left0, left1, right0, right1)


def on_core_pair(
    tokens,
    cotangent,
    gain_attn,
    w_query,
    w_key,
    w_value,
    w_out,
    rel_table,
    buckets,
    gain_ffn,
    w_gate,
    w_up,
    w_down,
):
    own_rows, features = tokens.shape
    seq_len = 2 * own_rows
    width = w_query.shape[1]
    units = w_gate.shape[1]
    chunk = units // 2
    pairs = width // LANES
    bucket_count, head_count = rel_table.shape
    local_heads = head_count // 2
    count = lax.axis_size("dp")
    far_bit, y_bit, x_bit = dp_place()
    me = lax.axis_index("mp")
    place = jnp.stack([y_bit, x_bit, me, far_bit]).astype(jnp.int32)
    rows = MXU_ROWS
    steps = seq_len // rows
    half_steps = steps // 2
    block_rows = w_query.shape[0]

    def swapped(array):
        return lax.ppermute(array, "mp", [(0, 1), (1, 0)])

    def in_order(array, other):
        first = jnp.where(me == 0, array, other)
        second = jnp.where(me == 0, other, array)
        return jnp.concatenate([first, second], axis=0)

    early = jnp.concatenate([w_query, w_key, w_value, w_out.T], axis=1)
    late = jnp.concatenate([w_gate, w_up, w_down.T], axis=1)
    early_pieces = far_pieces(early)
    x_other, g_other = swapped(tokens), swapped(cotangent)
    late_pieces = far_pieces(late)
    early_pieces = together(*early_pieces)
    near = far_stack(early, list(early_pieces))
    qk = near[:, : 2 * width]
    vo = near[:, 2 * width :]
    qk_next, vo_next = together(over_y(qk), over_x(vo))
    qk_own = in_bit_order(qk, qk_next, y_bit)
    vo_own = in_bit_order(vo, vo_next, x_bit)
    qk_other = over_x(qk_own)
    vo_other = over_y(vo_own)
    x_all = in_order(tokens, x_other)
    g_all = in_order(cotangent, g_other)
    qk_other, vo_other, x_all, g_all, *late_pieces = together(
        qk_other, vo_other, x_all, g_all, *late_pieces
    )
    near = far_stack(late, late_pieces)
    gu = near[:, : 3 * chunk]
    ud = near[:, 3 * chunk :]
    gu_next = over_y(gu)
    ud_next = over_x(ud)

    gain_a = gain_attn.reshape(1, features)
    gain_f = gain_ffn.reshape(1, features)

    one_hot = (buckets[:, None] == jnp.arange(bucket_count, dtype=jnp.int32)[None, :]).astype(HIGH)
    one_hot = jnp.pad(one_hot, ((1, 0), (0, 0)))
    my_table = lax.dynamic_slice_in_dim(rel_table, me * local_heads, local_heads, 1)
    strip = lax.dot_general(my_table, one_hot, (((0,), (1,)), ((), ())), precision=precise)
    strip = strip.reshape(pairs, 2, 2 * seq_len)

    def row_block(columns):
        return pl.BlockSpec((rows, columns), lambda i, *_: (i, 0))

    turned_shape = (2, 2, 2, 2, block_rows)
    turned_block = pl.BlockSpec(turned_shape + (rows,), lambda i, *_: (0, 0, 0, 0, 0, i))
    turned = shaped(turned_shape + (seq_len,), LOW)
    full_block = (count // 4, 2, 2, block_rows, 2 * width)
    half_block = (features // 2, 2 * width)
    normed_x_turned, normed_y_turned, queries, keys, values, w_qkv, w_o = call(
        project_body,
        (steps,),
        [row_block(features), whole((1, features))] + [whole(half_block)] * 4,
        [turned_block, turned_block]
        + [row_block(width)] * 3
        + [result((features, 3 * width)), result((features, width))],
        [turned, turned]
        + [shaped((seq_len, width), LOW)] * 3
        + [shaped((features, 3 * width), LOW), shaped((features, width), LOW)],
        [pltpu.VMEM(full_block, LOW), pltpu.VMEM(full_block, LOW)],
        prefetch=1,
        micros=7,
    )(place, x_all, gain_a, qk_own, qk_other, vo_own, vo_other)

    gu_next, ud_next, queries = together(gu_next, ud_next, queries)
    gu_own = in_bit_order(gu, gu_next, y_bit)
    ud_own = in_bit_order(ud, ud_next, x_bit)
    gu_other = over_x(gu_own)
    ud_other = over_y(ud_own)

    pair_block = pl.BlockSpec((seq_len, LANES), lambda p: (0, p))
    e_block = pl.BlockSpec((2, seq_len, seq_len), lambda p: (p, 0, 0))
    strip_block = pl.BlockSpec((1, 2, 2 * seq_len), lambda p: (p, 0, 0))
    table_scratch = pltpu.VMEM((2, rows, 2 * seq_len), HIGH)
    weights_e, mixed, mixed_low, inverse, part0, part1 = call(
        attend_body,
        (pairs,),
        [
            pair_block,
            pair_block,
            pair_block,
            strip_block,
            pl.BlockSpec((features, LANES), lambda p: (0, p)),
        ],
        [e_block, pair_block, pair_block, pair_block] + [result((own_rows, features))] * 2,
        [
            shaped((2 * pairs, seq_len, seq_len), LOW),
            shaped((seq_len, width), HIGH),
            shaped((seq_len, width), LOW),
            shaped((seq_len, width), HIGH),
            shaped((own_rows, features), LOW),
            shaped((own_rows, features), LOW),
        ],
        [table_scratch, pltpu.VMEM((seq_len, features), HIGH)],
        micros=20,
    )(queries, keys, values, strip, w_o)
    gu_other, ud_other, came0, came1 = together(
        gu_other, ud_other, swapped(part0), swapped(part1)
    )
    parts = (part0, part1, came0, came1)

    def moved(i, m):
        return (jnp.minimum(i, steps - 1) + half_steps * (1 - m[2])) % steps

    def turned_row(columns):
        return pl.BlockSpec((rows, columns), lambda i, m: (moved(i, m), 0))

    half0_row = pl.BlockSpec(
        (rows, features), lambda i, m: (jnp.minimum(moved(i, m), half_steps - 1), 0)
    )
    half1_row = pl.BlockSpec(
        (rows, features), lambda i, m: (jnp.maximum(moved(i, m) - half_steps, 0), 0)
    )
    moved_block = pl.BlockSpec(turned_shape + (rows,), lambda i, m: (0, 0, 0, 0, 0, moved(i, m)))
    send_row = pl.BlockSpec((rows, features), lambda i, m: (jnp.minimum(i, half_steps - 1), 0))
    keep_row = pl.BlockSpec(
        (rows, features),
        lambda i, m: (jnp.clip(i - half_steps, 0, half_steps - 1), 0),
    )

    def grads_block(first):
        return pl.BlockSpec(
            (features // 2, chunk), lambda i, m: (0, jnp.clip(i - steps - first, 0, 2))
        )

    full_block = (count // 4, 2, 2, block_rows, 3 * chunk)
    half_block = (features // 2, 3 * chunk)
    half_grads = shaped((features // 2, 3 * chunk), LOW)
    unit_f, scale_f, dn_part, out_send, out_own, gu_own, gu_send, ud_own, ud_send = call(
        functools.partial(feed_body, steps),
        (steps + 6,),
        [turned_row(features)]
        + [half0_row, half1_row] * 2
        + [turned_row(features), whole((1, features))]
        + [whole(half_block)] * 4,
        [turned_row(features), turned_row(LANES), turned_row(features), send_row, keep_row]
        + [grads_block(0)] * 2
        + [grads_block(3)] * 2,
        [
            shaped((seq_len, features), LOW),
            shaped((seq_len, LANES), HIGH),
            shaped((seq_len, features), LOW),
            shaped((own_rows, features), LOW),
            shaped((own_rows, features), HIGH),
        ]
        + [half_grads] * 4,
        [pltpu.VMEM(full_block, LOW), pltpu.VMEM(full_block, LOW)]
        + [pltpu.VMEM(turned_shape + (seq_len,), LOW)] * 3
        + [pltpu.VMEM((seq_len, units), LOW), pltpu.VMEM((seq_len, 2 * units), LOW)],
        prefetch=1,
        micros=28,
    )(place, x_all, *parts, g_all, gain_f, gu_own, gu_other, ud_own, ud_other)
    dn_other = swapped(dn_part)
    gu_came = over_x(gu_send)
    ud_came = over_y(ud_send)

    d_attended, d_low_turned, d_mixed, d_gain_f = call(
        turn_body,
        (steps,),
        [turned_row(features), turned_row(LANES)]
        + [turned_row(features)] * 3
        + [whole((1, features)), whole((features, width))],
        [keep_row, moved_block, turned_row(width), result((1, features))],
        [
            shaped((own_rows, features), HIGH),
            turned,
            shaped((seq_len, width), LOW),
            shaped((1, features), HIGH),
        ],
        prefetch=1,
        micros=4,
    )(place, unit_f, scale_f, g_all, dn_part, dn_other, gain_f, w_o)
    out_other = swapped(out_send)

    d_query, d_key, d_value, d_strip = call(
        backward_body,
        (pairs,),
        [pair_block, pair_block, pair_block, e_block, pair_block, pair_block, pair_block],
        [pair_block, pair_block, pair_block, strip_block],
        [shaped((seq_len, width), LOW)] * 3 + [shaped((pairs, 2, 2 * seq_len), HIGH)],
        [table_scratch, pltpu.VMEM((LANES, seq_len), HIGH), pltpu.VMEM((LANES, seq_len), HIGH)],
        micros=4,
    )(queries, keys, values, weights_e, d_mixed, mixed, inverse)

    gu_came, ud_came, out_other, d_query, d_key, d_value, d_strip = together(
        gu_came, ud_came, out_other, d_query, d_key, d_value, d_strip
    )

    def next_half(own, came, bit):
        return (
            add_low(part_of(own, bit, 2), part_of(came, bit, 2)),
            add_low(part_of(own, 1 - bit, 2), part_of(came, 1 - bit, 2)),
        )

    gu_own, gu_send = next_half(gu_own, gu_came, y_bit)
    ud_own, ud_send = next_half(ud_own, ud_came, x_bit)
    gu_came = over_y(gu_send)
    ud_came = over_x(ud_send)

    qk_own, qk_send = weight_grads(
        (normed_x_turned, d_query, 0, 1), (normed_x_turned, d_key, 0, 1), width, 5
    )
    qk_send, d_value = together(qk_send, d_value)
    vo_own, vo_send = weight_grads(
        (normed_y_turned, d_value, 0, 1), (d_low_turned, mixed_low, 0, 1), width, 5
    )
    output = (out_own + out_other.astype(HIGH)).astype(LOW)

    gu_came, ud_came, qk_send, vo_send, d_query = together(
        gu_came, ud_came, qk_send, vo_send, d_query
    )
    qk_came = over_x(qk_send)
    vo_came = over_y(vo_send)
    gu_own, gu_send = next_half(gu_own, gu_came, far_bit % 2)
    gu_came = over_far_bit(gu_send, 0)

    def inner_part(array, index):
        blocks = array.reshape(2, 2, block_rows, -1)
        return lax.dynamic_index_in_dim(blocks, index, 1, False).reshape(2 * block_rows, -1)

    ud_send = add_low(inner_part(ud_own, 1 - far_bit // 2), inner_part(ud_came, 1 - far_bit // 2))
    ud_own = add_low(inner_part(ud_own, far_bit // 2), inner_part(ud_came, far_bit // 2))
    ud_came = over_far_bit(ud_send, 1)

    dna_send, dna_own, d_gain_a = call(
        spread_body,
        (steps,),
        [turned_row(features)] + [turned_row(width)] * 3 + [whole((features, 3 * width))],
        [send_row, keep_row, result((1, features))],
        [
            shaped((own_rows, features), LOW),
            shaped((own_rows, features), HIGH),
            shaped((1, features), HIGH),
        ],
        prefetch=1,
        micros=2,
    )(place, x_all, d_query, d_key, d_value, w_qkv)
    qk_came, vo_came, gu_came, ud_came, dna_send, d_gain_a, d_strip = together(
        qk_came, vo_came, gu_came, ud_came, dna_send, d_gain_a, d_strip
    )
    gu_own, gu_send = next_half(gu_own, gu_came, far_bit // 2)
    ud_own, ud_send = next_half(ud_own, ud_came, far_bit % 2)
    gu_came = over_far_bit(gu_send, 1)
    ud_came = over_far_bit(ud_send, 0)
    dna_other = swapped(dna_send)
    qk_own, qk_send = next_half(qk_own, qk_came, y_bit)
    vo_own, vo_send = next_half(vo_own, vo_came, x_bit)
    qk_came = over_y(qk_send)
    vo_came = over_x(vo_send)

    d_bias = d_strip.reshape(local_heads, 2 * seq_len)
    my_d_table = lax.dot_general(one_hot, d_bias, (((0,), (1,)), ((), ())), precision=precise)
    d_table = lax.dynamic_update_slice_in_dim(
        jnp.zeros_like(rel_table), my_d_table, me * local_heads, 1
    )
    small_early = jnp.concatenate([0.5 * d_gain_f, d_table.reshape(1, -1)], axis=1)
    small_early = jnp.pad(small_early, ((0, 0), (0, -(features + small_early.shape[1]) % (4 * width))))
    small = jnp.concatenate([d_gain_a, small_early], axis=1)
    small = small.reshape(-1, 4 * width)
    small = small + swapped(small)
    small = small + over_x(small) + over_y(small) + over_xy(small)

    d_tokens = call(
        finish_body,
        (half_steps,),
        [row_block(features)] * 4 + [whole((1, features))],
        row_block(features),
        shaped((own_rows, features), LOW),
        micros=0.5,
    )(tokens, dna_own, dna_other, d_attended, gain_a)

    qk_came, vo_came, gu_came, ud_came, small = together(
        qk_came, vo_came, gu_came, ud_came, small
    )
    head_own = jnp.concatenate([qk_own, vo_own], axis=-1)
    head_came = jnp.concatenate([qk_came, vo_came], axis=-1)
    total = add_low(head_own, head_came)

    def far_part(far):
        return part_of(total, 2 * (far % 2) + far // 2, 4)

    small_rows = in_terms(small)
    pieces = [
        over_far(jnp.concatenate([far_part((far_bit + k) % 4), small_rows], axis=0), k)
        for k in range(1, 4)
    ]
    *pieces, d_tokens = together(*pieces, d_tokens)
    small = sum((from_terms(piece[block_rows:], small.shape[0]) for piece in pieces), small)
    small = small.reshape(-1)
    pieces = [piece[:block_rows] for piece in pieces]
    grads_head = sum((piece.astype(HIGH) for piece in pieces), far_part(far_bit).astype(HIGH))
    grads_qk, grads_vo = grads_head[:, : 2 * width], grads_head[:, 2 * width :]
    grads_gu = gu_own.astype(HIGH) + gu_came.astype(HIGH)
    grads_ud = ud_own.astype(HIGH) + ud_came.astype(HIGH)
    return (
        output,
        d_tokens,
        small[:features],
        grads_qk[:, :width],
        grads_qk[:, width:],
        grads_vo[:, :width],
        grads_vo[:, width:].T,
        small[2 * features : 2 * features + rel_table.size].reshape(rel_table.shape),
        small[features : 2 * features],
        grads_gu[:, :units],
        jnp.concatenate([grads_gu[:, units:], grads_ud[:, :chunk]], axis=1),
        grads_ud[:, chunk:].T,
    )


def solution(mesh):
    placed = (
        P(("dp", "mp"), None),
        P(("dp", "mp"), None),
        P(),
        P("dp", "mp"),
        P("dp", "mp"),
        P("dp", "mp"),
        P("mp", "dp"),
        P(),
        P(),
        P(),
        P("dp", "mp"),
        P("dp", "mp"),
        P("mp", "dp"),
    )
    paired = mesh.shape["mp"] == 2 and mesh.shape["dp"] == 16
    body = on_core_pair if paired else on_device
    return jax.shard_map(
        body,
        mesh=mesh,
        in_specs=placed,
        out_specs=(
            P(("dp", "mp"), None),
            P(("dp", "mp"), None),
            P(),
            P("dp", "mp"),
            P("dp", "mp"),
            P("dp", "mp"),
            P("mp", "dp"),
            P(),
            P(),
            P("dp", "mp"),
            P("dp", "mp"),
            P("mp", "dp"),
        ),
        check_vma=False,
    )
```
